128 devices in a mesh: dp: 4 (over z), expert: 32 (over x, y, core).
Axes of the slice: x: 4, y: 4, z: 4, core: 2. Of those that a mesh axis runs over, the one named last changes fastest.
Arguments:
- ids: int32 [4, 4096], P('dp'), may hold values from 0 to 32063
- targets: int32 [4, 4096], P('dp'), may hold values from 0 to 32063
- documents: int32 [128, 128], P(('dp', 'expert')), may hold values from 0 to 3, never falling along the last dimension, each value on 1 to 64 neighbouring positions
- domains: int32 [4, 4096], replicated, may hold values from 0 to 5
- loss_rows: int32 [4, 2048], replicated, may hold values from 0 to 127, as said below
- routes: int32 [16384, 6], P(('dp', 'expert')), may hold values from 0 to 31, all different within a row; in each aligned block of 128 rows (0 to 127, 128 to 255, ...) at most 32 rows name the same one
- dense_rows: float32 [1024, 6944], P(('dp', 'expert'))
- shared_down: float32 [1408, 1024], P(('dp', 'expert')), may hold values from -0.15625 to 0.15625
- gains: float32 [3, 1024], P(None, ('dp', 'expert'))
- tables: float32 [2, 32064, 1024], P(None, 'expert', 'dp')
- expert_up: float32 [32, 2, 1024, 704], P('expert', None, None, 'dp'), may hold values from -0.1875 to 0.1875
- expert_down: float32 [32, 704, 1024], P('expert', 'dp'), may hold values from -1.75 to 1.75
- dense_m: float32 [1024, 6944], P(('dp', 'expert')), may hold values from -1.1920929e-06 to 1.1920929e-06
- shared_m: float32 [1408, 1024], P(('dp', 'expert')), may hold values from -1.1920929e-06 to 1.1920929e-06
- gains_m: float32 [3, 1024], P(None, ('dp', 'expert')), may hold values from -1.1920929e-06 to 1.1920929e-06
- tables_m: float32 [2, 32064, 1024], P(None, 'expert', 'dp'), may hold values from -1.1920929e-06 to 1.1920929e-06
- up_m: float32 [32, 2, 1024, 704], P('expert', None, None, 'dp'), may hold values from -1.1920929e-06 to 1.1920929e-06
- down_m: float32 [32, 704, 1024], P('expert', 'dp'), may hold values from -2.3841858e-07 to 2.3841858e-07
- dense_v: float32 [1024, 6944], P(('dp', 'expert')), may hold values from 1.4641431e-13 to 5.8565723e-13
- shared_v: float32 [1408, 1024], P(('dp', 'expert')), may hold values from 1.4641431e-13 to 5.8565723e-13
- gains_v: float32 [3, 1024], P(None, ('dp', 'expert')), may hold values from 6.97211e-12 to 4.183266e-11
- tables_v: float32 [2, 32064, 1024], P(None, 'expert', 'dp'), may hold values from 1.4641431e-13 to 5.8565723e-13
- up_v: float32 [32, 2, 1024, 704], P('expert', None, None, 'dp'), may hold values from 1.4641431e-13 to 5.8565723e-13
- down_v: float32 [32, 704, 1024], P('expert', 'dp'), may hold values from 7.320715e-15 to 2.928286e-14
- expert_bias: float32 [32], replicated, may hold values from -1.25 to 1.25
Outputs:
- dense_new: float32 [1024, 6944], P(('dp', 'expert'))
- shared_new: float32 [1408, 1024], P(('dp', 'expert'))
- gains_new: float32 [3, 1024], P(None, ('dp', 'expert'))
- tables_new: float32 [2, 32064, 1024], P(None, 'expert', 'dp')
- up_new: float32 [32, 2, 1024, 704], P('expert', None, None, 'dp')
- down_new: float32 [32, 704, 1024], P('expert', 'dp')
- dense_m_new: float32 [1024, 6944], P(('dp', 'expert'))
- shared_m_new: float32 [1408, 1024], P(('dp', 'expert'))
- gains_m_new: float32 [3, 1024], P(None, ('dp', 'expert'))
- tables_m_new: float32 [2, 32064, 1024], P(None, 'expert', 'dp')
- up_m_new: float32 [32, 2, 1024, 704], P('expert', None, None, 'dp')
- down_m_new: float32 [32, 704, 1024], P('expert', 'dp')
- dense_v_new: float32 [1024, 6944], P(('dp', 'expert'))
- shared_v_new: float32 [1408, 1024], P(('dp', 'expert'))
- gains_v_new: float32 [3, 1024], P(None, ('dp', 'expert'))
- tables_v_new: float32 [2, 32064, 1024], P(None, 'expert', 'dp')
- up_v_new: float32 [32, 2, 1024, 704], P('expert', None, None, 'dp')
- down_v_new: float32 [32, 704, 1024], P('expert', 'dp')
- bias_new: float32 [32], replicated
- grad_norm: float32 [], replicated
- loss_sum: float32 [], replicated
- weight_sum: float32 [], replicated
The draws below stay inside these ranges and needn't reach their ends.
Inputs may be any that keep to these rules, and one draw needn't show every extreme that they name: `routes`: in each aligned block of 128 rows (the tokens of one device) no expert is named by more than 32 rows, a bound that some block reaches. `documents`: within each row the document numbers never fall. `loss_rows`: each device's 64 entries are distinct and ascending and include its first and last position.
All inputs are finite; a program needn't handle non-finite values.
Results may differ from the reference program's by a relative error of at most 0.02.
The reference program's roundings to bfloat16 on the way count: a program that leaves them out, or rounds other values in their place, can miss the bound.
Values may be sent and summed in bfloat16 or wider, within the bound.
No kernel may reach another device: no remote copies, remote signals or barrier semaphores. Data moves between devices by JAX's collectives and lax.ppermute only.
A program may use at most 256 MiB of HBM per device.

```python
import math
import jax
import jax.numpy as jnp
import numpy as np
from jax import lax

D = 1024
HD = 128
HEADS = 8
FF = 704
SFF = 1408
V = 32064
TOP = 6
EXPERTS = 32
TOK_DEV = 128
LOSS_DEV = 64
CAP = 32
GROUP = 4096
TOKENS = 16384
NDOM = 6
STEP = 10
PARAMS = 143428608
N_DP = 4
N_EXPERT = 32


def draw_gains(key, part):
    key = jax.random.fold_in(key, 11)
    column = jnp.arange(D, dtype=jnp.float32) / (D - 1)
    rise = 3.0 ** column * (math.log(3.0) / 2.0)
    noise = jax.random.uniform(key, (3, D), jnp.float32, 0.8, 1.2)
    return rise[None, :] * noise


def draw_dense_rows(key, part):
    key = jax.random.fold_in(key, 12)
    widths = [3 * D, D, 2 * SFF, EXPERTS]
    factors = [1.3, 2.0, 1.0, 0.5]
    scale = jnp.concatenate([jnp.full((width_part,), factor, jnp.float32) for width_part, factor in zip(widths, factors)]) / math.sqrt(D)
    columns = 4 * D + 2 * SFF + EXPERTS
    base = jax.random.normal(key, (D, columns), jnp.float32)
    return base * scale[None, :]


def draw_tables(key, part):
    key = jax.random.fold_in(key, 13)
    first_key, second_key = jax.random.split(key)
    row_place = jnp.arange(V, dtype=jnp.float32) / (V - 1)
    embed = jax.random.normal(first_key, (V, D), jnp.float32)
    head = jax.random.normal(second_key, (V, D), jnp.float32) * (3.0 ** row_place)[:, None]
    return jnp.stack([embed, head / math.sqrt(D)])


def draw_domains(key, part):
    key = jax.random.fold_in(key, 14)
    column = jnp.arange(N_EXPERT * TOK_DEV, dtype=jnp.int32) // TOK_DEV
    row_number = jnp.arange(N_DP, dtype=jnp.int32)
    level = 2 * row_number[:, None] // max(N_DP - 1, 1) + 2 * column[None, :] // max(N_EXPERT - 1, 1)
    base = jax.random.randint(key, (N_DP, N_EXPERT * TOK_DEV), 0, 2)
    base = base.at[:, ::TOK_DEV].set(0)
    base = base.at[:, TOK_DEV - 1::TOK_DEV].set(1)
    return jnp.minimum(base + level, NDOM - 1).astype(jnp.int32)


def draw_loss_rows(key, part):
    key = jax.random.fold_in(key, 15)
    blocks = N_DP * N_EXPERT
    keys = jax.random.split(key, blocks)
    inner = jax.vmap(lambda block_key: jax.random.permutation(block_key, TOK_DEV - 2)[:LOSS_DEV - 2] + 1)(keys)
    ends = jnp.broadcast_to(jnp.array([0, TOK_DEV - 1], jnp.int32), (blocks, 2))
    picked = jnp.sort(jnp.concatenate([ends, inner.astype(jnp.int32)], axis=1), axis=1)
    return picked.reshape(N_DP, N_EXPERT * LOSS_DEV).astype(jnp.int32)


def touch_ends(drawn, rng, low, high):
    longest = drawn.shape.index(max(drawn.shape))
    spots = []
    for shift in (0, 1):
        where = [jax.random.randint(jax.random.fold_in(rng, axis), (), 0, length) for axis, length in enumerate(drawn.shape)]
        where[longest] = (where[longest] + shift) % drawn.shape[longest]
        spots.append(tuple(where))
    return drawn.at[spots[0]].set(low).at[spots[1]].set(high)


def steps_of(own_key, extent, cuts, least, largest):
    loudness, own = 1.0, jax.random.fold_in(own_key, 6)
    for axis_at, parts in cuts:
        draws = jnp.exp(jax.random.uniform(jax.random.fold_in(own, axis_at), (parts,), jnp.float32, least / len(cuts), largest / len(cuts)))
        loudness = loudness * jnp.repeat(draws, extent[axis_at] // parts).reshape([-1 if axis == axis_at else 1 for axis in range(len(extent))])
    return loudness


def rank_bounds(count, lean):
    loads = [(1 << 20) // math.isqrt(rank ** lean) + 1 for rank in range(1, count + 1)]
    deviation = 1 + sum(loads) // (1 << 30)
    return np.cumsum(np.array([max(1, weight // deviation) for weight in loads]))


def ranked(rng, shape, amount, slope):
    grid = rank_bounds(amount, slope)
    ticket = jax.random.randint(jax.random.fold_in(rng, 1), shape, 0, int(grid[amount - 1]))
    grade = jnp.searchsorted(jnp.asarray(grid, jnp.int32), ticket, side="right")
    return jax.random.permutation(jax.random.fold_in(rng, 2), amount)[grade].astype(jnp.int32)


def split_up(count, total, most, lean):
    loads = [(1 << 20) // math.isqrt(grade ** lean) + 1 for grade in range(2, count + 1)]
    rest, holding = total - most - (count - 1), [1] * (count - 1)
    while rest > 0:
        candidates = [i for i in range(count - 1) if holding[i] < most]
        whole, budget = sum([loads[i] for i in candidates]), rest
        for i in candidates:
            more = min(most - holding[i], max(1, budget * loads[i] // whole), rest)
            holding[i] = holding[i] + more
            rest = rest - more
    return np.array([most] + holding)


def ragged(stream_key, count, total, limit, lean):
    if count == 2:
        one = jax.random.randint(stream_key, (), max(1, total - limit), min(limit, total - 1) + 1)
        return jnp.stack([one, total - one])
    sizes = jnp.asarray(split_up(count, total, limit, lean), jnp.int32)
    couples = (count - 1) // 2
    donor, taker = sizes[1:1 + 2 * couples:2], sizes[2:2 + 2 * couples:2]
    slack = jnp.minimum(donor - 1, limit - taker)
    passed = jax.random.randint(jax.random.fold_in(stream_key, 1), (couples,), 0, 1 << 20) % (slack + 1)
    sizes = sizes.at[1:1 + 2 * couples:2].set(donor - passed).at[2:2 + 2 * couples:2].set(taker + passed)
    return sizes[jax.random.permutation(jax.random.fold_in(stream_key, 2), count)]


def deal_out(key, own, number, rows, count, top, reach, lean):
    sequence = jax.random.permutation(key, count)
    crowded, usual = portions_of(count, rows * top, reach, lean, True), portions_of(count, rows * top, reach, lean, False)
    places = jnp.arange(count)

    def named(sizes, turn):
        used = int((sizes > 0).sum())
        fixed = max(1, used // 4)
        shifted = fixed + (places - fixed + turn * (used - fixed)) % max(1, count - fixed)
        return jnp.zeros((count,), jnp.int32).at[sequence[jnp.where(places < fixed, places, shifted)]].set(jnp.asarray(sizes, jnp.int32))

    sizes = jnp.where(number % 4 == 0, named(crowded, number // 4), named(usual, number - number // 4 - 1))
    mixed = jax.random.permutation(jax.random.fold_in(own, 3), count)
    donor, sink = mixed[0:count // 2 * 2:2], mixed[1:count // 2 * 2:2]
    room = jnp.minimum(sizes[donor] - 1, reach - sizes[sink]) // 2
    room = jnp.where((donor == sequence[0]) | (sink == sequence[0]) | (sizes[sink] == 0), 0, jnp.maximum(room, 0))
    shifted = jax.random.randint(jax.random.fold_in(own, 4), (count // 2,), 0, 1 << 20) % (room + 1)
    sizes = sizes.at[donor].add(-shifted).at[sink].add(shifted)
    members = jnp.searchsorted(jnp.cumsum(sizes), jnp.arange(rows * top), side="right").astype(jnp.int32)
    grid = members.reshape(top, rows).T
    grid = grid[jax.random.permutation(jax.random.fold_in(own, 1), rows)]
    turn = jax.random.randint(jax.random.fold_in(own, 2), (rows, 1), 0, top)
    return jnp.take_along_axis(grid, (jnp.arange(top)[None, :] + turn) % top, axis=1)


def portions_of(count, total, most, lean, full):
    loads = [(1 << 20) // math.isqrt(rank ** lean) + 1 for rank in range(1, count + 1)]
    largest = most if full else min(most, max(-(-total // count), total * loads[0] // sum(loads)))
    least = 1 if total - largest >= count - 1 else 0
    holding, surplus = [largest] + [least] * (count - 1), total - largest - least * (count - 1)
    while surplus > 0:
        free = [i for i in range(1, count) if holding[i] < largest] or [i for i in range(1, count) if holding[i] < most]
        mass, remaining = sum([loads[i] for i in free]), surplus
        for i in free:
            addition = min(most - holding[i], max(1, remaining * loads[i] // mass), surplus)
            holding[i] = holding[i] + addition
            surplus = surplus - addition
    return np.array(holding)


def scatter_about(key, shape, width, most, cuts=(), kind=jnp.bfloat16):
    level = steps_of(key, shape, cuts, -0.22, 0.18) if cuts else 1.0
    result = jax.random.normal(key, shape, jnp.float32) * width * level
    return jnp.minimum(jnp.maximum(result, -most), most).astype(kind)


def setup_inputs(seed: int = 0) -> dict:
    key_list = jax.random.split(jax.random.key(seed), 26)
    ids = touch_ends(ranked(key_list[0], (N_DP, GROUP), V, 1), jax.random.fold_in(key_list[0], 3), 0, V - 1).astype(jnp.int32)
    targets = touch_ends(ranked(key_list[1], (N_DP, GROUP), V, 1), jax.random.fold_in(key_list[1], 3), 0, V - 1).astype(jnp.int32)
    documents = jax.vmap(lambda own: jnp.searchsorted(jnp.cumsum(ragged(own, 4, TOK_DEV, TOK_DEV // 2, 0)), jnp.arange(TOK_DEV), side="right"))(jax.random.split(key_list[2], (N_DP * N_EXPERT))).reshape((N_DP * N_EXPERT, TOK_DEV)).astype(jnp.int32)
    domains = draw_domains(jax.random.fold_in(key_list[25], 71), 0)
    loss_rows = draw_loss_rows(jax.random.fold_in(key_list[25], 71), 0)
    routes_keys = jax.random.split(jax.random.fold_in(key_list[5], 1), TOKENS // TOK_DEV)
    routes_turns = jax.random.permutation(jax.random.fold_in(key_list[5], 3), TOKENS // TOK_DEV)
    routes = jax.vmap(lambda own, number: deal_out(jax.random.fold_in(key_list[5], 2), own, number, TOK_DEV, EXPERTS, TOP, CAP, 1))(routes_keys, routes_turns).reshape((TOKENS, TOP))
    dense_rows = draw_dense_rows(jax.random.fold_in(key_list[25], 71), 0)
    shared_down = scatter_about(key_list[7], (SFF, D), SFF ** -0.5, 0.15625, ((0, 128),), jnp.float32)
    gains = draw_gains(jax.random.fold_in(key_list[25], 71), 0)
    tables = draw_tables(jax.random.fold_in(key_list[25], 71), 0)
    expert_up = scatter_about(key_list[10], (EXPERTS, 2, D, FF), D ** -0.5, 0.1875, ((0, 32), (3, 4)), jnp.float32)
    expert_down = scatter_about(key_list[11], (EXPERTS, FF, D), (FF // 64) ** -0.5, 1.75, ((0, 32), (1, 4)), jnp.float32)
    dense_m = scatter_about(key_list[12], (D, 4 * D + 2 * SFF + EXPERTS), (0.00222 * PARAMS ** -0.5), 1.1920928955078125e-06, ((0, 128),), jnp.float32)
    shared_m = scatter_about(key_list[13], (SFF, D), (0.00222 * PARAMS ** -0.5), 1.1920928955078125e-06, ((0, 128),), jnp.float32)
    gains_m = scatter_about(key_list[14], (3, D), (0.00222 * PARAMS ** -0.5), 1.1920928955078125e-06, ((1, 128),), jnp.float32)
    tables_m = scatter_about(key_list[15], (2, V, D), (0.00222 * PARAMS ** -0.5), 1.1920928955078125e-06, ((1, 32), (2, 4)), jnp.float32)
    up_m = scatter_about(key_list[16], (EXPERTS, 2, D, FF), (0.00222 * PARAMS ** -0.5), 1.1920928955078125e-06, ((0, 32), (3, 4)), jnp.float32)
    down_m = scatter_about(key_list[17], (EXPERTS, FF, D), (0.00044 * PARAMS ** -0.5), 2.384185791015625e-07, ((0, 32), (1, 4)), jnp.float32)
    dense_v = jnp.clip(jnp.exp(math.log(5.8565722800899e-13) - 1.3862944 * jax.random.uniform(key_list[18], (D, 4 * D + 2 * SFF + EXPERTS), jnp.float32) ** steps_of(key_list[18], (D, 4 * D + 2 * SFF + EXPERTS), ((0, 128),), -0.2, 0.2)), 1.464143070022475e-13, 5.8565722800899e-13)
    shared_v = jnp.clip(jnp.exp(math.log(5.8565722800899e-13) - 1.3862944 * jax.random.uniform(key_list[19], (SFF, D), jnp.float32) ** steps_of(key_list[19], (SFF, D), ((0, 128),), -0.2, 0.2)), 1.464143070022475e-13, 5.8565722800899e-13)
    gains_v = jnp.clip(jnp.exp(math.log(4.183265886470444e-11) - 1.79175945 * jax.random.uniform(key_list[20], (3, D), jnp.float32) ** steps_of(key_list[20], (3, D), ((1, 128),), -0.2, 0.2)), 6.972109955344363e-12, 4.183265886470444e-11)
    tables_v = jnp.clip(jnp.exp(math.log(5.8565722800899e-13) - 1.3862944 * jax.random.uniform(key_list[21], (2, V, D), jnp.float32) ** steps_of(key_list[21], (2, V, D), ((1, 32), (2, 4)), -0.2, 0.2)), 1.464143070022475e-13, 5.8565722800899e-13)
    up_v = jnp.clip(jnp.exp(math.log(5.8565722800899e-13) - 1.3862944 * jax.random.uniform(key_list[22], (EXPERTS, 2, D, FF), jnp.float32) ** steps_of(key_list[22], (EXPERTS, 2, D, FF), ((0, 32), (3, 4)), -0.2, 0.2)), 1.464143070022475e-13, 5.8565722800899e-13)
    down_v = jnp.clip(jnp.exp(math.log(2.928286072282314e-14) - 1.3862944 * jax.random.uniform(key_list[23], (EXPERTS, FF, D), jnp.float32) ** steps_of(key_list[23], (EXPERTS, FF, D), ((0, 32), (1, 4)), -0.2, 0.2)), 7.320715180705786e-15, 2.928286072282314e-14)
    expert_bias = scatter_about(key_list[24], (EXPERTS,), 0.2, 1.25, (), jnp.float32)
    return dict(ids=ids, targets=targets, documents=documents, domains=domains, loss_rows=loss_rows, routes=routes, dense_rows=dense_rows, shared_down=shared_down, gains=gains, tables=tables, expert_up=expert_up, expert_down=expert_down, dense_m=dense_m, shared_m=shared_m, gains_m=gains_m, tables_m=tables_m, up_m=up_m, down_m=down_m, dense_v=dense_v, shared_v=shared_v, gains_v=gains_v, tables_v=tables_v, up_v=up_v, down_v=down_v, expert_bias=expert_bias)


@jax.custom_vjp
def low(v):
    return lax.optimization_barrier(v.astype(jnp.bfloat16)).astype(jnp.float32)

@jax.custom_vjp
def low_back(v):
    return v

def low_keep(v):
    return (low(v), None)

def low_pass(kept, grad):
    return (grad,)

def back_keep(v):
    return (v, None)

def back_low(kept, grad):
    return (low(grad),)
low.defvjp(low_keep, low_pass)
low_back.defvjp(back_keep, back_low)
NORM_EPS = 1e-06
HIGH = lax.Precision.HIGHEST
BETA_ONE = 0.9
BETA_TWO = 0.95
ADAM_EPS = 1e-08
DECAY = 0.1
CLIP_NORM = 0.02
BIAS_RATE = 0.05
ROPE_BASE = 10000.0
RATES = (0.03, 0.03, 0.5, 0.4, 0.03, 0.5)
MASKED = -1e+30

def matmul(left, right):
    return jnp.dot(left, right, precision=HIGH, preferred_element_type=jnp.float32)

def norm_apply(values, gain_row):
    return values * lax.rsqrt(lax.optimization_barrier(jnp.mean(values * values, axis=-1, keepdims=True)) + NORM_EPS) * gain_row

def swiglu(gate_act, up_act):
    return jax.nn.silu(gate_act) * up_act

def rope_tables(length, head_size):
    positions = jnp.arange(length, dtype=jnp.float32)
    frequency = ROPE_BASE ** (-2.0 * jnp.arange(head_size // 2, dtype=jnp.float32) / head_size)
    angles = positions[:, None] * frequency[None, :]
    return (jnp.cos(angles)[:, None, :], jnp.sin(angles)[:, None, :])

def rotate(values, cosine, sine):
    half_size = values.shape[-1] // 2
    first_half = values[..., :half_size]
    second_half = values[..., half_size:]
    return jnp.concatenate([first_half * cosine - second_half * sine, second_half * cosine + first_half * sine], axis=-1)

def slot_index(routes, experts):
    flat_routes = routes.reshape(-1)
    onehot = (flat_routes[:, None] == jnp.arange(experts, dtype=jnp.int32)[None, :]).astype(jnp.int32)
    earlier = jnp.cumsum(onehot, axis=0) - onehot
    return lax.optimization_barrier(jnp.sum(earlier * onehot, axis=1)).reshape(routes.shape)

def gate_values(router_logits, routes):
    chosen = jnp.take_along_axis(router_logits, routes, axis=1)
    scores = jax.nn.sigmoid(chosen)
    return scores / lax.optimization_barrier(jnp.sum(scores, axis=1, keepdims=True))

def adam_update(weight, grad, first, second, rate, clip_scale):
    grad = grad * clip_scale
    first = BETA_ONE * first + (1.0 - BETA_ONE) * grad
    second = BETA_TWO * second + (1.0 - BETA_TWO) * grad * grad
    first_fix = first / (1.0 - BETA_ONE ** STEP)
    second_fix = second / (1.0 - BETA_TWO ** STEP)
    weight = weight - rate * (first_fix / (jnp.sqrt(second_fix) + ADAM_EPS) + DECAY * weight)
    return (weight, first, second)

def expert_apply(inputs):
    expert_rows, up_pair, down_mat = inputs
    gate_act = low_back(matmul(expert_rows, up_pair[0]))
    up_act = low_back(matmul(expert_rows, up_pair[1]))
    return low(low_back(matmul(low(swiglu(gate_act, up_act)), down_mat)))

def head_block(inputs, head_table):
    chosen, target_ids, row_weights = inputs
    logits = low_back(lax.dot_general(chosen, head_table, (((1,), (1,)), ((), ())), precision=HIGH, preferred_element_type=jnp.float32))
    top_logit = lax.optimization_barrier(jnp.max(logits, axis=1, keepdims=True))
    log_norm = top_logit[:, 0] + jnp.log(lax.optimization_barrier(jnp.sum(jnp.exp(logits - top_logit), axis=1)))
    target_logit = jnp.take_along_axis(logits, target_ids[:, None], axis=1)[:, 0]
    return jnp.sum(row_weights * (log_norm - target_logit))

def loss_columns(loss_rows):
    offsets = jnp.arange(N_EXPERT, dtype=jnp.int32)[None, :, None] * TOK_DEV
    return (offsets + loss_rows.reshape(N_DP, N_EXPERT, LOSS_DEV)).reshape(N_DP, N_EXPERT * LOSS_DEV)

def forward(params, ids, targets, documents, routes, columns, row_weights):
    dense_w, down_shared, gain_full, table_w, up_w, down_w = [low(param) for param in params]
    devices = N_DP * N_EXPERT
    router_start = 4 * D + 2 * SFF
    x_first = table_w[0][ids.reshape(-1)]
    cosine, sine = rope_tables(TOK_DEV, HD)
    positions = jnp.arange(TOK_DEV)
    causal = (positions[:, None] >= positions[None, :])[None, None]
    mask = causal & (documents[:, None, :, None] == documents[:, None, None, :])
    h_first = low(norm_apply(x_first, gain_full[0]))
    qkv_all = low_back(matmul(h_first, dense_w[:, :3 * D])).reshape(devices, TOK_DEV, 3, HEADS, HD)
    query = low(rotate(qkv_all[:, :, 0], cosine, sine))
    key_rot = low(rotate(qkv_all[:, :, 1], cosine, sine))
    value_low = low(qkv_all[:, :, 2])
    scores = low_back(jnp.einsum('nqhd,nkhd->nhqk', query, key_rot, precision=HIGH) * (1.0 / math.sqrt(HD)))
    probs = low(jax.nn.softmax(jnp.where(mask, scores, MASKED), axis=-1))
    attended = low(low_back(jnp.einsum('nhqk,nkhd->nqhd', probs, value_low, precision=HIGH))).reshape(TOKENS, D)
    x_mid = x_first + low_back(matmul(attended, dense_w[:, 3 * D:4 * D]))
    h_mid = low(norm_apply(x_mid, gain_full[1]))
    gates = gate_values(matmul(h_mid, dense_w[:, router_start:]), routes)
    shared_in = low_back(matmul(h_mid, dense_w[:, 4 * D:router_start]))
    shared_out = low_back(matmul(low(swiglu(shared_in[:, :SFF], shared_in[:, SFF:])), down_shared))
    slots = jax.vmap(lambda route_block: slot_index(route_block, EXPERTS))(routes.reshape(devices, TOK_DEV, TOP)).reshape(TOKENS, TOP)
    source = jnp.broadcast_to((jnp.arange(TOKENS, dtype=jnp.int32) // TOK_DEV)[:, None], (TOKENS, TOP))
    buffer = jnp.zeros((EXPERTS, devices, CAP, D), jnp.float32)
    buffer = buffer.at[routes, source, slots].set(jnp.broadcast_to(h_mid[:, None, :], (TOKENS, TOP, D)))
    buffer = low_back(buffer).reshape(EXPERTS, devices * CAP, D)
    outputs = lax.map(jax.checkpoint(expert_apply), (buffer, up_w, down_w)).reshape(EXPERTS, devices, CAP, D)
    routed = lax.optimization_barrier(jnp.sum(gates[:, :, None] * outputs[routes, source, slots], axis=1))
    x_last = x_mid + shared_out + routed
    h_last = norm_apply(x_last, gain_full[2])
    token_rows = columns + (jnp.arange(N_DP, dtype=jnp.int32) * GROUP)[:, None]
    chosen = low(h_last[token_rows])
    target_ids = targets.reshape(-1)[token_rows]
    head_table = table_w[1]
    losses = lax.map(jax.checkpoint(lambda inputs: head_block(inputs, head_table)), (chosen, target_ids, row_weights))
    loss_total = jnp.sum(losses)
    return (loss_total / jnp.sum(row_weights), loss_total)

def reference(ids, targets, documents, domains, loss_rows, routes, dense_rows, shared_down, gains, tables, expert_up, expert_down, dense_m, shared_m, gains_m, tables_m, up_m, down_m, dense_v, shared_v, gains_v, tables_v, up_v, down_v, expert_bias):
    columns = loss_columns(loss_rows)
    row_weights = jnp.exp2(jnp.take_along_axis(domains, columns, axis=1).astype(jnp.float32) - 2.0)
    weight_total = jnp.sum(row_weights)
    params = (dense_rows, shared_down, gains, tables, expert_up, expert_down)

    def objective(param_set):
        return forward(param_set, ids, targets, documents, routes, columns, row_weights)
    mean_loss, pullback, loss_total = jax.vjp(objective, params, has_aux=True)
    grads = pullback(jnp.ones((), jnp.float32))[0]
    squares = jnp.sum(jnp.stack([jnp.sum(grad_part * grad_part) for grad_part in grads]))
    norm_value = jnp.sqrt(squares)
    clip_scale = jnp.minimum(1.0, CLIP_NORM / (norm_value + 1e-06))
    firsts = (dense_m, shared_m, gains_m, tables_m, up_m, down_m)
    seconds = (dense_v, shared_v, gains_v, tables_v, up_v, down_v)
    updated = [adam_update(params[index], grads[index], firsts[index], seconds[index], RATES[index], clip_scale) for index in range(6)]
    counts = lax.optimization_barrier(jnp.sum((routes.reshape(-1)[:, None] == jnp.arange(EXPERTS, dtype=jnp.int32)[None, :]).astype(jnp.float32), axis=0))
    mean_load = jnp.sum(counts) / EXPERTS
    bias_new = expert_bias + BIAS_RATE * jnp.sign(mean_load - counts)
    return (updated[0][0], updated[1][0], updated[2][0], updated[3][0], updated[4][0], updated[5][0], updated[0][1], updated[1][1], updated[2][1], updated[3][1], updated[4][1], updated[5][1], updated[0][2], updated[1][2], updated[2][2], updated[3][2], updated[4][2], updated[5][2], bias_new, norm_value, loss_total, weight_total)
```

```python
import math

import jax
import jax.numpy as jnp
from jax import lax
from jax.sharding import PartitionSpec as P

HD = 128
TOP = 6
STEP = 10


NORM_EPS = 1e-06
HIGH = lax.Precision.HIGHEST
BETA_ONE = 0.9
BETA_TWO = 0.95
ADAM_EPS = 1e-08
DECAY = 0.1
CLIP_NORM = 0.02
BIAS_RATE = 0.05
ROPE_BASE = 10000.0
RATES = (0.03, 0.03, 0.5, 0.4, 0.03, 0.5)
MASKED = -1e30
LOW = jnp.bfloat16
BOTH = ("dp", "expert")
STREAMS = 4


def product(left, right):
    return jnp.dot(left, right, preferred_element_type=jnp.float32)


def inner_rows(left, right, precision=None):
    return lax.dot_general(
        left,
        right,
        (((0,), (0,)), ((), ())),
        precision=precision,
        preferred_element_type=jnp.float32,
    )


def inner_cols(left, right, precision=None):
    return lax.dot_general(
        left,
        right,
        (((1,), (1,)), ((), ())),
        precision=precision,
        preferred_element_type=jnp.float32,
    )


def split_three(values):
    high = values.astype(LOW)
    rest = values - high.astype(jnp.float32)
    middle = rest.astype(LOW)
    last = (rest - middle.astype(jnp.float32)).astype(LOW)
    return high, middle, last


def pick_exact(choice, values):
    return sum(product(choice, part) for part in split_three(values))


def norm_apply(values, gain_row):
    return (
        values * lax.rsqrt(jnp.mean(values * values, axis=-1, keepdims=True) + NORM_EPS) * gain_row
    )


def swiglu(gate_act, up_act):
    return jax.nn.silu(gate_act) * up_act


def rope_tables(length, head_size):
    positions = jnp.arange(length, dtype=jnp.float32)
    frequency = ROPE_BASE ** (-2.0 * jnp.arange(head_size // 2, dtype=jnp.float32) / head_size)
    angles = positions[:, None] * frequency[None, :]
    return (jnp.cos(angles)[:, None, :], jnp.sin(angles)[:, None, :])


def rotate(values, cosine, sine):
    half_size = values.shape[-1] // 2
    first_half = values[..., :half_size]
    second_half = values[..., half_size:]
    return jnp.concatenate(
        [first_half * cosine - second_half * sine, second_half * cosine + first_half * sine],
        axis=-1,
    )


def adam_update(weight, grad, first, second, rate, clip_scale):
    grad = grad * clip_scale
    first = BETA_ONE * first + (1.0 - BETA_ONE) * grad
    second = BETA_TWO * second + (1.0 - BETA_TWO) * grad * grad
    first_fix = first / (1.0 - BETA_ONE**STEP)
    second_fix = second / (1.0 - BETA_TWO**STEP)
    weight = weight - rate * (first_fix / (jnp.sqrt(second_fix) + ADAM_EPS) + DECAY * weight)
    return (weight, first, second)


def swap(value, number):
    return lax.ppermute(value, "expert", [(i, i ^ number) for i in range(32)])


def by_distance(values, index):
    rest = values.shape[1:]
    for bit in range(5):
        halves = values.reshape((32 >> (bit + 1), 2, 1 << bit) + rest)
        values = jnp.where(((index >> bit) & 1) == 1, halves[:, ::-1], halves)
    return values.reshape((32,) + rest)


def add_low(left, right):
    return (left.astype(jnp.float32) + right.astype(jnp.float32)).astype(LOW)


def ring_sum(blocks, shift, other_way):
    near, far = (3, 1) if other_way else (1, 3)
    if other_way:
        sent = jnp.stack([blocks[3], blocks[2]])
        kept = blocks[0:2]
    else:
        sent = blocks[1:3]
        kept = jnp.stack([blocks[0], blocks[3]])
    kept = add_low(kept, swap(sent, near << shift))
    return add_low(kept[0], swap(kept[1], far << shift))


def ring_gather(block, shift, other_way):
    near, far = (3, 1) if other_way else (1, 3)
    pair = jnp.stack([block, swap(block, far << shift)])
    met = swap(pair, near << shift)
    if other_way:
        return jnp.stack([pair[0], pair[1], met[1], met[0]])
    return jnp.stack([pair[0], met[0], met[1], pair[1]])


def plane_sum(blocks, stream):
    other_way = stream % 2 == 1
    if stream // 2 == 0:
        return ring_sum(ring_sum(blocks, 3, other_way), 1, other_way)
    turned = jnp.swapaxes(blocks, 0, 1)
    return ring_sum(ring_sum(turned, 1, other_way), 3, other_way)


def plane_gather(block, stream):
    other_way = stream % 2 == 1
    if stream // 2 == 0:
        return ring_gather(ring_gather(block, 1, other_way), 3, other_way)
    return jnp.swapaxes(
        ring_gather(ring_gather(block, 3, other_way), 1, other_way), 0, 1
    )


def expert_sum(blocks):
    _, rows, width = blocks.shape
    blocks = blocks.reshape(4, 4, 2, STREAMS, rows // STREAMS, width)
    mine = add_low(blocks[:, :, 0], swap(blocks[:, :, 1], 1))
    return jnp.concatenate([plane_sum(mine[:, :, s], s) for s in range(STREAMS)], axis=0)


def expert_gather(block):
    rows, width = block.shape
    part = rows // STREAMS
    mine = jnp.stack(
        [plane_gather(block[s * part : (s + 1) * part], s) for s in range(STREAMS)], axis=2
    )
    return jnp.stack([mine, swap(mine, 1)], axis=2).reshape(32, rows, width)


def merge_stats(first_part, second_part):
    top_value = jnp.maximum(first_part[0], second_part[0])
    total_exp = first_part[1] * jnp.exp(first_part[0] - top_value) + second_part[1] * jnp.exp(
        second_part[0] - top_value
    )
    return jnp.stack([top_value, total_exp, first_part[2] + second_part[2]])


def flip_blocks(stats, number):
    rows = stats.shape[-1]
    stats = stats.reshape(3, 2, 2, 2, 2, 2, rows)
    axes = [5 - bit for bit in range(5) if (number >> bit) & 1]
    return jnp.flip(stats, axes).reshape(3, 32, rows)


def meet_stats(stats):
    for shift in (3, 1):
        others = [flip_blocks(swap(stats, k << shift), k << shift) for k in (1, 2, 3)]
        for other in others:
            stats = merge_stats(stats, other)
    return merge_stats(stats, flip_blocks(swap(stats, 1), 1))


def hot(indices, count):
    return (indices[..., None] == jnp.arange(count, dtype=jnp.int32)).astype(LOW)


def attention_scores(query, key_rot, mask):
    scores = jnp.einsum("qhd,khd->hqk", query, key_rot, preferred_element_type=jnp.float32) * (
        1.0 / math.sqrt(HD)
    )
    return jnp.where(mask[None], scores, MASKED)


def body(
    ids,
    targets,
    documents,
    domains,
    loss_rows,
    routes,
    dense_rows,
    shared_down,
    gains,
    tables,
    expert_up,
    expert_down,
    dense_m,
    shared_m,
    gains_m,
    tables_m,
    up_m,
    down_m,
    dense_v,
    shared_v,
    gains_v,
    tables_v,
    up_v,
    down_v,
    expert_bias,
):
    f32 = jnp.float32
    groups = lax.axis_size("dp")
    axis_width = lax.axis_size("expert")
    expert_index = lax.axis_index("expert")
    group_index = lax.axis_index("dp")
    devices = groups * axis_width
    rows_dev = routes.shape[0]
    own_rows, dense_width = dense_rows.shape
    own_down, width_model = shared_down.shape
    hidden_shared = own_down * devices
    heads_count = width_model // HD
    experts = expert_bias.shape[0]
    slot_cap = min(rows_dev, rows_dev * TOP * 4 // (3 * experts))
    slots_all = experts * slot_cap
    vocab_part = tables.shape[1]
    part_width = tables.shape[2]
    vocab_start = expert_index * vocab_part
    hidden = expert_down.shape[1] * groups

    gap = -(dense_width + gains.shape[0]) % 128
    down_low = shared_down.astype(LOW)
    packed = jnp.concatenate(
        [
            dense_rows.astype(LOW),
            gains.astype(LOW).T,
            jnp.zeros((own_rows, gap), LOW),
            down_low[:own_rows],
            jnp.pad(down_low[own_rows:], ((0, 2 * own_rows - own_down), (0, 0))),
        ],
        axis=1,
    )
    packed_all = lax.all_gather(packed, BOTH, axis=0, tiled=True)
    start = dense_width + gains.shape[0] + gap
    router_start = 4 * width_model + 2 * hidden_shared
    w_qkv = packed_all[:, : 3 * width_model]
    w_out = packed_all[:, 3 * width_model : 4 * width_model]
    w_shared = packed_all[:, 4 * width_model : router_start]
    w_router = packed_all[:, router_start:dense_width]
    gain_full = packed_all[:, dense_width : dense_width + gains.shape[0]].T.astype(f32)
    down_first = packed_all[:, start : start + width_model]
    down_second = packed_all[:, start + width_model :]

    ids_all = lax.all_to_all(
        jnp.broadcast_to(ids, (groups,) + ids.shape[1:]), "dp", split_axis=0, concat_axis=0, tiled=True
    )
    ids_near = by_distance(
        ids_all.reshape(groups, axis_width, rows_dev).swapaxes(0, 1), expert_index
    )
    local_ids = (ids_near - vocab_start).reshape(4, 4, 2, groups, rows_dev)
    table_words = tables[0].astype(LOW)
    looked_up = []
    for core in (1, 0):
        found = product(hot(local_ids[:, :, core].reshape(-1), vocab_part), table_words)
        looked_up.append(found.astype(LOW).reshape(4, 4, groups, rows_dev, part_width))
    looked_up = add_low(looked_up[1], swap(looked_up[0], 1))
    x_first = jnp.stack([plane_sum(looked_up[:, :, s], s) for s in range(groups)])
    x_first = lax.all_to_all(x_first, "dp", split_axis=0, concat_axis=0, tiled=True)
    x_first = x_first.swapaxes(0, 1).reshape(rows_dev, width_model).astype(f32)

    expert_part = jnp.concatenate(
        [expert_up[0].astype(LOW).swapaxes(1, 2), expert_down.astype(LOW)], axis=0
    )
    expert_all = lax.all_gather(expert_part, "dp", axis=1, tiled=True)
    w_gate, w_up, w_down = expert_all[0], expert_all[1], expert_all[2]
    head = lax.all_gather(tables[1].astype(LOW), "dp", axis=1, tiled=True)

    positions = jnp.arange(rows_dev)
    experts_range = jnp.arange(experts, dtype=jnp.int32)
    chosen = jnp.any(routes[:, :, None] == experts_range[None, None, :], axis=1)
    earlier = product(
        (positions[:, None] > positions[None, :]).astype(LOW), chosen.astype(LOW)
    ).astype(jnp.int32)
    place = jnp.where(chosen, earlier, slot_cap)
    token_slots = hot(place, slot_cap).reshape(rows_dev, slots_all)
    slot_tokens = token_slots.T
    slot_experts = (
        jnp.arange(slots_all, dtype=jnp.int32)[:, None] // slot_cap == experts_range[None, :]
    )
    spread = slot_experts.T.astype(LOW)

    per_device = loss_rows.shape[1] // axis_width
    loss_places = loss_rows.reshape(groups, axis_width, per_device)
    at_place = loss_places[..., None] == jnp.arange(rows_dev, dtype=jnp.int32)
    counted_domains = jnp.sum(
        jnp.where(at_place, domains.reshape(groups, axis_width, 1, rows_dev), 0), axis=-1
    )
    all_weights = jnp.exp2(counted_domains.astype(f32) - 2.0)
    weight_total = jnp.sum(all_weights)
    group_weights = by_distance(lax.dynamic_index_in_dim(all_weights, group_index, 0, False), expert_index)
    group_places = lax.dynamic_index_in_dim(loss_places, group_index, 0, False)
    group_targets = jnp.sum(
        jnp.where(
            group_places[..., None] == jnp.arange(rows_dev, dtype=jnp.int32),
            targets.reshape(axis_width, 1, rows_dev),
            0,
        ),
        axis=-1,
    )
    target_local = (by_distance(group_targets, expert_index) - vocab_start).reshape(-1)
    own_choice = hot(by_distance(group_places, expert_index)[0], rows_dev)
    grad_weights = group_weights.reshape(-1) / weight_total

    docs_row = documents[0]
    mask = (positions[:, None] >= positions[None, :]) & (docs_row[:, None] == docs_row[None, :])
    cosine, sine = rope_tables(rows_dev, HD)
    h_first_low = norm_apply(x_first, gain_full[0]).astype(LOW)
    qkv_all = product(h_first_low, w_qkv)
    query = rotate(
        qkv_all[:, :width_model].reshape(rows_dev, heads_count, HD), cosine, sine
    ).astype(LOW)
    key_rot = rotate(
        qkv_all[:, width_model : 2 * width_model].reshape(rows_dev, heads_count, HD), cosine, sine
    ).astype(LOW)
    value_low = qkv_all[:, 2 * width_model :].reshape(rows_dev, heads_count, HD).astype(LOW)
    scores = attention_scores(query, key_rot, mask)
    top_score = jnp.max(scores, axis=-1, keepdims=True)
    expo = jnp.exp(scores - top_score)
    probs = expo / jnp.sum(expo, axis=-1, keepdims=True)
    attended = jnp.einsum(
        "hqk,khd->qhd", probs.astype(LOW), value_low, preferred_element_type=f32
    )
    attended = attended.reshape(rows_dev, width_model).astype(LOW)
    x_mid = x_first + product(attended, w_out)
    h_low = norm_apply(x_mid, gain_full[1]).astype(LOW)

    buffer = product(slot_tokens, h_low).astype(LOW)
    expert_rows = lax.all_to_all(buffer, "expert", split_axis=0, concat_axis=0, tiled=True)

    gate_scores = jnp.where(chosen, jax.nn.sigmoid(product(h_low, w_router)), 0.0)
    gate_total = jnp.sum(gate_scores, axis=1, keepdims=True)
    gates = gate_scores / gate_total
    gate_slots = jnp.concatenate(
        [token_slots * product(part, spread).astype(LOW) for part in split_three(gates)], axis=0
    )
    slot_gates = jnp.sum(
        jnp.where(slot_experts, pick_exact(slot_tokens, gates), 0.0), axis=1, keepdims=True
    )
    down_rows = jnp.arange(hidden_shared, dtype=jnp.int32)
    down_place = (down_rows // own_down) * own_rows + down_rows % own_down
    down_spot = jnp.where(
        down_rows % own_down < own_rows,
        down_place,
        down_place + (devices - 1) * own_rows,
    )
    down_choice = hot(down_spot, 2 * devices * own_rows)
    w_sdown = (
        product(down_choice[:, : devices * own_rows], down_first)
        + product(down_choice[:, devices * own_rows :], down_second)
    ).astype(LOW)
    shared_in = product(h_low, w_shared)
    shared_hidden = swiglu(shared_in[:, :hidden_shared], shared_in[:, hidden_shared:]).astype(LOW)
    shared_out = product(shared_hidden, w_sdown)

    gate_act = inner_cols(expert_rows, w_gate)
    up_act = inner_cols(expert_rows, w_up)
    expert_hidden = swiglu(gate_act, up_act).astype(LOW)
    expert_out = product(expert_hidden, w_down).astype(LOW)
    returned = lax.all_to_all(expert_out, "expert", split_axis=0, concat_axis=0, tiled=True)
    routed = product(gate_slots, returned).reshape(3, rows_dev, width_model)
    x_last = x_mid + shared_out + (routed[0] + routed[1] + routed[2])

    chosen_rows = product(own_choice, norm_apply(x_last, gain_full[2]).astype(LOW)).astype(LOW)
    gathered = expert_gather(chosen_rows).reshape(axis_width * per_device, width_model)
    logits = inner_cols(gathered, head)
    is_target = target_local[:, None] == jnp.arange(vocab_part, dtype=jnp.int32)[None, :]
    row_top = jnp.max(logits, axis=1)
    expos = jnp.exp(logits - row_top[:, None])
    row_total = jnp.sum(expos, axis=1)
    row_target = jnp.sum(jnp.where(is_target, logits, 0.0), axis=1)
    rest_low = jnp.where(is_target, 0.0, expos).astype(LOW)
    stats = meet_stats(
        jnp.stack([row_top, row_total, row_target]).reshape(3, axis_width, per_device)
    )
    log_norm = (stats[0] + jnp.log(stats[1])).reshape(-1)
    entropy = log_norm.reshape(axis_width, per_device)[0] - stats[2, 0]
    own_loss = jnp.sum(group_weights[0] * entropy)
    rest_scale = jnp.exp(row_top - log_norm) * grad_weights
    target_grad = (jnp.exp(stats[2].reshape(-1) - log_norm) - 1.0) * grad_weights
    target_head = product(is_target.astype(LOW), head)
    d_rows_all = product(rest_low, head) * rest_scale[:, None] + target_grad[:, None] * target_head
    d_chosen = expert_sum(
        d_rows_all.astype(LOW).reshape(axis_width, per_device, width_model)
    ).astype(f32)
    d_logits = jnp.where(
        is_target, target_grad[:, None], rest_low.astype(f32) * rest_scale[:, None]
    ).astype(LOW)
    d_head = inner_rows(d_logits, gathered).astype(LOW)
    d_head = d_head.reshape(vocab_part, groups, part_width).swapaxes(0, 1)
    d_head_part = lax.psum_scatter(d_head, "dp", scatter_dimension=0, tiled=True)[0].astype(f32)

    _, final_back = jax.vjp(norm_apply, x_last, gain_full[2])
    d_last, d_gain_last = final_back(pick_exact(own_choice.T, d_chosen))
    d_branch = d_last.astype(LOW)
    d_last_parts = split_three(d_last)

    d_buffer = (sum(product(slot_tokens, part) for part in d_last_parts) * slot_gates).astype(LOW)
    d_rows = lax.all_to_all(d_buffer, "expert", split_axis=0, concat_axis=0, tiled=True)

    d_slots = inner_cols(jnp.concatenate(d_last_parts, axis=0), returned)
    d_slots = jnp.sum(d_slots.reshape(3, rows_dev, slots_all), axis=0) * token_slots.astype(f32)
    d_gates = sum(inner_cols(part, spread) for part in split_three(d_slots))
    d_scores = (d_gates - jnp.sum(gates * d_gates, axis=1, keepdims=True)) / gate_total
    d_router_logits = jnp.where(chosen, d_scores * gate_scores * (1.0 - gate_scores), 0.0)
    d_hmid = inner_cols(d_router_logits, w_router.astype(f32), HIGH)

    _, shared_back = jax.vjp(swiglu, shared_in[:, :hidden_shared], shared_in[:, hidden_shared:])
    d_gate_shared, d_up_shared = shared_back(inner_cols(d_branch, w_sdown))
    d_shared_in = jnp.concatenate([d_gate_shared, d_up_shared], axis=1).astype(LOW)
    d_hmid = d_hmid + inner_cols(d_shared_in, w_shared)

    features = jnp.arange(width_model, dtype=jnp.int32)
    owner, row = features // own_rows, features % own_rows
    turned = (owner % axis_width) * groups + owner // axis_width
    turn_choice = hot(turned * own_rows + row, width_model)
    downs = down_rows // own_down
    down_turned = (downs % axis_width) * groups + downs // axis_width
    down_turn = hot(down_turned * (2 * own_rows) + down_rows % own_down, 2 * devices * own_rows)
    h_mid_turned = product(h_low, turn_choice).astype(LOW)
    attended_turned = product(attended, turn_choice).astype(LOW)
    h_first_turned = product(h_first_low, turn_choice).astype(LOW)
    hidden_turned = product(shared_hidden, down_turn).astype(LOW)
    d_wshared = inner_rows(h_mid_turned, d_shared_in).astype(LOW)
    d_wrouter = sum(
        inner_rows(h_mid_turned, part) for part in split_three(d_router_logits)
    ).astype(LOW)
    d_sdown = inner_rows(hidden_turned, d_branch).astype(LOW)

    d_expert_hidden = inner_cols(d_rows, w_down)
    _, expert_back = jax.vjp(swiglu, gate_act, up_act)
    d_gate_expert, d_up_expert = expert_back(d_expert_hidden)
    d_gate_expert = d_gate_expert.astype(LOW)
    d_up_expert = d_up_expert.astype(LOW)
    d_sent = (product(d_gate_expert, w_gate) + product(d_up_expert, w_up)).astype(LOW)
    d_returned = lax.all_to_all(d_sent, "expert", split_axis=0, concat_axis=0, tiled=True)
    d_experts = jnp.stack(
        [
            inner_rows(d_gate_expert, expert_rows).astype(LOW),
            inner_rows(d_up_expert, expert_rows).astype(LOW),
            inner_rows(expert_hidden, d_rows).astype(LOW),
        ]
    )
    experts_part = lax.psum_scatter(d_experts, "dp", scatter_dimension=1, tiled=True).astype(f32)

    d_hmid = d_hmid + product(token_slots, d_returned)
    _, mid_back = jax.vjp(norm_apply, x_mid, gain_full[1])
    d_mid_part, d_gain_mid = mid_back(d_hmid)
    d_mid = d_last + d_mid_part
    d_att_in = d_mid.astype(LOW)
    d_wout = inner_rows(attended_turned, d_att_in).astype(LOW)
    d_attended = inner_cols(d_att_in, w_out).astype(LOW).reshape(rows_dev, heads_count, HD)
    d_value = jnp.einsum("hqk,qhd->khd", probs.astype(LOW), d_attended, preferred_element_type=f32)
    d_probs = jnp.einsum("qhd,khd->hqk", d_attended, value_low, preferred_element_type=f32)
    d_scores = (probs * (d_probs - jnp.sum(probs * d_probs, axis=-1, keepdims=True))).astype(LOW)
    scale_query = 1.0 / math.sqrt(HD)
    d_query = (
        jnp.einsum("hqk,khd->qhd", d_scores, key_rot, preferred_element_type=f32) * scale_query
    )
    d_key = jnp.einsum("hqk,qhd->khd", d_scores, query, preferred_element_type=f32) * scale_query
    d_qkv = jnp.concatenate(
        [
            rotate(d_query, cosine, -sine).reshape(rows_dev, width_model),
            rotate(d_key, cosine, -sine).reshape(rows_dev, width_model),
            d_value.reshape(rows_dev, width_model),
        ],
        axis=1,
    ).astype(LOW)
    d_wqkv = inner_rows(h_first_turned, d_qkv).astype(LOW)
    _, first_back = jax.vjp(norm_apply, x_first, gain_full[0])
    d_first_part, d_gain_first = first_back(inner_cols(d_qkv, w_qkv))
    d_first = (d_mid + d_first_part).astype(LOW)

    d_first = d_first.reshape(rows_dev, groups, part_width).swapaxes(0, 1)
    d_first = lax.all_to_all(d_first, "dp", split_axis=0, concat_axis=0, tiled=True)
    d_tokens = jnp.stack([plane_gather(d_first[s], s) for s in range(groups)], axis=2)
    d_embed = 0.0
    for core, tokens in ((0, d_tokens), (1, swap(d_tokens, 1))):
        words = hot(local_ids[:, :, core].reshape(-1), vocab_part)
        d_embed = d_embed + inner_rows(words, tokens.reshape(-1, part_width))

    gain_grad = jnp.stack([d_gain_first, d_gain_mid, d_gain_last], axis=1)
    gain_grad = gain_grad.reshape(groups, axis_width, own_rows, -1).swapaxes(0, 1)
    gain_grad = gain_grad.reshape(width_model, -1).astype(LOW)
    early = jnp.concatenate(
        [
            d_wshared,
            d_wrouter,
            jnp.zeros((width_model, -d_wrouter.shape[1] % 128), LOW),
            d_sdown.reshape(devices, 2, own_rows, width_model)[:, 0].reshape(width_model, -1),
            d_sdown.reshape(devices, 2, own_rows, width_model)[:, 1].reshape(width_model, -1),
            d_wout,
        ],
        axis=1,
    )
    late = jnp.concatenate([d_wqkv, jnp.pad(gain_grad, ((0, 0), (0, 128 - gain_grad.shape[1])))], axis=1)
    parts = []
    for grad in (early, late):
        part = lax.psum_scatter(grad, "expert", scatter_dimension=0, tiled=True)
        part = lax.all_to_all(part, "dp", split_axis=0, concat_axis=0, tiled=True)
        parts.append(jnp.sum(part.reshape(groups, own_rows, -1).astype(f32), axis=0))
    early, late = parts
    wide = 2 * hidden_shared + -(-d_wrouter.shape[1] // 128) * 128
    dense_part = jnp.concatenate(
        [
            late[:, : 3 * width_model],
            early[:, wide + 2 * width_model :],
            early[:, : 2 * hidden_shared + d_wrouter.shape[1]],
        ],
        axis=1,
    )
    shared_part = jnp.concatenate(
        [
            early[:, wide : wide + width_model],
            early[: own_down - own_rows, wide + width_model : wide + 2 * width_model],
        ],
        axis=0,
    )
    gains_part = late[:, 3 * width_model : 3 * width_model + gains.shape[0]].T
    up_part = experts_part[:2].swapaxes(1, 2)[None]
    down_part = experts_part[2:]

    grads = (dense_part, shared_part, gains_part, d_embed, d_head_part, up_part, down_part)
    squares = sum(jnp.sum(grad_part * grad_part) for grad_part in grads)
    counts = jnp.sum(chosen.astype(f32), axis=0)
    sums = jnp.concatenate([squares[None], own_loss[None], counts, jnp.zeros((126 - experts,), f32)])
    sums = lax.all_to_all(
        jnp.broadcast_to(sums[None], (devices, 128)), BOTH, split_axis=0, concat_axis=0, tiled=True
    )
    sums = jnp.sum(sums, axis=0)
    total_squares, loss_total, counts_all = sums[0], sums[1], sums[2 : 2 + experts]
    norm_value = jnp.sqrt(total_squares)
    clip_scale = jnp.minimum(1.0, CLIP_NORM / (norm_value + 1e-06))
    tables_part = jnp.stack([d_embed, d_head_part])
    grads = (dense_part, shared_part, gains_part, tables_part, up_part, down_part)
    masters = (dense_rows, shared_down, gains, tables, expert_up, expert_down)
    firsts = (dense_m, shared_m, gains_m, tables_m, up_m, down_m)
    seconds = (dense_v, shared_v, gains_v, tables_v, up_v, down_v)
    updated = [
        adam_update(
            masters[index], grads[index], firsts[index], seconds[index], RATES[index], clip_scale
        )
        for index in range(6)
    ]
    mean_load = jnp.sum(counts_all) / experts
    bias_new = expert_bias + BIAS_RATE * jnp.sign(mean_load - counts_all)
    return (
        *(new[0] for new in updated),
        *(new[1] for new in updated),
        *(new[2] for new in updated),
        bias_new,
        norm_value,
        loss_total,
        weight_total,
    )


def solution(mesh):
    in_specs = (
        P("dp", None),
        P("dp", None),
        P(("dp", "expert"), None),
        P(),
        P(),
        P(("dp", "expert"), None),
        P(("dp", "expert"), None),
        P(("dp", "expert"), None),
        P(None, ("dp", "expert")),
        P(None, "expert", "dp"),
        P("expert", None, None, "dp"),
        P("expert", "dp", None),
        P(("dp", "expert"), None),
        P(("dp", "expert"), None),
        P(None, ("dp", "expert")),
        P(None, "expert", "dp"),
        P("expert", None, None, "dp"),
        P("expert", "dp", None),
        P(("dp", "expert"), None),
        P(("dp", "expert"), None),
        P(None, ("dp", "expert")),
        P(None, "expert", "dp"),
        P("expert", None, None, "dp"),
        P("expert", "dp", None),
        P(),
    )
    out_specs = (
        P(("dp", "expert"), None),
        P(("dp", "expert"), None),
        P(None, ("dp", "expert")),
        P(None, "expert", "dp"),
        P("expert", None, None, "dp"),
        P("expert", "dp", None),
        P(("dp", "expert"), None),
        P(("dp", "expert"), None),
        P(None, ("dp", "expert")),
        P(None, "expert", "dp"),
        P("expert", None, None, "dp"),
        P("expert", "dp", None),
        P(("dp", "expert"), None),
        P(("dp", "expert"), None),
        P(None, ("dp", "expert")),
        P(None, "expert", "dp"),
        P("expert", None, None, "dp"),
        P("expert", "dp", None),
        P(),
        P(),
        P(),
        P(),
    )
    return jax.shard_map(body, mesh=mesh, in_specs=in_specs, out_specs=out_specs, check_vma=False)
```

```python
import math

import jax
import jax.numpy as jnp
from jax import lax
from jax.sharding import PartitionSpec as P

HD = 128
TOP = 6
STEP = 10


NORM_EPS = 1e-06
HIGH = lax.Precision.HIGHEST
BETA_ONE = 0.9
BETA_TWO = 0.95
ADAM_EPS = 1e-08
DECAY = 0.1
CLIP_NORM = 0.02
BIAS_RATE = 0.05
ROPE_BASE = 10000.0
RATES = (0.03, 0.03, 0.5, 0.4, 0.03, 0.5)
MASKED = -1e30
LOW = jnp.bfloat16
BOTH = ("dp", "expert")
STREAMS = 4


def product(left, right):
    return jnp.dot(left, right, preferred_element_type=jnp.float32)


def inner_rows(left, right, precision=None):
    return lax.dot_general(
        left,
        right,
        (((0,), (0,)), ((), ())),
        precision=precision,
        preferred_element_type=jnp.float32,
    )


def inner_cols(left, right, precision=None):
    return lax.dot_general(
        left,
        right,
        (((1,), (1,)), ((), ())),
        precision=precision,
        preferred_element_type=jnp.float32,
    )


def split_three(values):
    high = values.astype(LOW)
    rest = values - high.astype(jnp.float32)
    middle = rest.astype(LOW)
    last = (rest - middle.astype(jnp.float32)).astype(LOW)
    return high, middle, last


def pick_exact(choice, values):
    return sum(product(choice, part) for part in split_three(values))


def norm_apply(values, gain_row):
    return (
        values * lax.rsqrt(jnp.mean(values * values, axis=-1, keepdims=True) + NORM_EPS) * gain_row
    )


def swiglu(gate_act, up_act):
    return jax.nn.silu(gate_act) * up_act


def rope_tables(length, head_size):
    positions = jnp.arange(length, dtype=jnp.float32)
    frequency = ROPE_BASE ** (-2.0 * jnp.arange(head_size // 2, dtype=jnp.float32) / head_size)
    angles = positions[:, None] * frequency[None, :]
    return (jnp.cos(angles)[:, None, :], jnp.sin(angles)[:, None, :])


def rotate(values, cosine, sine):
    half_size = values.shape[-1] // 2
    first_half = values[..., :half_size]
    second_half = values[..., half_size:]
    return jnp.concatenate(
        [first_half * cosine - second_half * sine, second_half * cosine + first_half * sine],
        axis=-1,
    )


def adam_update(weight, grad, first, second, rate, clip_scale):
    grad = grad * clip_scale
    first = BETA_ONE * first + (1.0 - BETA_ONE) * grad
    second = BETA_TWO * second + (1.0 - BETA_TWO) * grad * grad
    first_fix = first / (1.0 - BETA_ONE**STEP)
    second_fix = second / (1.0 - BETA_TWO**STEP)
    weight = weight - rate * (first_fix / (jnp.sqrt(second_fix) + ADAM_EPS) + DECAY * weight)
    return (weight, first, second)


def swap(value, number):
    return lax.ppermute(value, "expert", [(i, i ^ number) for i in range(32)])


def swap_group(value, number):
    return lax.ppermute(value, "dp", [(i, i ^ number) for i in range(4)])


def by_distance(values, index):
    shape = values.shape
    rest = shape[1:]
    for bit in range(shape[0].bit_length() - 1):
        halves = values.reshape((shape[0] >> (bit + 1), 2, 1 << bit) + rest)
        values = jnp.where(((index >> bit) & 1) == 1, halves[:, ::-1], halves)
    return values.reshape(shape)


def after(values, trigger):
    return lax.optimization_barrier((values, trigger))[0]


def add_low(left, right):
    return (left.astype(jnp.float32) + right.astype(jnp.float32)).astype(LOW)


def ring_sum(blocks, shift, other_way):
    near, far = (3, 1) if other_way else (1, 3)
    if other_way:
        sent = jnp.stack([blocks[3], blocks[2]])
        kept = blocks[0:2]
    else:
        sent = blocks[1:3]
        kept = jnp.stack([blocks[0], blocks[3]])
    kept = add_low(kept, swap(sent, near << shift))
    return add_low(kept[0], swap(kept[1], far << shift))


def ring_gather(block, shift, other_way):
    near, far = (3, 1) if other_way else (1, 3)
    pair = jnp.stack([block, swap(block, far << shift)])
    met = swap(pair, near << shift)
    if other_way:
        return jnp.stack([pair[0], pair[1], met[1], met[0]])
    return jnp.stack([pair[0], met[0], met[1], pair[1]])


ORDERS = ((0, 3, 1, 2), (0, 1, 3, 2))


def in_order(values, stream):
    order = ORDERS[stream % 2]
    if stream >= 2:
        values = jnp.swapaxes(values, 0, 1)
    values = jnp.stack([values[i] for i in order])
    return jnp.stack([values[:, i] for i in order], axis=1)


def rank_in_order(distance, stream):
    return sum(
        jnp.where(distance == number, spot, 0) for spot, number in enumerate(ORDERS[stream % 2])
    )


def steps_of(stream):
    near, far = (3, 1) if stream % 2 == 1 else (1, 3)
    shifts = (3, 1) if stream < 2 else (1, 3)
    return [number << shift for shift in shifts for number in (near, far)]


def ordered_sum(blocks, stream):
    shape = blocks.shape[2:]
    blocks = blocks.reshape((16,) + shape)
    for number in steps_of(stream):
        half = blocks.shape[0] // 2
        blocks = add_low(blocks[:half], swap(blocks[half:], number))
    return blocks[0]


def ordered_gather(block, stream):
    blocks = block[None]
    for number in reversed(steps_of(stream)):
        blocks = jnp.concatenate([blocks, swap(blocks, number)], axis=0)
    return blocks


def plane_sum(blocks, stream):
    other_way = stream % 2 == 1
    if stream // 2 == 0:
        return ring_sum(ring_sum(blocks, 3, other_way), 1, other_way)
    turned = jnp.swapaxes(blocks, 0, 1)
    return ring_sum(ring_sum(turned, 1, other_way), 3, other_way)


def plane_gather(block, stream):
    other_way = stream % 2 == 1
    if stream // 2 == 0:
        return ring_gather(ring_gather(block, 1, other_way), 3, other_way)
    return jnp.swapaxes(
        ring_gather(ring_gather(block, 3, other_way), 1, other_way), 0, 1
    )


def expert_sum(blocks):
    _, rows, width = blocks.shape
    blocks = blocks.reshape(4, 4, 2, STREAMS, rows // STREAMS, width)
    mine = add_low(blocks[:, :, 0], swap(blocks[:, :, 1], 1))
    return jnp.concatenate([plane_sum(mine[:, :, s], s) for s in range(STREAMS)], axis=0)


def expert_gather(block):
    rows, width = block.shape
    part = rows // STREAMS
    mine = jnp.stack(
        [plane_gather(block[s * part : (s + 1) * part], s) for s in range(STREAMS)], axis=2
    )
    return jnp.stack([mine, swap(mine, 1)], axis=2).reshape(32, rows, width)


def merge_stats(first_part, second_part):
    top_value = jnp.maximum(first_part[0], second_part[0])
    total_exp = first_part[1] * jnp.exp(first_part[0] - top_value) + second_part[1] * jnp.exp(
        second_part[0] - top_value
    )
    return jnp.stack([top_value, total_exp, first_part[2] + second_part[2]])


def flip_blocks(stats, number):
    rows = stats.shape[-1]
    stats = stats.reshape(3, 2, 2, 2, 2, 2, rows)
    axes = [5 - bit for bit in range(5) if (number >> bit) & 1]
    return jnp.flip(stats, axes).reshape(3, 32, rows)


def meet_stats(stats, beside):
    for shift in (3, 1):
        others = [flip_blocks(swap(stats, k << shift), k << shift) for k in (1, 2, 3)]
        for other in others:
            stats = merge_stats(stats, other)
    other, beside = lax.optimization_barrier((swap(stats, 1), beside))
    return merge_stats(stats, flip_blocks(other, 1)), beside


def hot(indices, count):
    return (indices[..., None] == jnp.arange(count, dtype=jnp.int32)).astype(LOW)


def attention_scores(query, key_rot, mask):
    scores = jnp.einsum("qhd,khd->hqk", query, key_rot, preferred_element_type=jnp.float32) * (
        1.0 / math.sqrt(HD)
    )
    return jnp.where(mask[None], scores, MASKED)


def body(
    ids,
    targets,
    documents,
    domains,
    loss_rows,
    routes,
    dense_rows,
    shared_down,
    gains,
    tables,
    expert_up,
    expert_down,
    dense_m,
    shared_m,
    gains_m,
    tables_m,
    up_m,
    down_m,
    dense_v,
    shared_v,
    gains_v,
    tables_v,
    up_v,
    down_v,
    expert_bias,
):
    f32 = jnp.float32
    groups = lax.axis_size("dp")
    axis_width = lax.axis_size("expert")
    expert_index = lax.axis_index("expert")
    group_index = lax.axis_index("dp")
    devices = groups * axis_width
    rows_dev = routes.shape[0]
    own_rows, dense_width = dense_rows.shape
    own_down, width_model = shared_down.shape
    hidden_shared = own_down * devices
    heads_count = width_model // HD
    experts = expert_bias.shape[0]
    slot_cap = min(rows_dev, rows_dev * TOP * 4 // (3 * experts))
    slots_all = experts * slot_cap
    vocab_part = tables.shape[1]
    part_width = tables.shape[2]
    vocab_start = expert_index * vocab_part
    hidden = expert_down.shape[1] * groups

    gap = -(dense_width + gains.shape[0]) % 128
    down_low = shared_down.astype(LOW)
    packed = jnp.concatenate(
        [
            dense_rows.astype(LOW),
            gains.astype(LOW).T,
            jnp.zeros((own_rows, gap), LOW),
            down_low[:own_rows],
            jnp.pad(down_low[own_rows:], ((0, 2 * own_rows - own_down), (0, 0))),
        ],
        axis=1,
    )
    packed_all = lax.all_gather(packed, BOTH, axis=0, tiled=True)
    start = dense_width + gains.shape[0] + gap
    router_start = 4 * width_model + 2 * hidden_shared
    w_qkv = packed_all[:, : 3 * width_model]
    w_out = packed_all[:, 3 * width_model : 4 * width_model]
    w_shared = packed_all[:, 4 * width_model : router_start]
    w_router = packed_all[:, router_start:dense_width]
    gain_full = packed_all[:, dense_width : dense_width + gains.shape[0]].T.astype(f32)
    down_first = packed_all[:, start : start + width_model]
    down_second = packed_all[:, start + width_model :]

    local_ids = []
    for k in range(groups):
        group_ids = ids[0] if k == 0 else swap_group(ids, k)[0]
        group_ids = by_distance(group_ids.reshape(axis_width, rows_dev), expert_index)
        local_ids.append(in_order(group_ids.reshape(4, 4, 2, rows_dev) - vocab_start, k))
    table_words = tables[0].astype(LOW)
    per_half = 16 * rows_dev

    def look_up(streams, core):
        wanted = jnp.concatenate([local_ids[k][:, :, core].reshape(-1) for k in streams])
        found = product(hot(wanted, vocab_part), table_words).astype(LOW)
        return found.reshape(len(streams), per_half, part_width)

    x_first = []
    for streams in ((0,), (1, 2, 3)):
        sent = swap(look_up(streams, 1), 1)
        summed = add_low(look_up(streams, 0), sent)
        for place, k in enumerate(streams):
            block = ordered_sum(summed[place].reshape(4, 4, rows_dev, part_width), k)
            x_first.append(block if k == 0 else swap_group(block, k))
    x_first = by_distance(jnp.stack(x_first), group_index)
    x_first = x_first.swapaxes(0, 1).reshape(rows_dev, width_model).astype(f32)

    expert_part = jnp.concatenate(
        [expert_up[0].astype(LOW).swapaxes(1, 2), expert_down.astype(LOW)], axis=0
    )
    expert_all = jnp.concatenate(
        [expert_part] + [swap_group(expert_part, k) for k in range(1, groups)], axis=1
    )
    w_gate, w_up, w_down = expert_all[0], expert_all[1], expert_all[2]
    head = lax.all_gather(tables[1].astype(LOW), "dp", axis=1, tiled=True)

    positions = jnp.arange(rows_dev)
    experts_range = jnp.arange(experts, dtype=jnp.int32)
    chosen = jnp.any(routes[:, :, None] == experts_range[None, None, :], axis=1)
    earlier = product(
        (positions[:, None] > positions[None, :]).astype(LOW), chosen.astype(LOW)
    ).astype(jnp.int32)
    place = jnp.where(chosen, earlier, slot_cap)
    token_slots = hot(place, slot_cap).reshape(rows_dev, slots_all)
    slot_tokens = token_slots.T
    slot_experts = (
        jnp.arange(slots_all, dtype=jnp.int32)[:, None] // slot_cap == experts_range[None, :]
    )
    spread = slot_experts.T.astype(LOW)

    per_device = loss_rows.shape[1] // axis_width
    loss_places = loss_rows.reshape(groups, axis_width, per_device)
    at_place = loss_places[..., None] == jnp.arange(rows_dev, dtype=jnp.int32)
    counted_domains = jnp.sum(
        jnp.where(at_place, domains.reshape(groups, axis_width, 1, rows_dev), 0), axis=-1
    )
    all_weights = jnp.exp2(counted_domains.astype(f32) - 2.0)
    weight_total = jnp.sum(all_weights)
    group_weights = by_distance(lax.dynamic_index_in_dim(all_weights, group_index, 0, False), expert_index)
    group_places = lax.dynamic_index_in_dim(loss_places, group_index, 0, False)
    group_targets = jnp.sum(
        jnp.where(
            group_places[..., None] == jnp.arange(rows_dev, dtype=jnp.int32),
            targets.reshape(axis_width, 1, rows_dev),
            0,
        ),
        axis=-1,
    )
    target_local = (by_distance(group_targets, expert_index) - vocab_start).reshape(-1)
    own_choice = hot(by_distance(group_places, expert_index)[0], rows_dev)
    grad_weights = group_weights.reshape(-1) / weight_total

    docs_row = documents[0]
    mask = (positions[:, None] >= positions[None, :]) & (docs_row[:, None] == docs_row[None, :])
    cosine, sine = rope_tables(rows_dev, HD)
    h_first_low = norm_apply(x_first, gain_full[0]).astype(LOW)
    qkv_all = product(h_first_low, w_qkv)
    query = rotate(
        qkv_all[:, :width_model].reshape(rows_dev, heads_count, HD), cosine, sine
    ).astype(LOW)
    key_rot = rotate(
        qkv_all[:, width_model : 2 * width_model].reshape(rows_dev, heads_count, HD), cosine, sine
    ).astype(LOW)
    value_low = qkv_all[:, 2 * width_model :].reshape(rows_dev, heads_count, HD).astype(LOW)
    scores = attention_scores(query, key_rot, mask)
    top_score = jnp.max(scores, axis=-1, keepdims=True)
    expo = jnp.exp(scores - top_score)
    probs = expo / jnp.sum(expo, axis=-1, keepdims=True)
    attended = jnp.einsum(
        "hqk,khd->qhd", probs.astype(LOW), value_low, preferred_element_type=f32
    )
    attended = attended.reshape(rows_dev, width_model).astype(LOW)
    x_mid = x_first + product(attended, w_out)
    h_low = norm_apply(x_mid, gain_full[1]).astype(LOW)

    buffer = product(slot_tokens, h_low).astype(LOW)
    expert_rows = lax.all_to_all(buffer, "expert", split_axis=0, concat_axis=0, tiled=True)

    gate_scores = jnp.where(chosen, jax.nn.sigmoid(product(h_low, w_router)), 0.0)
    gate_total = jnp.sum(gate_scores, axis=1, keepdims=True)
    gates = gate_scores / gate_total
    gate_slots = jnp.concatenate(
        [token_slots * product(part, spread).astype(LOW) for part in split_three(gates)], axis=0
    )
    slot_gates = jnp.sum(
        jnp.where(slot_experts, pick_exact(slot_tokens, gates), 0.0), axis=1, keepdims=True
    )
    down_rows = jnp.arange(hidden_shared, dtype=jnp.int32)
    down_place = (down_rows // own_down) * own_rows + down_rows % own_down
    down_spot = jnp.where(
        down_rows % own_down < own_rows,
        down_place,
        down_place + (devices - 1) * own_rows,
    )
    down_choice = hot(down_spot, 2 * devices * own_rows)
    w_sdown = (
        product(down_choice[:, : devices * own_rows], down_first)
        + product(down_choice[:, devices * own_rows :], down_second)
    ).astype(LOW)
    shared_in = product(h_low, w_shared)
    shared_hidden = swiglu(shared_in[:, :hidden_shared], shared_in[:, hidden_shared:]).astype(LOW)
    shared_out = product(shared_hidden, w_sdown)

    gate_act = inner_cols(expert_rows, w_gate)
    up_act = inner_cols(expert_rows, w_up)
    expert_hidden = swiglu(gate_act, up_act).astype(LOW)
    expert_out = product(expert_hidden, w_down).astype(LOW)
    returned = lax.all_to_all(expert_out, "expert", split_axis=0, concat_axis=0, tiled=True)
    is_target = target_local[:, None] == jnp.arange(vocab_part, dtype=jnp.int32)[None, :]
    target_head = product(is_target.astype(LOW), head).astype(LOW)
    returned, target_head = lax.optimization_barrier((returned, target_head))
    routed = product(gate_slots, returned).reshape(3, rows_dev, width_model)
    x_last = x_mid + shared_out + (routed[0] + routed[1] + routed[2])

    chosen_rows = product(own_choice, norm_apply(x_last, gain_full[2]).astype(LOW)).astype(LOW)
    gathered = expert_gather(chosen_rows).reshape(axis_width * per_device, width_model)
    logits = inner_cols(gathered, head)
    row_top = jnp.max(logits, axis=1)
    expos = jnp.exp(logits - row_top[:, None])
    row_total = jnp.sum(expos, axis=1)
    row_target = jnp.sum(jnp.where(is_target, logits, 0.0), axis=1)
    rest_low = jnp.where(is_target, 0.0, expos).astype(LOW)
    d_rest = product(rest_low, head)
    stats, d_rest = meet_stats(
        jnp.stack([row_top, row_total, row_target]).reshape(3, axis_width, per_device), d_rest
    )
    log_norm = (stats[0] + jnp.log(stats[1])).reshape(-1)
    entropy = log_norm.reshape(axis_width, per_device)[0] - stats[2, 0]
    own_loss = jnp.sum(group_weights[0] * entropy)
    rest_scale = jnp.exp(row_top - log_norm) * grad_weights
    target_grad = (jnp.exp(stats[2].reshape(-1) - log_norm) - 1.0) * grad_weights
    d_rows_all = d_rest * rest_scale[:, None] + target_grad[:, None] * target_head.astype(f32)
    d_chosen = expert_sum(
        d_rows_all.astype(LOW).reshape(axis_width, per_device, width_model)
    ).astype(f32)
    d_logits = jnp.where(
        is_target, target_grad[:, None], rest_low.astype(f32) * rest_scale[:, None]
    ).astype(LOW)
    d_head_part = 0.0
    for k in range(groups):
        columns = lax.dynamic_slice_in_dim(
            gathered, (group_index ^ k) * part_width, part_width, axis=1
        )
        d_columns = inner_rows(d_logits, columns).astype(LOW)
        d_columns = d_columns if k == 0 else swap_group(d_columns, k)
        d_head_part = d_head_part + d_columns.astype(f32)

    _, final_back = jax.vjp(norm_apply, x_last, gain_full[2])
    d_last, d_gain_last = final_back(pick_exact(own_choice.T, d_chosen))
    d_branch = d_last.astype(LOW)
    d_last_parts = split_three(d_last)

    d_buffer = (sum(product(slot_tokens, part) for part in d_last_parts) * slot_gates).astype(LOW)
    d_rows = lax.all_to_all(d_buffer, "expert", split_axis=0, concat_axis=0, tiled=True)

    d_slots = inner_cols(jnp.concatenate(d_last_parts, axis=0), returned)
    d_slots = jnp.sum(d_slots.reshape(3, rows_dev, slots_all), axis=0) * token_slots.astype(f32)
    d_gates = sum(inner_cols(part, spread) for part in split_three(d_slots))
    d_scores = (d_gates - jnp.sum(gates * d_gates, axis=1, keepdims=True)) / gate_total
    d_router_logits = jnp.where(chosen, d_scores * gate_scores * (1.0 - gate_scores), 0.0)
    d_hmid = inner_cols(d_router_logits, w_router.astype(f32), HIGH)

    _, shared_back = jax.vjp(swiglu, shared_in[:, :hidden_shared], shared_in[:, hidden_shared:])
    d_gate_shared, d_up_shared = shared_back(inner_cols(d_branch, w_sdown))
    d_shared_in = jnp.concatenate([d_gate_shared, d_up_shared], axis=1).astype(LOW)
    d_hmid = d_hmid + inner_cols(d_shared_in, w_shared)

    features = jnp.arange(width_model, dtype=jnp.int32)
    owner, row = features // own_rows, features % own_rows
    turned = (owner % axis_width) * groups + owner // axis_width
    turn_choice = hot(turned * own_rows + row, width_model)
    downs, down_row = down_rows // own_down, down_rows % own_down
    down_turned = ((downs % axis_width) * groups + downs // axis_width) * own_rows
    down_firsts = hot(jnp.where(down_row < own_rows, down_turned + down_row, -1), width_model)
    down_seconds = hot(
        jnp.where(down_row < own_rows, -1, down_turned + down_row - own_rows), width_model
    )
    h_mid_turned = product(h_low, turn_choice).astype(LOW)
    d_wrouter = sum(
        inner_rows(h_mid_turned, part) for part in split_three(d_router_logits)
    ).astype(LOW)
    early = jnp.concatenate(
        [
            inner_rows(product(shared_hidden, down_firsts).astype(LOW), d_branch).astype(LOW),
            inner_rows(product(shared_hidden, down_seconds).astype(LOW), d_branch).astype(LOW),
            inner_rows(h_mid_turned, d_shared_in).astype(LOW),
            jnp.pad(d_wrouter, ((0, 0), (0, -experts % 128))),
        ],
        axis=1,
    )
    d_rows, early = lax.optimization_barrier((d_rows, early))
    early = lax.psum_scatter(early, "expert", scatter_dimension=0, tiled=True)

    d_expert_hidden = inner_cols(d_rows, w_down)
    _, expert_back = jax.vjp(swiglu, gate_act, up_act)
    d_gate_expert, d_up_expert = expert_back(d_expert_hidden)
    d_gate_expert = d_gate_expert.astype(LOW)
    d_up_expert = d_up_expert.astype(LOW)
    d_sent = (product(d_gate_expert, w_gate) + product(d_up_expert, w_up)).astype(LOW)
    d_returned = lax.all_to_all(d_sent, "expert", split_axis=0, concat_axis=0, tiled=True)
    expert_rows, expert_hidden, d_rows = after((expert_rows, expert_hidden, d_rows), d_sent)
    d_experts = jnp.stack(
        [
            inner_rows(d_gate_expert, expert_rows).astype(LOW),
            inner_rows(d_up_expert, expert_rows).astype(LOW),
            inner_rows(expert_hidden, d_rows).astype(LOW),
        ]
    )
    d_returned, d_experts = lax.optimization_barrier((d_returned, d_experts))
    own_hidden = hidden // groups
    experts_part = d_experts[:, :own_hidden].astype(f32)
    for k in range(1, groups):
        part = swap_group(d_experts[:, k * own_hidden : (k + 1) * own_hidden], k)
        experts_part = experts_part + part.astype(f32)

    d_hmid = d_hmid + product(token_slots, d_returned)
    _, mid_back = jax.vjp(norm_apply, x_mid, gain_full[1])
    d_mid_part, d_gain_mid = mid_back(d_hmid)
    d_mid = d_last + d_mid_part
    d_att_in = d_mid.astype(LOW)
    d_attended = inner_cols(d_att_in, w_out).astype(LOW).reshape(rows_dev, heads_count, HD)
    d_value = jnp.einsum("hqk,qhd->khd", probs.astype(LOW), d_attended, preferred_element_type=f32)
    d_probs = jnp.einsum("qhd,khd->hqk", d_attended, value_low, preferred_element_type=f32)
    d_scores = (probs * (d_probs - jnp.sum(probs * d_probs, axis=-1, keepdims=True))).astype(LOW)
    scale_query = 1.0 / math.sqrt(HD)
    d_query = (
        jnp.einsum("hqk,khd->qhd", d_scores, key_rot, preferred_element_type=f32) * scale_query
    )
    d_key = jnp.einsum("hqk,qhd->khd", d_scores, query, preferred_element_type=f32) * scale_query
    d_qkv = jnp.concatenate(
        [
            rotate(d_query, cosine, -sine).reshape(rows_dev, width_model),
            rotate(d_key, cosine, -sine).reshape(rows_dev, width_model),
            d_value.reshape(rows_dev, width_model),
        ],
        axis=1,
    ).astype(LOW)
    _, first_back = jax.vjp(norm_apply, x_first, gain_full[0])
    d_first_part, d_gain_first = first_back(inner_cols(d_qkv, w_qkv))
    d_first = (d_mid + d_first_part).astype(LOW)

    d_first_blocks = by_distance(
        d_first.reshape(rows_dev, groups, part_width).swapaxes(0, 1), group_index
    )
    d_embed = 0.0
    for k in range(groups):
        block = d_first_blocks[k] if k == 0 else swap_group(d_first_blocks[k], k)
        tokens = ordered_gather(block, k)
        for core in (0, 1):
            words = hot(local_ids[k][:, :, core].reshape(-1), vocab_part)
            part = tokens if core == 0 else swap(tokens, 1)
            d_embed = d_embed + inner_rows(words, part.reshape(-1, part_width))

    d_qkv, d_att_in = after((d_qkv, d_att_in), d_first_blocks)
    gain_grad = jnp.stack([d_gain_first, d_gain_mid, d_gain_last], axis=1)
    gain_grad = jnp.pad(gain_grad, ((0, 0), (0, 128 - gain_grad.shape[1])))
    late = []
    for stream, (left, right) in enumerate(
        (
            (h_first_low, d_qkv[:, 2 * width_model :]),
            (h_first_low, d_qkv[:, width_model : 2 * width_model]),
            (h_first_low, d_qkv[:, :width_model]),
            (attended, d_att_in),
        )
    ):
        distance = (owner % axis_width) ^ expert_index
        axes = [rank_in_order(distance >> 3, stream), rank_in_order((distance >> 1) & 3, stream)]
        first_axis, second_axis = axes if stream < 2 else axes[::-1]
        spot = ((distance & 1) * 16 + first_axis * 4 + second_axis) * groups + owner // axis_width
        choice = hot(spot * own_rows + row, width_model)
        left = product(left, choice).astype(LOW)
        half = width_model // 2
        grad = inner_rows(left, right)
        if stream == 2:
            high, middle, _ = split_three(gain_grad)
            gain_turned = inner_rows(choice, high) + inner_rows(choice, middle)
            grad = jnp.concatenate([grad, gain_turned], axis=1)
        grad = grad.astype(LOW)
        grad = add_low(grad[:half], swap(grad[half:], 1))
        grad = ordered_sum(grad.reshape(4, 4, groups * own_rows, -1), stream)
        late.append(grad)
    late = jnp.concatenate(late[:2] + [late[3], late[2]], axis=1)
    parts = []
    for part in (early, late):
        part = lax.all_to_all(part, "dp", split_axis=0, concat_axis=0, tiled=True)
        parts.append(jnp.sum(part.reshape(groups, own_rows, -1).astype(f32), axis=0))
    early, late = parts
    dense_part = jnp.concatenate(
        [
            late[:, 3 * width_model : 4 * width_model],
            late[:, width_model : 2 * width_model],
            late[:, :width_model],
            late[:, 2 * width_model : 3 * width_model],
            early[:, 2 * width_model : 2 * width_model + 2 * hidden_shared + experts],
        ],
        axis=1,
    )
    shared_part = jnp.concatenate(
        [early[:, :width_model], early[: own_down - own_rows, width_model : 2 * width_model]],
        axis=0,
    )
    gains_part = late[:, 4 * width_model : 4 * width_model + gains.shape[0]].T
    up_part = experts_part[:2]
    down_part = experts_part[2:]

    grads = (dense_part, shared_part, gains_part, d_embed, d_head_part, up_part, down_part)
    squares = sum(jnp.sum(grad_part * grad_part) for grad_part in grads)
    counts = jnp.sum(chosen.astype(f32), axis=0)
    sums = jnp.concatenate([squares[None], own_loss[None], counts, jnp.zeros((126 - experts,), f32)])
    sums = lax.all_to_all(
        jnp.broadcast_to(sums[None], (devices, 128)), BOTH, split_axis=0, concat_axis=0, tiled=True
    )
    sums = jnp.sum(sums, axis=0)
    total_squares, loss_total, counts_all = sums[0], sums[1], sums[2 : 2 + experts]
    norm_value = jnp.sqrt(total_squares)
    clip_scale = jnp.minimum(1.0, CLIP_NORM / (norm_value + 1e-06))
    tables_part = jnp.stack([d_embed, d_head_part], axis=1)
    grads = (dense_part, shared_part, gains_part, tables_part, up_part, down_part)
    masters = (dense_rows, shared_down, gains, tables, expert_up, expert_down)
    firsts = (dense_m, shared_m, gains_m, tables_m, up_m, down_m)
    seconds = (dense_v, shared_v, gains_v, tables_v, up_v, down_v)

    def turn(index, value):
        if index == 3:
            return value.swapaxes(0, 1)
        return value[0].swapaxes(1, 2) if index == 4 else value

    def turn_back(index, value):
        if index == 3:
            return value.swapaxes(0, 1)
        return value.swapaxes(1, 2)[None] if index == 4 else value

    updated = []
    for index in range(6):
        state = [turn(index, value[index]) for value in (masters, firsts, seconds)]
        new = adam_update(state[0], grads[index], *state[1:], RATES[index], clip_scale)
        updated.append(tuple(turn_back(index, value) for value in new))
    mean_load = jnp.sum(counts_all) / experts
    bias_new = expert_bias + BIAS_RATE * jnp.sign(mean_load - counts_all)
    return (
        *(new[0] for new in updated),
        *(new[1] for new in updated),
        *(new[2] for new in updated),
        bias_new,
        norm_value,
        loss_total,
        weight_total,
    )


def solution(mesh):
    in_specs = (
        P("dp", None),
        P("dp", None),
        P(("dp", "expert"), None),
        P(),
        P(),
        P(("dp", "expert"), None),
        P(("dp", "expert"), None),
        P(("dp", "expert"), None),
        P(None, ("dp", "expert")),
        P(None, "expert", "dp"),
        P("expert", None, None, "dp"),
        P("expert", "dp", None),
        P(("dp", "expert"), None),
        P(("dp", "expert"), None),
        P(None, ("dp", "expert")),
        P(None, "expert", "dp"),
        P("expert", None, None, "dp"),
        P("expert", "dp", None),
        P(("dp", "expert"), None),
        P(("dp", "expert"), None),
        P(None, ("dp", "expert")),
        P(None, "expert", "dp"),
        P("expert", None, None, "dp"),
        P("expert", "dp", None),
        P(),
    )
    out_specs = (
        P(("dp", "expert"), None),
        P(("dp", "expert"), None),
        P(None, ("dp", "expert")),
        P(None, "expert", "dp"),
        P("expert", None, None, "dp"),
        P("expert", "dp", None),
        P(("dp", "expert"), None),
        P(("dp", "expert"), None),
        P(None, ("dp", "expert")),
        P(None, "expert", "dp"),
        P("expert", None, None, "dp"),
        P("expert", "dp", None),
        P(("dp", "expert"), None),
        P(("dp", "expert"), None),
        P(None, ("dp", "expert")),
        P(None, "expert", "dp"),
        P("expert", None, None, "dp"),
        P("expert", "dp", None),
        P(),
        P(),
        P(),
        P(),
    )
    return jax.shard_map(body, mesh=mesh, in_specs=in_specs, out_specs=out_specs, check_vma=False)
```

```python
import functools
import math

import jax
import jax.numpy as jnp
from jax import lax
from jax.experimental import pallas as pl
from jax.experimental.pallas import tpu as pltpu
from jax.sharding import PartitionSpec as P

HD = 128
TOP = 6
STEP = 10


NORM_EPS = 1e-06
HIGH = lax.Precision.HIGHEST
BETA_ONE = 0.9
BETA_TWO = 0.95
ADAM_EPS = 1e-08
DECAY = 0.1
CLIP_NORM = 0.02
BIAS_RATE = 0.05
ROPE_BASE = 10000.0
RATES = (0.03, 0.03, 0.5, 0.4, 0.03, 0.5)
MASKED = -1e30
LOW = jnp.bfloat16
BOTH = ("dp", "expert")
STREAMS = 4


def product(left, right):
    return jnp.dot(left, right, preferred_element_type=jnp.float32)


def inner_rows(left, right, precision=None):
    return lax.dot_general(
        left,
        right,
        (((0,), (0,)), ((), ())),
        precision=precision,
        preferred_element_type=jnp.float32,
    )


def inner_cols(left, right, precision=None):
    return lax.dot_general(
        left,
        right,
        (((1,), (1,)), ((), ())),
        precision=precision,
        preferred_element_type=jnp.float32,
    )


def split_three(values):
    high = values.astype(LOW)
    rest = values - high.astype(jnp.float32)
    middle = rest.astype(LOW)
    last = (rest - middle.astype(jnp.float32)).astype(LOW)
    return high, middle, last


def pick_exact(choice, values):
    return sum(product(choice, part) for part in split_three(values))


def norm_apply(values, gain_row):
    return (
        values * lax.rsqrt(jnp.mean(values * values, axis=-1, keepdims=True) + NORM_EPS) * gain_row
    )


def swiglu(gate_act, up_act):
    return jax.nn.silu(gate_act) * up_act


def rope_tables(length, head_size):
    positions = jnp.arange(length, dtype=jnp.float32)
    frequency = ROPE_BASE ** (-2.0 * jnp.arange(head_size // 2, dtype=jnp.float32) / head_size)
    angles = positions[:, None] * frequency[None, :]
    return (jnp.cos(angles)[:, None, :], jnp.sin(angles)[:, None, :])


def rotate(values, cosine, sine):
    half_size = values.shape[-1] // 2
    first_half = values[..., :half_size]
    second_half = values[..., half_size:]
    return jnp.concatenate(
        [first_half * cosine - second_half * sine, second_half * cosine + first_half * sine],
        axis=-1,
    )


def adam_update(weight, grad, first, second, rate, clip_scale):
    grad = grad * clip_scale
    first = BETA_ONE * first + (1.0 - BETA_ONE) * grad
    second = BETA_TWO * second + (1.0 - BETA_TWO) * grad * grad
    first_fix = first / (1.0 - BETA_ONE**STEP)
    second_fix = second / (1.0 - BETA_TWO**STEP)
    weight = weight - rate * (first_fix / (jnp.sqrt(second_fix) + ADAM_EPS) + DECAY * weight)
    return (weight, first, second)


def tables_kernel(rate, clip, weight, grad, first, second, weight_out, first_out, second_out):
    new = adam_update(weight[...], grad[...], first[...], second[...], rate, clip[0, 0])
    weight_out[...], first_out[...], second_out[...] = new


def tables_update(weight, grad, first, second, rate, clip_scale):
    words, pair, width = weight.shape
    rows = max(count for count in range(1, 257) if words % count == 0)
    block = pl.BlockSpec((rows, pair, width), lambda i: (i, 0, 0))
    return pl.pallas_call(
        functools.partial(tables_kernel, rate),
        grid=(words // rows,),
        in_specs=[pl.BlockSpec(memory_space=pltpu.SMEM)] + [block] * 4,
        out_specs=[block] * 3,
        out_shape=[jax.ShapeDtypeStruct(weight.shape, jnp.float32)] * 3,
        compiler_params=pltpu.CompilerParams(vmem_limit_bytes=48 * 1024 * 1024),
        name="tables_update",
    )(clip_scale.reshape(1, 1), weight, grad, first, second)


def swap(value, number):
    return lax.ppermute(value, "expert", [(i, i ^ number) for i in range(32)])


def swap_group(value, number):
    return lax.ppermute(value, "dp", [(i, i ^ number) for i in range(4)])


def by_distance(values, index):
    shape = values.shape
    rest = shape[1:]
    for bit in range(shape[0].bit_length() - 1):
        halves = values.reshape((shape[0] >> (bit + 1), 2, 1 << bit) + rest)
        values = jnp.where(((index >> bit) & 1) == 1, halves[:, ::-1], halves)
    return values.reshape(shape)


def after(values, trigger):
    return lax.optimization_barrier((values, trigger))[0]


def add_low(left, right):
    return (left.astype(jnp.float32) + right.astype(jnp.float32)).astype(LOW)


def ring_sum(blocks, shift, other_way):
    near, far = (3, 1) if other_way else (1, 3)
    if other_way:
        sent = jnp.stack([blocks[3], blocks[2]])
        kept = blocks[0:2]
    else:
        sent = blocks[1:3]
        kept = jnp.stack([blocks[0], blocks[3]])
    kept = add_low(kept, swap(sent, near << shift))
    return add_low(kept[0], swap(kept[1], far << shift))


def ring_gather(block, shift, other_way):
    near, far = (3, 1) if other_way else (1, 3)
    pair = jnp.stack([block, swap(block, far << shift)])
    met = swap(pair, near << shift)
    if other_way:
        return jnp.stack([pair[0], pair[1], met[1], met[0]])
    return jnp.stack([pair[0], met[0], met[1], pair[1]])


ORDERS = ((0, 3, 1, 2), (0, 1, 3, 2))


def in_order(values, stream):
    order = ORDERS[stream % 2]
    if stream >= 2:
        values = jnp.swapaxes(values, 0, 1)
    values = jnp.stack([values[i] for i in order])
    return jnp.stack([values[:, i] for i in order], axis=1)


def rank_in_order(distance, stream):
    return sum(
        jnp.where(distance == number, spot, 0) for spot, number in enumerate(ORDERS[stream % 2])
    )


def steps_of(stream):
    near, far = (3, 1) if stream % 2 == 1 else (1, 3)
    shifts = (3, 1) if stream < 2 else (1, 3)
    return [number << shift for shift in shifts for number in (near, far)]


def ordered_sum(blocks, stream):
    shape = blocks.shape[2:]
    blocks = blocks.reshape((16,) + shape)
    for number in steps_of(stream):
        half = blocks.shape[0] // 2
        blocks = add_low(blocks[:half], swap(blocks[half:], number))
    return blocks[0]


def ordered_gather(block, stream):
    blocks = block[None]
    for number in reversed(steps_of(stream)):
        blocks = jnp.concatenate([blocks, swap(blocks, number)], axis=0)
    return blocks


def plane_sum(blocks, stream):
    other_way = stream % 2 == 1
    if stream // 2 == 0:
        return ring_sum(ring_sum(blocks, 3, other_way), 1, other_way)
    turned = jnp.swapaxes(blocks, 0, 1)
    return ring_sum(ring_sum(turned, 1, other_way), 3, other_way)


def plane_gather(block, stream):
    other_way = stream % 2 == 1
    if stream // 2 == 0:
        return ring_gather(ring_gather(block, 1, other_way), 3, other_way)
    return jnp.swapaxes(
        ring_gather(ring_gather(block, 3, other_way), 1, other_way), 0, 1
    )


def expert_sum(blocks):
    _, rows, width = blocks.shape
    blocks = blocks.reshape(4, 4, 2, STREAMS, rows // STREAMS, width)
    mine = add_low(blocks[:, :, 0], swap(blocks[:, :, 1], 1))
    return jnp.concatenate([plane_sum(mine[:, :, s], s) for s in range(STREAMS)], axis=0)


def expert_gather(block):
    rows, width = block.shape
    part = rows // STREAMS
    mine = jnp.stack(
        [plane_gather(block[s * part : (s + 1) * part], s) for s in range(STREAMS)], axis=2
    )
    return jnp.stack([mine, swap(mine, 1)], axis=2).reshape(32, rows, width)


def merge_stats(first_part, second_part):
    top_value = jnp.maximum(first_part[0], second_part[0])
    total_exp = first_part[1] * jnp.exp(first_part[0] - top_value) + second_part[1] * jnp.exp(
        second_part[0] - top_value
    )
    return jnp.stack([top_value, total_exp, first_part[2] + second_part[2]])


def flip_blocks(stats, number):
    rows = stats.shape[-1]
    stats = stats.reshape(3, 2, 2, 2, 2, 2, rows)
    axes = [5 - bit for bit in range(5) if (number >> bit) & 1]
    return jnp.flip(stats, axes).reshape(3, 32, rows)


def meet_stats(stats, beside):
    for shift in (3, 1):
        others = [swap(stats, k << shift) for k in (1, 2, 3)]
        if shift == 3:
            others = after(others, beside)
        for k, other in enumerate(others, 1):
            stats = merge_stats(stats, flip_blocks(other, k << shift))
    return merge_stats(stats, flip_blocks(swap(stats, 1), 1))


def hot(indices, count):
    return (indices[..., None] == jnp.arange(count, dtype=jnp.int32)).astype(LOW)


def attention_scores(query, key_rot, mask):
    scores = jnp.einsum("qhd,khd->hqk", query, key_rot, preferred_element_type=jnp.float32) * (
        1.0 / math.sqrt(HD)
    )
    return jnp.where(mask[None], scores, MASKED)


def body(
    ids,
    targets,
    documents,
    domains,
    loss_rows,
    routes,
    dense_rows,
    shared_down,
    gains,
    tables,
    expert_up,
    expert_down,
    dense_m,
    shared_m,
    gains_m,
    tables_m,
    up_m,
    down_m,
    dense_v,
    shared_v,
    gains_v,
    tables_v,
    up_v,
    down_v,
    expert_bias,
):
    f32 = jnp.float32
    groups = lax.axis_size("dp")
    axis_width = lax.axis_size("expert")
    expert_index = lax.axis_index("expert")
    group_index = lax.axis_index("dp")
    devices = groups * axis_width
    rows_dev = routes.shape[0]
    own_rows, dense_width = dense_rows.shape
    own_down, width_model = shared_down.shape
    hidden_shared = own_down * devices
    heads_count = width_model // HD
    experts = expert_bias.shape[0]
    slot_cap = min(rows_dev, rows_dev * TOP * 4 // (3 * experts))
    slots_all = experts * slot_cap
    vocab_part = tables.shape[1]
    part_width = tables.shape[2]
    vocab_start = expert_index * vocab_part
    hidden = expert_down.shape[1] * groups

    gap = -(dense_width + gains.shape[0]) % 128
    down_low = shared_down.astype(LOW)
    packed = jnp.concatenate(
        [
            dense_rows.astype(LOW),
            gains.astype(LOW).T,
            jnp.zeros((own_rows, gap), LOW),
            down_low[:own_rows],
            jnp.pad(down_low[own_rows:], ((0, 2 * own_rows - own_down), (0, 0))),
        ],
        axis=1,
    )
    packed_all = lax.all_gather(packed, BOTH, axis=0, tiled=True)
    start = dense_width + gains.shape[0] + gap
    router_start = 4 * width_model + 2 * hidden_shared
    w_qkv = packed_all[:, : 3 * width_model]
    w_out = packed_all[:, 3 * width_model : 4 * width_model]
    w_shared = packed_all[:, 4 * width_model : router_start]
    w_router = packed_all[:, router_start:dense_width]
    gain_full = packed_all[:, dense_width : dense_width + gains.shape[0]].T.astype(f32)
    down_first = packed_all[:, start : start + width_model]
    down_second = packed_all[:, start + width_model :]

    ids_all = lax.all_to_all(
        jnp.broadcast_to(ids, (groups,) + ids.shape[1:]), "dp", split_axis=0, concat_axis=0, tiled=True
    ).reshape(groups, axis_width, rows_dev)
    ids_near = by_distance(ids_all.swapaxes(0, 1), expert_index) - vocab_start
    ids_near = ids_near.reshape(4, 4, 2, groups, rows_dev)
    ids_near = jnp.stack([in_order(ids_near[:, :, :, s], s) for s in range(groups)])
    table_words = tables[0].astype(LOW)
    looked_up = []
    for core in (1, 0):
        found = product(hot(ids_near[:, :, :, core].reshape(-1), vocab_part), table_words)
        looked_up.append(found.astype(LOW).reshape(groups, 16 * rows_dev, part_width))
    looked_up = add_low(looked_up[1], swap(looked_up[0], 1))
    routes, loss_rows, domains, targets, documents = after(
        (routes, loss_rows, domains, targets, documents), looked_up
    )
    x_first = jnp.stack(
        [
            ordered_sum(looked_up[s].reshape(4, 4, rows_dev, part_width), s)
            for s in range(groups)
        ]
    )
    x_first = lax.all_to_all(x_first, "dp", split_axis=0, concat_axis=0, tiled=True)
    x_first = x_first.swapaxes(0, 1).reshape(rows_dev, width_model).astype(f32)

    expert_part = jnp.concatenate(
        [expert_up[0].astype(LOW).swapaxes(1, 2), expert_down.astype(LOW)], axis=0
    )
    expert_all = lax.all_gather(expert_part, "dp", axis=1, tiled=True)
    w_gate, w_up, w_down = expert_all[0], expert_all[1], expert_all[2]

    positions = jnp.arange(rows_dev)
    experts_range = jnp.arange(experts, dtype=jnp.int32)
    chosen = jnp.any(routes[:, :, None] == experts_range[None, None, :], axis=1)
    earlier = product(
        (positions[:, None] > positions[None, :]).astype(LOW), chosen.astype(LOW)
    ).astype(jnp.int32)
    place = jnp.where(chosen, earlier, slot_cap)
    token_slots = hot(place, slot_cap).reshape(rows_dev, slots_all)
    slot_tokens = token_slots.T
    slot_experts = (
        jnp.arange(slots_all, dtype=jnp.int32)[:, None] // slot_cap == experts_range[None, :]
    )
    spread = slot_experts.T.astype(LOW)

    per_device = loss_rows.shape[1] // axis_width
    loss_places = loss_rows.reshape(groups, axis_width, per_device)
    at_place = loss_places[..., None] == jnp.arange(rows_dev, dtype=jnp.int32)
    counted_domains = jnp.sum(
        jnp.where(at_place, domains.reshape(groups, axis_width, 1, rows_dev), 0), axis=-1
    )
    all_weights = jnp.exp2(counted_domains.astype(f32) - 2.0)
    weight_total = jnp.sum(all_weights)
    group_weights = by_distance(lax.dynamic_index_in_dim(all_weights, group_index, 0, False), expert_index)
    group_places = lax.dynamic_index_in_dim(loss_places, group_index, 0, False)
    group_targets = jnp.sum(
        jnp.where(
            group_places[..., None] == jnp.arange(rows_dev, dtype=jnp.int32),
            targets.reshape(axis_width, 1, rows_dev),
            0,
        ),
        axis=-1,
    )
    target_local = (by_distance(group_targets, expert_index) - vocab_start).reshape(-1)
    own_choice = hot(by_distance(group_places, expert_index)[0], rows_dev)
    grad_weights = group_weights.reshape(-1) / weight_total

    docs_row = documents[0]
    mask = (positions[:, None] >= positions[None, :]) & (docs_row[:, None] == docs_row[None, :])
    cosine, sine = rope_tables(rows_dev, HD)
    h_first_low = norm_apply(x_first, gain_full[0]).astype(LOW)
    qkv_all = product(h_first_low, w_qkv)
    query = rotate(
        qkv_all[:, :width_model].reshape(rows_dev, heads_count, HD), cosine, sine
    ).astype(LOW)
    key_rot = rotate(
        qkv_all[:, width_model : 2 * width_model].reshape(rows_dev, heads_count, HD), cosine, sine
    ).astype(LOW)
    value_low = qkv_all[:, 2 * width_model :].reshape(rows_dev, heads_count, HD).astype(LOW)
    scores = attention_scores(query, key_rot, mask)
    top_score = jnp.max(scores, axis=-1, keepdims=True)
    expo = jnp.exp(scores - top_score)
    probs = expo / jnp.sum(expo, axis=-1, keepdims=True)
    attended = jnp.einsum(
        "hqk,khd->qhd", probs.astype(LOW), value_low, preferred_element_type=f32
    )
    attended = attended.reshape(rows_dev, width_model).astype(LOW)
    head = lax.all_gather(after(tables[1].astype(LOW), attended), "dp", axis=1, tiled=True)
    x_mid = x_first + product(attended, w_out)
    h_low = norm_apply(x_mid, gain_full[1]).astype(LOW)

    buffer = product(slot_tokens, h_low).astype(LOW)
    expert_rows = lax.all_to_all(buffer, "expert", split_axis=0, concat_axis=0, tiled=True)

    gate_scores = jnp.where(chosen, jax.nn.sigmoid(product(h_low, w_router)), 0.0)
    gate_total = jnp.sum(gate_scores, axis=1, keepdims=True)
    gates = gate_scores / gate_total
    gate_slots = jnp.concatenate(
        [token_slots * product(part, spread).astype(LOW) for part in split_three(gates)], axis=0
    )
    slot_gates = jnp.sum(
        jnp.where(slot_experts, pick_exact(slot_tokens, gates), 0.0), axis=1, keepdims=True
    )
    down_rows = after(jnp.arange(hidden_shared, dtype=jnp.int32), buffer)
    down_place = (down_rows // own_down) * own_rows + down_rows % own_down
    down_spot = jnp.where(
        down_rows % own_down < own_rows,
        down_place,
        down_place + (devices - 1) * own_rows,
    )
    down_choice = hot(down_spot, 2 * devices * own_rows)
    w_sdown = (
        product(down_choice[:, : devices * own_rows], down_first)
        + product(down_choice[:, devices * own_rows :], down_second)
    ).astype(LOW)
    shared_in = product(h_low, w_shared)
    shared_hidden = swiglu(shared_in[:, :hidden_shared], shared_in[:, hidden_shared:]).astype(LOW)
    shared_out = product(shared_hidden, w_sdown)

    gate_act = inner_cols(expert_rows, w_gate)
    up_act = inner_cols(expert_rows, w_up)
    expert_hidden = swiglu(gate_act, up_act).astype(LOW)
    expert_out = product(expert_hidden, w_down).astype(LOW)
    returned = lax.all_to_all(expert_out, "expert", split_axis=0, concat_axis=0, tiled=True)
    is_target = target_local[:, None] == jnp.arange(vocab_part, dtype=jnp.int32)[None, :]
    target_head = product(is_target.astype(LOW), head).astype(LOW)
    returned = after(returned, target_head)
    routed = product(gate_slots, returned).reshape(3, rows_dev, width_model)
    x_last = x_mid + shared_out + (routed[0] + routed[1] + routed[2])

    chosen_rows = product(own_choice, norm_apply(x_last, gain_full[2]).astype(LOW)).astype(LOW)
    gathered = expert_gather(chosen_rows).reshape(axis_width * per_device, width_model)
    logits = inner_cols(gathered, head)
    row_top = jnp.max(logits, axis=1)
    expos = jnp.exp(logits - row_top[:, None])
    row_total = jnp.sum(expos, axis=1)
    row_target = jnp.sum(jnp.where(is_target, logits, 0.0), axis=1)
    rest_low = jnp.where(is_target, 0.0, expos).astype(LOW)
    d_rest = product(rest_low, head)
    stats = meet_stats(
        jnp.stack([row_top, row_total, row_target]).reshape(3, axis_width, per_device), d_rest
    )
    log_norm = (stats[0] + jnp.log(stats[1])).reshape(-1)
    entropy = log_norm.reshape(axis_width, per_device)[0] - stats[2, 0]
    own_loss = jnp.sum(group_weights[0] * entropy)
    rest_scale = jnp.exp(row_top - log_norm) * grad_weights
    target_grad = (jnp.exp(stats[2].reshape(-1) - log_norm) - 1.0) * grad_weights
    d_rows_all = d_rest * rest_scale[:, None] + target_grad[:, None] * target_head.astype(f32)
    d_rows_all = d_rows_all.astype(LOW)
    d_logits = jnp.where(
        is_target, target_grad[:, None], rest_low.astype(f32) * rest_scale[:, None]
    ).astype(LOW)
    d_chosen = expert_sum(d_rows_all.reshape(axis_width, per_device, width_model)).astype(f32)

    _, final_back = jax.vjp(norm_apply, x_last, gain_full[2])
    d_last, d_gain_last = final_back(pick_exact(own_choice.T, d_chosen))
    d_branch = d_last.astype(LOW)
    d_last_parts = split_three(d_last)

    d_buffer = (sum(product(slot_tokens, part) for part in d_last_parts) * slot_gates).astype(LOW)
    d_rows = lax.all_to_all(d_buffer, "expert", split_axis=0, concat_axis=0, tiled=True)

    _, shared_back = jax.vjp(swiglu, shared_in[:, :hidden_shared], shared_in[:, hidden_shared:])
    d_gate_shared, d_up_shared = shared_back(inner_cols(d_branch, w_sdown))
    d_shared_in = jnp.concatenate([d_gate_shared, d_up_shared], axis=1).astype(LOW)
    d_hmid = inner_cols(d_shared_in, w_shared)

    features = jnp.arange(width_model, dtype=jnp.int32)
    owner, row = features // own_rows, features % own_rows
    turned = (owner % axis_width) * groups + owner // axis_width
    turn_choice = hot(turned * own_rows + row, width_model)
    downs, down_row = down_rows // own_down, down_rows % own_down
    down_turned = ((downs % axis_width) * groups + downs // axis_width) * own_rows
    down_firsts = hot(jnp.where(down_row < own_rows, down_turned + down_row, -1), width_model)
    down_seconds = hot(
        jnp.where(down_row < own_rows, -1, down_turned + down_row - own_rows), width_model
    )
    early_left = after((h_low, shared_hidden), d_buffer)
    h_mid_turned = product(early_left[0], turn_choice).astype(LOW)
    left = jnp.concatenate(
        [
            h_mid_turned,
            product(early_left[1], down_firsts).astype(LOW),
            product(early_left[1], down_seconds).astype(LOW),
        ],
        axis=0,
    )

    def spread_out(before, value, behind):
        return jnp.pad(value, ((0, 0), (before, behind)))

    right = jnp.concatenate(
        [
            spread_out(0, d_shared_in, 2 * width_model),
            spread_out(2 * hidden_shared, d_branch, width_model),
            spread_out(2 * hidden_shared + width_model, d_branch, 0),
        ],
        axis=0,
    )
    early = inner_rows(left, right).astype(LOW)
    d_logits, gathered = after((d_logits, gathered), d_buffer)
    d_head = inner_rows(d_logits, gathered).astype(LOW)

    def head_block(k):
        return lax.dynamic_slice_in_dim(
            d_head, (group_index ^ k) * part_width, part_width, axis=1
        )

    head_parts = [head_block(0), swap_group(head_block(1), 1), swap_group(head_block(3), 3)]
    d_rows = after(d_rows, (early, head_parts[1:]))
    early = lax.psum_scatter(early, "expert", scatter_dimension=0, tiled=True)

    d_expert_hidden = inner_cols(d_rows, w_down)
    _, expert_back = jax.vjp(swiglu, gate_act, up_act)
    d_gate_expert, d_up_expert = expert_back(d_expert_hidden)
    d_gate_expert = d_gate_expert.astype(LOW)
    d_up_expert = d_up_expert.astype(LOW)
    d_sent = (product(d_gate_expert, w_gate) + product(d_up_expert, w_up)).astype(LOW)
    d_returned = lax.all_to_all(d_sent, "expert", split_axis=0, concat_axis=0, tiled=True)
    d_last_late, returned = after((d_last_parts, returned), d_sent)
    d_slots = inner_cols(jnp.concatenate(d_last_late, axis=0), returned)
    d_slots = jnp.sum(d_slots.reshape(3, rows_dev, slots_all), axis=0) * token_slots.astype(f32)
    d_gates = sum(inner_cols(part, spread) for part in split_three(d_slots))
    d_scores = (d_gates - jnp.sum(gates * d_gates, axis=1, keepdims=True)) / gate_total
    d_router_logits = jnp.where(chosen, d_scores * gate_scores * (1.0 - gate_scores), 0.0)
    d_hmid = d_hmid + inner_cols(d_router_logits, w_router.astype(f32), HIGH)

    expert_rows, expert_hidden, d_rows = after((expert_rows, expert_hidden, d_rows), d_sent)
    d_experts = jnp.stack(
        [
            inner_rows(d_gate_expert, expert_rows).astype(LOW),
            inner_rows(d_up_expert, expert_rows).astype(LOW),
            inner_rows(expert_hidden, d_rows).astype(LOW),
        ]
    )
    d_experts = d_experts.reshape(3, groups, hidden // groups, width_model)

    def experts_block(k):
        return lax.dynamic_index_in_dim(d_experts, group_index ^ k, 1, False)

    expert_parts = [
        experts_block(0), swap_group(experts_block(1), 1), swap_group(experts_block(3), 3)
    ]
    d_returned = after(d_returned, expert_parts[1:])

    d_hmid = d_hmid + product(token_slots, d_returned)
    _, mid_back = jax.vjp(norm_apply, x_mid, gain_full[1])
    d_mid_part, d_gain_mid = mid_back(d_hmid)
    d_mid = d_last + d_mid_part
    d_att_in = d_mid.astype(LOW)
    d_attended = inner_cols(d_att_in, w_out).astype(LOW).reshape(rows_dev, heads_count, HD)
    d_value = jnp.einsum("hqk,qhd->khd", probs.astype(LOW), d_attended, preferred_element_type=f32)
    d_probs = jnp.einsum("qhd,khd->hqk", d_attended, value_low, preferred_element_type=f32)
    d_scores = (probs * (d_probs - jnp.sum(probs * d_probs, axis=-1, keepdims=True))).astype(LOW)
    scale_query = 1.0 / math.sqrt(HD)
    d_query = (
        jnp.einsum("hqk,khd->qhd", d_scores, key_rot, preferred_element_type=f32) * scale_query
    )
    d_key = jnp.einsum("hqk,qhd->khd", d_scores, query, preferred_element_type=f32) * scale_query
    d_qkv = jnp.concatenate(
        [
            rotate(d_query, cosine, -sine).reshape(rows_dev, width_model),
            rotate(d_key, cosine, -sine).reshape(rows_dev, width_model),
            d_value.reshape(rows_dev, width_model),
        ],
        axis=1,
    ).astype(LOW)
    _, first_back = jax.vjp(norm_apply, x_first, gain_full[0])
    d_first_part, d_gain_first = first_back(inner_cols(d_qkv, w_qkv))
    d_first = (d_mid + d_first_part).astype(LOW)

    d_first = d_first.reshape(rows_dev, groups, part_width).swapaxes(0, 1)
    d_qkv, d_att_in = after((d_qkv, d_att_in), d_first)
    d_first = lax.all_to_all(d_first, "dp", split_axis=0, concat_axis=0, tiled=True)
    d_first = after(d_first, early)
    d_tokens = lax.all_gather(
        d_first.reshape(groups * rows_dev, part_width), "expert", axis=0, tiled=True
    )
    token_words = (ids_all.swapaxes(0, 1) - vocab_start).reshape(1, -1)
    words = (token_words == jnp.arange(vocab_part, dtype=jnp.int32)[:, None]).astype(LOW)
    d_embed = product(words, d_tokens)

    gain_grad = split_three(jnp.stack([d_gain_first, d_gain_mid, d_gain_last]))
    router_parts = split_three(d_router_logits)
    units = jnp.eye(gains.shape[0], 128, dtype=LOW)
    late = []
    for stream, (left, right) in enumerate(
        (
            (attended, d_att_in),
            (h_first_low, d_qkv[:, 2 * width_model :]),
            (h_first_low, d_qkv[:, width_model : 2 * width_model]),
            (h_first_low, d_qkv[:, :width_model]),
        )
    ):
        distance = (owner % axis_width) ^ expert_index
        axes = [rank_in_order(distance >> 3, stream), rank_in_order((distance >> 1) & 3, stream)]
        first_axis, second_axis = axes if stream < 2 else axes[::-1]
        spot = ((distance & 1) * 16 + first_axis * 4 + second_axis) * groups + owner // axis_width
        choice = hot(spot * own_rows + row, width_model)
        if stream == 0:
            left = jnp.concatenate([left, h_low, h_low], axis=0)
            right = jnp.concatenate(
                [
                    spread_out(0, right, 128),
                    spread_out(width_model, router_parts[0], 128 - experts),
                    spread_out(width_model, router_parts[1], 128 - experts),
                ],
                axis=0,
            )
        if stream == 3:
            left = jnp.concatenate([left, *gain_grad], axis=0)
            right = jnp.concatenate(
                [jnp.pad(right, ((0, 0), (0, 128)))]
                + [jnp.pad(units, ((0, 0), (width_model, 0)))] * 3,
                axis=0,
            )
        left = product(left, choice).astype(LOW)
        half = width_model // 2
        sent = swap(inner_rows(left[:, half:], right).astype(LOW), 1)
        grad = (inner_rows(left[:, :half], right) + sent.astype(f32)).astype(LOW)
        late.append(grad.reshape(4, 4, groups * own_rows, -1))
    late = [grad.reshape((16,) + grad.shape[2:]) for grad in late]
    for step in range(4):
        if step == 1:
            far = after((head_block(2), experts_block(2)), late)
            far = [swap_group(part, 2) for part in far]
        if step == 3:
            late = after(late, far)
        half = late[0].shape[0] // 2
        late = [
            add_low(grad[:half], swap(grad[half:], steps_of(stream)[step]))
            for stream, grad in enumerate(late)
        ]
    late = [grad[0] for grad in late]
    d_head_part = sum(part.astype(f32) for part in head_parts + far[:1])
    experts_part = sum(part.astype(f32) for part in expert_parts + far[1:])
    late_width = sum(part.shape[1] for part in late)
    parts = lax.all_to_all(
        jnp.concatenate(late + [early], axis=1), "dp", split_axis=0, concat_axis=0, tiled=True
    )
    parts = after(parts, d_embed)
    parts = jnp.sum(parts.reshape(groups, own_rows, -1).astype(f32), axis=0)
    late, early = parts[:, :late_width], parts[:, late_width:]
    behind = width_model + 128
    dense_part = jnp.concatenate(
        [
            late[:, 2 * width_model + behind : 3 * width_model + behind],
            late[:, width_model + behind : 2 * width_model + behind],
            late[:, behind : width_model + behind],
            late[:, :width_model],
            early[:, : 2 * hidden_shared],
            late[:, width_model : width_model + experts],
        ],
        axis=1,
    )
    start = 2 * hidden_shared
    shared_part = jnp.concatenate(
        [
            early[:, start : start + width_model],
            early[: own_down - own_rows, start + width_model :],
        ],
        axis=0,
    )
    start = 3 * width_model + behind
    gains_part = late[:, start : start + gains.shape[0]].T
    up_part = experts_part[:2]
    down_part = experts_part[2:]

    grads = (dense_part, shared_part, gains_part, d_embed, d_head_part, up_part, down_part)
    squares = sum(jnp.sum(grad_part * grad_part) for grad_part in grads)
    counts = jnp.sum(chosen.astype(f32), axis=0)
    sums = jnp.concatenate([squares[None], own_loss[None], counts, jnp.zeros((126 - experts,), f32)])
    sums = lax.all_to_all(
        jnp.broadcast_to(sums[None], (devices, 128)), BOTH, split_axis=0, concat_axis=0, tiled=True
    )
    sums = jnp.sum(sums, axis=0)
    total_squares, loss_total, counts_all = sums[0], sums[1], sums[2 : 2 + experts]
    norm_value = jnp.sqrt(total_squares)
    clip_scale = jnp.minimum(1.0, CLIP_NORM / (norm_value + 1e-06))
    tables_part = jnp.stack([d_embed, d_head_part], axis=1)
    grads = (dense_part, shared_part, gains_part, tables_part, up_part, down_part)
    masters = (dense_rows, shared_down, gains, tables, expert_up, expert_down)
    firsts = (dense_m, shared_m, gains_m, tables_m, up_m, down_m)
    seconds = (dense_v, shared_v, gains_v, tables_v, up_v, down_v)

    def turn(index, value):
        if index == 3:
            return value.swapaxes(0, 1)
        return value[0].swapaxes(1, 2) if index == 4 else value

    def turn_back(index, value):
        if index == 3:
            return value.swapaxes(0, 1)
        return value.swapaxes(1, 2)[None] if index == 4 else value

    updated = []
    for index in range(6):
        state = [turn(index, value[index]) for value in (masters, firsts, seconds)]
        update = tables_update if index == 3 else adam_update
        new = update(state[0], grads[index], *state[1:], RATES[index], clip_scale)
        updated.append(tuple(turn_back(index, value) for value in new))
    mean_load = jnp.sum(counts_all) / experts
    bias_new = expert_bias + BIAS_RATE * jnp.sign(mean_load - counts_all)
    return (
        *(new[0] for new in updated),
        *(new[1] for new in updated),
        *(new[2] for new in updated),
        bias_new,
        norm_value,
        loss_total,
        weight_total,
    )


def solution(mesh):
    in_specs = (
        P("dp", None),
        P("dp", None),
        P(("dp", "expert"), None),
        P(),
        P(),
        P(("dp", "expert"), None),
        P(("dp", "expert"), None),
        P(("dp", "expert"), None),
        P(None, ("dp", "expert")),
        P(None, "expert", "dp"),
        P("expert", None, None, "dp"),
        P("expert", "dp", None),
        P(("dp", "expert"), None),
        P(("dp", "expert"), None),
        P(None, ("dp", "expert")),
        P(None, "expert", "dp"),
        P("expert", None, None, "dp"),
        P("expert", "dp", None),
        P(("dp", "expert"), None),
        P(("dp", "expert"), None),
        P(None, ("dp", "expert")),
        P(None, "expert", "dp"),
        P("expert", None, None, "dp"),
        P("expert", "dp", None),
        P(),
    )
    out_specs = (
        P(("dp", "expert"), None),
        P(("dp", "expert"), None),
        P(None, ("dp", "expert")),
        P(None, "expert", "dp"),
        P("expert", None, None, "dp"),
        P("expert", "dp", None),
        P(("dp", "expert"), None),
        P(("dp", "expert"), None),
        P(None, ("dp", "expert")),
        P(None, "expert", "dp"),
        P("expert", None, None, "dp"),
        P("expert", "dp", None),
        P(("dp", "expert"), None),
        P(("dp", "expert"), None),
        P(None, ("dp", "expert")),
        P(None, "expert", "dp"),
        P("expert", None, None, "dp"),
        P("expert", "dp", None),
        P(),
        P(),
        P(),
        P(),
    )
    return jax.shard_map(body, mesh=mesh, in_specs=in_specs, out_specs=out_specs, check_vma=False)
```

```python
import functools
import math

import jax
import jax.numpy as jnp
from jax import lax
from jax.experimental import pallas as pl
from jax.experimental.pallas import tpu as pltpu
from jax.sharding import PartitionSpec as P

HD = 128
TOP = 6
STEP = 10


NORM_EPS = 1e-06
HIGH = lax.Precision.HIGHEST
BETA_ONE = 0.9
BETA_TWO = 0.95
ADAM_EPS = 1e-08
DECAY = 0.1
CLIP_NORM = 0.02
BIAS_RATE = 0.05
ROPE_BASE = 10000.0
RATES = (0.03, 0.03, 0.5, 0.4, 0.03, 0.5)
MASKED = -1e30
LOW = jnp.bfloat16
BOTH = ("dp", "expert")
STREAMS = 4


def product(left, right):
    return jnp.dot(left, right, preferred_element_type=jnp.float32)


def inner_rows(left, right, precision=None):
    return lax.dot_general(
        left,
        right,
        (((0,), (0,)), ((), ())),
        precision=precision,
        preferred_element_type=jnp.float32,
    )


def inner_cols(left, right, precision=None):
    return lax.dot_general(
        left,
        right,
        (((1,), (1,)), ((), ())),
        precision=precision,
        preferred_element_type=jnp.float32,
    )


def split_three(values):
    high = values.astype(LOW)
    rest = values - high.astype(jnp.float32)
    middle = rest.astype(LOW)
    last = (rest - middle.astype(jnp.float32)).astype(LOW)
    return high, middle, last


def pick_exact(choice, values):
    return sum(product(choice, part) for part in split_three(values))


def norm_apply(values, gain_row):
    return (
        values * lax.rsqrt(jnp.mean(values * values, axis=-1, keepdims=True) + NORM_EPS) * gain_row
    )


def swiglu(gate_act, up_act):
    return jax.nn.silu(gate_act) * up_act


def rope_tables(length, head_size):
    positions = jnp.arange(length, dtype=jnp.float32)
    frequency = ROPE_BASE ** (-2.0 * jnp.arange(head_size // 2, dtype=jnp.float32) / head_size)
    angles = positions[:, None] * frequency[None, :]
    return (jnp.cos(angles)[:, None, :], jnp.sin(angles)[:, None, :])


def rotate(values, cosine, sine):
    half_size = values.shape[-1] // 2
    first_half = values[..., :half_size]
    second_half = values[..., half_size:]
    return jnp.concatenate(
        [first_half * cosine - second_half * sine, second_half * cosine + first_half * sine],
        axis=-1,
    )


def adam_update(weight, grad, first, second, rate, clip_scale):
    grad = grad * clip_scale
    first = BETA_ONE * first + (1.0 - BETA_ONE) * grad
    second = BETA_TWO * second + (1.0 - BETA_TWO) * grad * grad
    first_fix = first / (1.0 - BETA_ONE**STEP)
    second_fix = second / (1.0 - BETA_TWO**STEP)
    weight = weight - rate * (first_fix / (jnp.sqrt(second_fix) + ADAM_EPS) + DECAY * weight)
    return (weight, first, second)


def lane_squares(values):
    sums = jnp.sum(values * values, axis=tuple(range(values.ndim - 1)))
    return jnp.sum(jnp.pad(sums, (0, -sums.shape[0] % 128)).reshape(-1, 128), axis=0)


def tables_kernel(rate, clip, weight, grad, first, second, weight_out, first_out, second_out):
    new = adam_update(weight[...], grad[...], first[...], second[...], rate, clip[0, 0])
    weight_out[...], first_out[...], second_out[...] = new


def tables_update(weight, grad, first, second, rate, clip_scale):
    words, pair, width = weight.shape
    rows = max(count for count in range(1, 257) if words % count == 0)
    block = pl.BlockSpec((rows, pair, width), lambda i: (i, 0, 0))
    return pl.pallas_call(
        functools.partial(tables_kernel, rate),
        grid=(words // rows,),
        in_specs=[pl.BlockSpec(memory_space=pltpu.SMEM)] + [block] * 4,
        out_specs=[block] * 3,
        out_shape=[jax.ShapeDtypeStruct(weight.shape, jnp.float32)] * 3,
        compiler_params=pltpu.CompilerParams(vmem_limit_bytes=56 * 1024 * 1024),
        name="tables_update",
    )(clip_scale.reshape(1, 1), weight, grad, first, second)


def swap(value, number):
    return lax.ppermute(value, "expert", [(i, i ^ number) for i in range(32)])


def swap_group(value, number):
    return lax.ppermute(value, "dp", [(i, i ^ number) for i in range(4)])


def by_distance(values, index):
    shape = values.shape
    rest = shape[1:]
    for bit in range(shape[0].bit_length() - 1):
        halves = values.reshape((shape[0] >> (bit + 1), 2, 1 << bit) + rest)
        values = jnp.where(((index >> bit) & 1) == 1, halves[:, ::-1], halves)
    return values.reshape(shape)


def after(values, trigger):
    return lax.optimization_barrier((values, trigger))[0]


def add_low(left, right):
    return (left.astype(jnp.float32) + right.astype(jnp.float32)).astype(LOW)


def ring_sum(blocks, shift, other_way):
    near, far = (3, 1) if other_way else (1, 3)
    if other_way:
        sent = jnp.stack([blocks[3], blocks[2]])
        kept = blocks[0:2]
    else:
        sent = blocks[1:3]
        kept = jnp.stack([blocks[0], blocks[3]])
    kept = add_low(kept, swap(sent, near << shift))
    return add_low(kept[0], swap(kept[1], far << shift))


def ring_gather(block, shift, other_way):
    near, far = (3, 1) if other_way else (1, 3)
    pair = jnp.stack([block, swap(block, far << shift)])
    met = swap(pair, near << shift)
    if other_way:
        return jnp.stack([pair[0], pair[1], met[1], met[0]])
    return jnp.stack([pair[0], met[0], met[1], pair[1]])


ORDERS = ((0, 3, 1, 2), (0, 1, 3, 2))


def in_order(values, stream):
    if stream >= 2:
        values = jnp.swapaxes(values, 0, 1)
    values = jnp.stack([values[i] for i in ORDERS[stream % 2]])
    return jnp.stack([values[:, i] for i in ORDERS[stream // 2]], axis=1)


def rank_in_order(distance, way):
    return sum(jnp.where(distance == number, spot, 0) for spot, number in enumerate(ORDERS[way]))


def ring_steps(shift, way):
    return [number << shift for number in ((1, 3), (3, 1))[way]]


def halve(blocks, number):
    half = blocks.shape[0] // 2
    return add_low(blocks[:half], swap(blocks[half:], number))


def streams_sum(streams, between=lambda step, streams: streams, joined=True):
    streams = list(streams)
    for step in (0, 1):
        streams = between(step, streams)
        streams = [
            halve(blocks, ring_steps(3 if stream < 2 else 1, stream % 2)[step])
            for stream, blocks in enumerate(streams)
        ]
    if not joined:
        for step in (0, 1):
            streams = [
                halve(blocks, ring_steps(1 if stream < 2 else 3, stream // 2)[step])
                for stream, blocks in enumerate(streams)
            ]
        return [blocks[0] for blocks in streams]
    widths = [blocks.shape[-1] for blocks in streams]
    pairs = [jnp.concatenate(streams[pair : pair + 2], axis=-1) for pair in (0, 2)]
    for step in (0, 1):
        pairs = between(2 + step, pairs)
        pairs = [
            halve(blocks, ring_steps(1 if pair == 0 else 3, pair)[step])
            for pair, blocks in enumerate(pairs)
        ]
    return [
        part
        for pair, blocks in enumerate(pairs)
        for part in jnp.split(blocks[0], [widths[2 * pair]], axis=-1)
    ]


def planes_sum(streams):
    sums = []
    for pair, shifts in enumerate(((3, 1), (1, 3))):
        firsts = []
        for way in (0, 1):
            blocks = streams[2 * pair + way]
            blocks = blocks if pair == 0 else jnp.swapaxes(blocks, 0, 1)
            firsts.append(ring_sum(blocks, shifts[0], way == 1))
        sums.append(ring_sum(jnp.concatenate(firsts, axis=1), shifts[1], pair == 1))
    return jnp.concatenate(sums, axis=0)


def planes_gather(block):
    rows, width = block.shape
    halves = block.reshape(2, rows // 2, width)
    streams = []
    for pair, shifts in enumerate(((1, 3), (3, 1))):
        joined = ring_gather(halves[pair], shifts[0], pair == 1).reshape(4, 2, rows // 4, width)
        for way in (0, 1):
            met = ring_gather(joined[:, way], shifts[1], way == 1)
            streams.append(met if pair == 0 else jnp.swapaxes(met, 0, 1))
    return jnp.stack(streams, axis=2)


def expert_sum(blocks):
    _, rows, width = blocks.shape
    blocks = blocks.reshape(2, 4, 4, STREAMS, rows // STREAMS, width)
    mine = add_low(blocks[0], swap(blocks[1], 1))
    return planes_sum([mine[:, :, s] for s in range(STREAMS)])


def expert_gather(block):
    rows, width = block.shape
    mine = planes_gather(block).reshape(16, rows, width)
    return jnp.concatenate([mine, swap(mine, 1)], axis=0)


def core_first(values):
    return jnp.moveaxis(values.reshape((16, 2) + values.shape[1:]), 1, 0).reshape(values.shape)


def merge_kernel(numbers, rows, stats, *refs):
    others, merged = refs[:-1], refs[-1]
    top, total, target = stats[0:1, :], stats[1:2, :], stats[2:3, :]
    for number, other in zip(numbers, others, strict=True):
        values = other[...]
        kc, kx, ky = number & 1, number >> 3, (number >> 1) & 3
        pieces = []
        for block in range(32):
            source = ((block >> 4) ^ kc) * 16 + (((block >> 2) & 3) ^ kx) * 4 + ((block & 3) ^ ky)
            pieces.append(values[:, source * rows : (source + 1) * rows])
        values = jnp.concatenate(pieces, axis=1)
        other_top, other_total = values[0:1, :], values[1:2, :]
        new_top = jnp.maximum(top, other_top)
        total = total * jnp.exp(top - new_top) + other_total * jnp.exp(other_top - new_top)
        top, target = new_top, target + values[2:3, :]
    merged[...] = jnp.concatenate([top, total, target], axis=0)


def merge_stats(stats, others, numbers):
    return pl.pallas_call(
        functools.partial(merge_kernel, numbers, stats.shape[1] // 32),
        out_shape=jax.ShapeDtypeStruct(stats.shape, stats.dtype),
        name="merge_stats",
    )(stats, *others)


def meet_stats(stats, beside):
    for shift in (3, 1):
        numbers = [k << shift for k in (1, 2, 3)]
        others = [swap(stats, number) for number in numbers]
        if shift == 3:
            others = after(others, beside)
        stats = merge_stats(stats, others, numbers)
    return merge_stats(stats, [swap(stats, 1)], [1])


def hot(indices, count):
    return (indices[..., None] == jnp.arange(count, dtype=jnp.int32)).astype(LOW)


def attention_scores(query, key_rot, mask):
    scores = jnp.einsum("qhd,khd->hqk", query, key_rot, preferred_element_type=jnp.float32) * (
        1.0 / math.sqrt(HD)
    )
    return jnp.where(mask[None], scores, MASKED)


def body(
    ids,
    targets,
    documents,
    domains,
    loss_rows,
    routes,
    dense_rows,
    shared_down,
    gains,
    tables,
    expert_up,
    expert_down,
    dense_m,
    shared_m,
    gains_m,
    tables_m,
    up_m,
    down_m,
    dense_v,
    shared_v,
    gains_v,
    tables_v,
    up_v,
    down_v,
    expert_bias,
):
    f32 = jnp.float32
    groups = lax.axis_size("dp")
    axis_width = lax.axis_size("expert")
    expert_index = lax.axis_index("expert")
    group_index = lax.axis_index("dp")
    devices = groups * axis_width
    rows_dev = routes.shape[0]
    own_rows, dense_width = dense_rows.shape
    own_down, width_model = shared_down.shape
    hidden_shared = own_down * devices
    heads_count = width_model // HD
    experts = expert_bias.shape[0]
    slot_cap = min(rows_dev, rows_dev * TOP * 4 // (3 * experts))
    slots_all = experts * slot_cap
    vocab_part = tables.shape[1]
    part_width = tables.shape[2]
    vocab_start = expert_index * vocab_part
    hidden = expert_down.shape[1] * groups

    gap = -(dense_width + gains.shape[0]) % 128
    down_low = shared_down.astype(LOW)
    packed = jnp.concatenate(
        [
            dense_rows.astype(LOW),
            gains.astype(LOW).T,
            jnp.zeros((own_rows, gap), LOW),
            down_low[:own_rows],
            jnp.pad(down_low[own_rows:], ((0, 2 * own_rows - own_down), (0, 0))),
        ],
        axis=1,
    )
    packed_all = lax.all_gather(packed, BOTH, axis=0, tiled=True)
    start = dense_width + gains.shape[0] + gap
    router_start = 4 * width_model + 2 * hidden_shared
    w_qkv = packed_all[:, : 3 * width_model]
    w_out = packed_all[:, 3 * width_model : 4 * width_model]
    w_shared = packed_all[:, 4 * width_model : router_start]
    w_router = packed_all[:, router_start:dense_width]
    gain_full = packed_all[:, dense_width : dense_width + gains.shape[0]].T.astype(f32)
    down_first = packed_all[:, start : start + width_model]
    down_second = packed_all[:, start + width_model :]

    ids_all = by_distance(
        jnp.concatenate([ids] + [swap_group(ids, k) for k in range(1, groups)], axis=0), group_index
    ).reshape(groups, axis_width, rows_dev)
    ids_near = by_distance(ids_all.swapaxes(0, 1), expert_index) - vocab_start
    ids_near = ids_near.reshape(4, 4, 2, groups, rows_dev)
    ids_near = jnp.stack([in_order(ids_near[:, :, :, s], s) for s in range(groups)])
    table_words = tables[0].astype(LOW)
    looked_up = []
    for core in (1, 0):
        found = product(hot(ids_near[:, :, :, core].reshape(-1), vocab_part), table_words)
        looked_up.append(found.astype(LOW).reshape(groups, 16 * rows_dev, part_width))
    looked_up = add_low(looked_up[1], swap(looked_up[0], 1))
    summed = []

    def note(step, streams):
        if step == 1:
            summed.append(streams[0])
        return streams

    x_first = jnp.stack(
        streams_sum(
            (looked_up[s].reshape(16, rows_dev, part_width) for s in range(groups)),
            note,
            joined=False,
        )
    )
    routes, loss_rows, domains, targets, documents = after(
        (routes, loss_rows, domains, targets, documents), summed
    )
    x_first = lax.all_to_all(x_first, "dp", split_axis=0, concat_axis=0, tiled=True)
    x_first = x_first.swapaxes(0, 1).reshape(rows_dev, width_model).astype(f32)

    expert_part = jnp.concatenate(
        [expert_up[0].astype(LOW).swapaxes(1, 2), expert_down.astype(LOW)], axis=0
    )
    expert_all = lax.all_gather(expert_part, "dp", axis=1, tiled=True)
    w_gate, w_up, w_down = expert_all[0], expert_all[1], expert_all[2]

    positions = jnp.arange(rows_dev)
    experts_range = jnp.arange(experts, dtype=jnp.int32)
    chosen = jnp.any(routes[:, :, None] == experts_range[None, None, :], axis=1)
    earlier = product(
        (positions[:, None] > positions[None, :]).astype(LOW), chosen.astype(LOW)
    ).astype(jnp.int32)
    place = jnp.where(chosen, earlier, slot_cap)
    token_slots = hot(place, slot_cap).reshape(rows_dev, slots_all)
    slot_tokens = token_slots.T
    slot_experts = (
        jnp.arange(slots_all, dtype=jnp.int32)[:, None] // slot_cap == experts_range[None, :]
    )
    spread = slot_experts.T.astype(LOW)

    per_device = loss_rows.shape[1] // axis_width
    loss_places = loss_rows.reshape(groups, axis_width, per_device)
    at_place = loss_places[..., None] == jnp.arange(rows_dev, dtype=jnp.int32)
    counted_domains = jnp.sum(
        jnp.where(at_place, domains.reshape(groups, axis_width, 1, rows_dev), 0), axis=-1
    )
    all_weights = jnp.exp2(counted_domains.astype(f32) - 2.0)
    weight_total = jnp.sum(all_weights)
    group_weights = core_first(
        by_distance(lax.dynamic_index_in_dim(all_weights, group_index, 0, False), expert_index)
    )
    group_places = lax.dynamic_index_in_dim(loss_places, group_index, 0, False)
    group_targets = jnp.sum(
        jnp.where(
            group_places[..., None] == jnp.arange(rows_dev, dtype=jnp.int32),
            targets.reshape(axis_width, 1, rows_dev),
            0,
        ),
        axis=-1,
    )
    target_local = core_first(by_distance(group_targets, expert_index)).reshape(-1) - vocab_start
    own_choice = hot(by_distance(group_places, expert_index)[0], rows_dev)
    grad_weights = group_weights.reshape(-1) / weight_total

    docs_row = documents[0]
    mask = (positions[:, None] >= positions[None, :]) & (docs_row[:, None] == docs_row[None, :])
    cosine, sine = rope_tables(rows_dev, HD)
    h_first_low = norm_apply(x_first, gain_full[0]).astype(LOW)
    qkv_all = product(h_first_low, w_qkv)
    query = rotate(
        qkv_all[:, :width_model].reshape(rows_dev, heads_count, HD), cosine, sine
    ).astype(LOW)
    key_rot = rotate(
        qkv_all[:, width_model : 2 * width_model].reshape(rows_dev, heads_count, HD), cosine, sine
    ).astype(LOW)
    value_low = qkv_all[:, 2 * width_model :].reshape(rows_dev, heads_count, HD).astype(LOW)
    scores = attention_scores(query, key_rot, mask)
    top_score = jnp.max(scores, axis=-1, keepdims=True)
    expo = jnp.exp(scores - top_score)
    probs = expo / jnp.sum(expo, axis=-1, keepdims=True)
    attended = jnp.einsum(
        "hqk,khd->qhd", probs.astype(LOW), value_low, preferred_element_type=f32
    )
    attended = attended.reshape(rows_dev, width_model).astype(LOW)
    head = lax.all_gather(after(tables[1].astype(LOW), attended), "dp", axis=1, tiled=True)
    x_mid = x_first + product(attended, w_out)
    h_low = norm_apply(x_mid, gain_full[1]).astype(LOW)

    buffer = product(slot_tokens, h_low).astype(LOW)
    expert_rows = lax.all_to_all(buffer, "expert", split_axis=0, concat_axis=0, tiled=True)

    gate_scores = jnp.where(chosen, jax.nn.sigmoid(product(h_low, w_router)), 0.0)
    gate_total = jnp.sum(gate_scores, axis=1, keepdims=True)
    gates = gate_scores / gate_total
    gate_slots = jnp.concatenate(
        [token_slots * product(part, spread).astype(LOW) for part in split_three(gates)], axis=0
    )
    slot_gates = jnp.sum(
        jnp.where(slot_experts, pick_exact(slot_tokens, gates), 0.0), axis=1, keepdims=True
    )
    down_rows = after(jnp.arange(hidden_shared, dtype=jnp.int32), buffer)
    down_place = (down_rows // own_down) * own_rows + down_rows % own_down
    down_spot = jnp.where(
        down_rows % own_down < own_rows,
        down_place,
        down_place + (devices - 1) * own_rows,
    )
    down_choice = hot(down_spot, 2 * devices * own_rows)
    w_sdown = (
        product(down_choice[:, : devices * own_rows], down_first)
        + product(down_choice[:, devices * own_rows :], down_second)
    ).astype(LOW)
    shared_in = product(h_low, w_shared)
    shared_hidden = swiglu(shared_in[:, :hidden_shared], shared_in[:, hidden_shared:]).astype(LOW)
    shared_out = product(shared_hidden, w_sdown)

    features = jnp.arange(width_model, dtype=jnp.int32)
    owner, row = features // own_rows, features % own_rows
    turned = (owner % axis_width) * groups + owner // axis_width
    turn_choice = hot(turned * own_rows + row, width_model)
    downs, down_row = down_rows // own_down, down_rows % own_down
    down_turned = ((downs % axis_width) * groups + downs // axis_width) * own_rows
    down_firsts = hot(jnp.where(down_row < own_rows, down_turned + down_row, -1), width_model)
    down_seconds = hot(
        jnp.where(down_row < own_rows, -1, down_turned + down_row - own_rows), width_model
    )
    early_left = jnp.concatenate(
        [
            product(h_low, turn_choice).astype(LOW),
            product(shared_hidden, down_firsts).astype(LOW),
            product(shared_hidden, down_seconds).astype(LOW),
        ],
        axis=0,
    )
    late_left, late_choice = [], []
    for stream, left in enumerate((attended, h_first_low, h_first_low, h_first_low)):
        distance = (owner % axis_width) ^ expert_index
        axes = [distance >> 3, (distance >> 1) & 3]
        first_axis, second_axis = axes if stream < 2 else axes[::-1]
        first_axis = rank_in_order(first_axis, stream % 2)
        second_axis = rank_in_order(second_axis, stream // 2)
        spot = ((distance & 1) * 16 + first_axis * 4 + second_axis) * groups + owner // axis_width
        choice = hot(spot * own_rows + row, width_model)
        if stream == 0:
            left = jnp.concatenate([left, h_low, h_low], axis=0)
        late_left.append(product(left, choice).astype(LOW))
        late_choice.append(choice)

    gate_act = inner_cols(expert_rows, w_gate)
    up_act = inner_cols(expert_rows, w_up)
    expert_hidden = swiglu(gate_act, up_act).astype(LOW)
    expert_out = product(expert_hidden, w_down).astype(LOW)
    returned = lax.all_to_all(expert_out, "expert", split_axis=0, concat_axis=0, tiled=True)
    is_target = target_local[:, None] == jnp.arange(vocab_part, dtype=jnp.int32)[None, :]
    target_head = product(is_target.astype(LOW), head).astype(LOW)
    returned = after(returned, (target_head, early_left, late_left))
    routed = product(gate_slots, returned).reshape(3, rows_dev, width_model)
    x_last = x_mid + shared_out + (routed[0] + routed[1] + routed[2])

    chosen_rows = product(own_choice, norm_apply(x_last, gain_full[2]).astype(LOW)).astype(LOW)
    gathered = expert_gather(chosen_rows).reshape(axis_width * per_device, width_model)
    logits = inner_cols(gathered, head)
    row_top = jnp.max(logits, axis=1)
    expos = jnp.exp(logits - row_top[:, None])
    row_total = jnp.sum(expos, axis=1)
    row_target = jnp.sum(jnp.where(is_target, logits, 0.0), axis=1)
    rest_low = jnp.where(is_target, 0.0, expos).astype(LOW)
    d_rest = product(rest_low, head)
    stats = meet_stats(jnp.stack([row_top, row_total, row_target]), d_rest)
    log_norm = stats[0] + jnp.log(stats[1])
    entropy = log_norm[:per_device] - stats[2, :per_device]
    own_loss = jnp.sum(group_weights[0] * entropy)
    counts = jnp.sum(chosen.astype(f32), axis=0)
    terms = jnp.concatenate([own_loss[None], counts, jnp.zeros((127 - experts,), f32)])
    rest_scale = jnp.exp(row_top - log_norm) * grad_weights
    target_grad = (jnp.exp(stats[2] - log_norm) - 1.0) * grad_weights
    d_rows_all = d_rest * rest_scale[:, None] + target_grad[:, None] * target_head.astype(f32)
    d_rows_all = d_rows_all.astype(LOW)
    d_logits = jnp.where(
        is_target, target_grad[:, None], rest_low.astype(f32) * rest_scale[:, None]
    ).astype(LOW)
    d_chosen = expert_sum(d_rows_all.reshape(axis_width, per_device, width_model)).astype(f32)

    _, final_back = jax.vjp(norm_apply, x_last, gain_full[2])
    d_last, d_gain_last = final_back(pick_exact(own_choice.T, d_chosen))
    d_branch = d_last.astype(LOW)
    d_last_parts = split_three(d_last)

    d_buffer = (sum(product(slot_tokens, part) for part in d_last_parts) * slot_gates).astype(LOW)
    d_rows = lax.all_to_all(d_buffer, "expert", split_axis=0, concat_axis=0, tiled=True)

    _, shared_back = jax.vjp(swiglu, shared_in[:, :hidden_shared], shared_in[:, hidden_shared:])
    d_gate_shared, d_up_shared = shared_back(inner_cols(d_branch, w_sdown))
    d_shared_in = jnp.concatenate([d_gate_shared, d_up_shared], axis=1).astype(LOW)
    d_hmid = inner_cols(d_shared_in, w_shared)

    def spread_out(before, value, behind):
        return jnp.pad(value, ((0, 0), (before, behind)))

    right = jnp.concatenate(
        [
            spread_out(0, d_shared_in, 2 * width_model),
            spread_out(2 * hidden_shared, d_branch, width_model),
            spread_out(2 * hidden_shared + width_model, d_branch, 0),
        ],
        axis=0,
    )
    early = inner_rows(early_left, right).astype(LOW)
    d_logits, gathered = after((d_logits, gathered), d_buffer)
    d_head = inner_rows(d_logits, gathered).astype(LOW)

    def head_block(k):
        return lax.dynamic_slice_in_dim(
            d_head, (group_index ^ k) * part_width, part_width, axis=1
        )

    head_parts = [head_block(0), swap_group(head_block(1), 1), swap_group(head_block(3), 3)]
    d_rows = after(d_rows, (early, head_parts[1:]))
    early = lax.psum_scatter(early, "expert", scatter_dimension=0, tiled=True)

    d_expert_hidden = inner_cols(d_rows, w_down)
    _, expert_back = jax.vjp(swiglu, gate_act, up_act)
    d_gate_expert, d_up_expert = expert_back(d_expert_hidden)
    d_gate_expert = d_gate_expert.astype(LOW)
    d_up_expert = d_up_expert.astype(LOW)
    d_sent = (product(d_gate_expert, w_gate) + product(d_up_expert, w_up)).astype(LOW)
    d_returned = lax.all_to_all(d_sent, "expert", split_axis=0, concat_axis=0, tiled=True)
    d_last_late, returned = after((d_last_parts, returned), d_sent)
    d_slots = inner_cols(jnp.concatenate(d_last_late, axis=0), returned)
    d_slots = jnp.sum(d_slots.reshape(3, rows_dev, slots_all), axis=0) * token_slots.astype(f32)
    d_gates = sum(inner_cols(part, spread) for part in split_three(d_slots))
    d_scores = (d_gates - jnp.sum(gates * d_gates, axis=1, keepdims=True)) / gate_total
    d_router_logits = jnp.where(chosen, d_scores * gate_scores * (1.0 - gate_scores), 0.0)
    d_hmid = d_hmid + inner_cols(d_router_logits, w_router.astype(f32), HIGH)

    expert_rows, expert_hidden, d_rows = after((expert_rows, expert_hidden, d_rows), d_sent)
    d_experts = jnp.stack(
        [
            inner_rows(d_gate_expert, expert_rows).astype(LOW),
            inner_rows(d_up_expert, expert_rows).astype(LOW),
            inner_rows(expert_hidden, d_rows).astype(LOW),
        ]
    )
    d_experts = d_experts.reshape(3, groups, hidden // groups, width_model)

    def experts_block(k):
        return lax.dynamic_index_in_dim(d_experts, group_index ^ k, 1, False)

    expert_parts = [
        experts_block(0), swap_group(experts_block(1), 1), swap_group(experts_block(3), 3)
    ]

    d_hmid = d_hmid + product(token_slots, d_returned)
    _, mid_back = jax.vjp(norm_apply, x_mid, gain_full[1])
    d_mid_part, d_gain_mid = mid_back(d_hmid)
    d_mid = d_last + d_mid_part
    d_att_in = d_mid.astype(LOW)
    d_attended = inner_cols(d_att_in, w_out).astype(LOW).reshape(rows_dev, heads_count, HD)
    d_attended = after(d_attended, expert_parts[1:])
    d_value = jnp.einsum("hqk,qhd->khd", probs.astype(LOW), d_attended, preferred_element_type=f32)
    d_probs = jnp.einsum("qhd,khd->hqk", d_attended, value_low, preferred_element_type=f32)
    d_scores = (probs * (d_probs - jnp.sum(probs * d_probs, axis=-1, keepdims=True))).astype(LOW)
    scale_query = 1.0 / math.sqrt(HD)
    d_query = (
        jnp.einsum("hqk,khd->qhd", d_scores, key_rot, preferred_element_type=f32) * scale_query
    )
    d_key = jnp.einsum("hqk,qhd->khd", d_scores, query, preferred_element_type=f32) * scale_query
    d_qkv = jnp.concatenate(
        [
            rotate(d_query, cosine, -sine).reshape(rows_dev, width_model),
            rotate(d_key, cosine, -sine).reshape(rows_dev, width_model),
            d_value.reshape(rows_dev, width_model),
        ],
        axis=1,
    ).astype(LOW)
    _, first_back = jax.vjp(norm_apply, x_first, gain_full[0])
    d_first_part, d_gain_first = first_back(inner_cols(d_qkv, w_qkv))
    d_first = (d_mid + d_first_part).astype(LOW)

    d_first = d_first.reshape(rows_dev, groups, part_width).swapaxes(0, 1)
    d_qkv, d_att_in = after((d_qkv, d_att_in), d_first)
    d_first = lax.all_to_all(d_first, "dp", split_axis=0, concat_axis=0, tiled=True)
    d_tokens = lax.all_gather(
        d_first.reshape(groups * rows_dev, part_width), "expert", axis=0, tiled=True
    )
    token_words = (ids_all.swapaxes(0, 1) - vocab_start).reshape(1, -1)
    words = (token_words == jnp.arange(vocab_part, dtype=jnp.int32)[:, None]).astype(LOW)
    d_embed = product(words, d_tokens)

    gain_grad = split_three(jnp.stack([d_gain_first, d_gain_mid, d_gain_last]))
    router_parts = split_three(d_router_logits)
    units = jnp.eye(gains.shape[0], 128, dtype=LOW)
    late = []
    for stream, right in enumerate(
        (
            d_att_in,
            d_qkv[:, 2 * width_model :],
            d_qkv[:, width_model : 2 * width_model],
            d_qkv[:, :width_model],
        )
    ):
        left = late_left[stream]
        if stream == 0:
            right = jnp.concatenate(
                [
                    spread_out(0, right, 128),
                    spread_out(width_model, router_parts[0], 128 - experts),
                    spread_out(width_model, router_parts[1], 128 - experts),
                ],
                axis=0,
            )
        if stream == 3:
            gain_left = product(jnp.concatenate(gain_grad, axis=0), late_choice[3]).astype(LOW)
            left = jnp.concatenate([left, gain_left], axis=0)
            right = jnp.concatenate(
                [spread_out(0, right, 128)] + [spread_out(width_model, units, 0)] * 3, axis=0
            )
        half = width_model // 2
        sent = swap(inner_rows(left[:, half:], right).astype(LOW), 1)
        grad = (inner_rows(left[:, :half], right) + sent.astype(f32)).astype(LOW)
        late.append(grad.reshape(16, groups * own_rows, -1))
    far = []

    def between(step, streams):
        if step == 0:
            streams = after(streams, early)
        if step == 1:
            parts = after((head_block(2), experts_block(2)), streams)
            far.extend(swap_group(part, 2) for part in parts)
        return after(streams, (far, d_embed)) if step == 3 else streams

    late = streams_sum(late, between)
    d_head_part = sum(part.astype(f32) for part in head_parts + far[:1])
    experts_part = sum(part.astype(f32) for part in expert_parts + far[1:])
    late_width = sum(part.shape[1] for part in late)
    parts = lax.all_to_all(
        jnp.concatenate(late + [early], axis=1), "dp", split_axis=0, concat_axis=0, tiled=True
    )
    parts = jnp.sum(parts.reshape(groups, own_rows, -1).astype(f32), axis=0)
    late, early = parts[:, :late_width], parts[:, late_width:]
    behind = width_model + 128
    dense_part = jnp.concatenate(
        [
            late[:, 2 * width_model + behind : 3 * width_model + behind],
            late[:, width_model + behind : 2 * width_model + behind],
            late[:, behind : width_model + behind],
            late[:, :width_model],
            early[:, : 2 * hidden_shared],
            late[:, width_model : width_model + experts],
        ],
        axis=1,
    )
    start = 2 * hidden_shared
    shared_part = jnp.concatenate(
        [
            early[:, start : start + width_model],
            early[: own_down - own_rows, start + width_model :],
        ],
        axis=0,
    )
    start = 3 * width_model + behind
    gains_part = late[:, start : start + gains.shape[0]].T
    up_part = experts_part[:2]
    down_part = experts_part[2:]

    grads = (parts, d_embed, d_head_part, experts_part)
    squares = sum(lane_squares(grad) for grad in grads)
    sums = jnp.stack([squares, terms])
    d_embed, d_head_part, gains_part = after((d_embed, d_head_part, gains_part), sums)
    sums = lax.all_to_all(
        jnp.broadcast_to(sums[None], (devices, 2, 128)), BOTH, split_axis=0, concat_axis=0, tiled=True
    )
    sums = jnp.sum(sums, axis=0)
    total_squares = jnp.sum(sums[0])
    loss_total, counts_all = sums[1, 0], sums[1, 1 : 1 + experts]
    norm_value = jnp.sqrt(total_squares)
    clip_scale = jnp.minimum(1.0, CLIP_NORM / (norm_value + 1e-06))
    tables_part = jnp.stack([d_embed, d_head_part], axis=1)
    grads = (dense_part, shared_part, gains_part, tables_part, up_part, down_part)
    masters = (dense_rows, shared_down, gains, tables, expert_up, expert_down)
    firsts = (dense_m, shared_m, gains_m, tables_m, up_m, down_m)
    seconds = (dense_v, shared_v, gains_v, tables_v, up_v, down_v)

    def turn(index, value):
        if index == 3:
            return value.swapaxes(0, 1)
        return value[0].swapaxes(1, 2) if index == 4 else value

    def turn_back(index, value):
        if index == 3:
            return value.swapaxes(0, 1)
        return value.swapaxes(1, 2)[None] if index == 4 else value

    updated = []
    for index in range(6):
        state = [turn(index, value[index]) for value in (masters, firsts, seconds)]
        update = tables_update if index == 3 else adam_update
        new = update(state[0], grads[index], *state[1:], RATES[index], clip_scale)
        updated.append(tuple(turn_back(index, value) for value in new))
    mean_load = jnp.sum(counts_all) / experts
    bias_new = expert_bias + BIAS_RATE * jnp.sign(mean_load - counts_all)
    return (
        *(new[0] for new in updated),
        *(new[1] for new in updated),
        *(new[2] for new in updated),
        bias_new,
        norm_value,
        loss_total,
        weight_total,
    )


def solution(mesh):
    in_specs = (
        P("dp", None),
        P("dp", None),
        P(("dp", "expert"), None),
        P(),
        P(),
        P(("dp", "expert"), None),
        P(("dp", "expert"), None),
        P(("dp", "expert"), None),
        P(None, ("dp", "expert")),
        P(None, "expert", "dp"),
        P("expert", None, None, "dp"),
        P("expert", "dp", None),
        P(("dp", "expert"), None),
        P(("dp", "expert"), None),
        P(None, ("dp", "expert")),
        P(None, "expert", "dp"),
        P("expert", None, None, "dp"),
        P("expert", "dp", None),
        P(("dp", "expert"), None),
        P(("dp", "expert"), None),
        P(None, ("dp", "expert")),
        P(None, "expert", "dp"),
        P("expert", None, None, "dp"),
        P("expert", "dp", None),
        P(),
    )
    out_specs = (
        P(("dp", "expert"), None),
        P(("dp", "expert"), None),
        P(None, ("dp", "expert")),
        P(None, "expert", "dp"),
        P("expert", None, None, "dp"),
        P("expert", "dp", None),
        P(("dp", "expert"), None),
        P(("dp", "expert"), None),
        P(None, ("dp", "expert")),
        P(None, "expert", "dp"),
        P("expert", None, None, "dp"),
        P("expert", "dp", None),
        P(("dp", "expert"), None),
        P(("dp", "expert"), None),
        P(None, ("dp", "expert")),
        P(None, "expert", "dp"),
        P("expert", None, None, "dp"),
        P("expert", "dp", None),
        P(),
        P(),
        P(),
        P(),
    )
    return jax.shard_map(body, mesh=mesh, in_specs=in_specs, out_specs=out_specs, check_vma=False)
```

```python
import functools
import math

import jax
import jax.numpy as jnp
from jax import lax
from jax.experimental import pallas as pl
from jax.experimental.pallas import tpu as pltpu
from jax.sharding import PartitionSpec as P

HD = 128
TOP = 6
STEP = 10


NORM_EPS = 1e-06
HIGH = lax.Precision.HIGHEST
BETA_ONE = 0.9
BETA_TWO = 0.95
ADAM_EPS = 1e-08
DECAY = 0.1
CLIP_NORM = 0.02
BIAS_RATE = 0.05
ROPE_BASE = 10000.0
RATES = (0.03, 0.03, 0.5, 0.4, 0.03, 0.5)
MASKED = -1e30
LOW = jnp.bfloat16
BOTH = ("dp", "expert")
STREAMS = 4
ROUND_ROWS = 24


def product(left, right):
    return jnp.dot(left, right, preferred_element_type=jnp.float32)


def inner_rows(left, right, precision=None):
    return lax.dot_general(
        left,
        right,
        (((0,), (0,)), ((), ())),
        precision=precision,
        preferred_element_type=jnp.float32,
    )


def inner_cols(left, right, precision=None):
    return lax.dot_general(
        left,
        right,
        (((1,), (1,)), ((), ())),
        precision=precision,
        preferred_element_type=jnp.float32,
    )


def split_three(values):
    high = values.astype(LOW)
    rest = values - high.astype(jnp.float32)
    middle = rest.astype(LOW)
    last = (rest - middle.astype(jnp.float32)).astype(LOW)
    return high, middle, last


def pick_exact(choice, values):
    return sum(product(choice, part) for part in split_three(values))


def norm_apply(values, gain_row):
    return (
        values * lax.rsqrt(jnp.mean(values * values, axis=-1, keepdims=True) + NORM_EPS) * gain_row
    )


def swiglu(gate_act, up_act):
    return jax.nn.silu(gate_act) * up_act


def rope_tables(length, head_size):
    positions = jnp.arange(length, dtype=jnp.float32)
    frequency = ROPE_BASE ** (-2.0 * jnp.arange(head_size // 2, dtype=jnp.float32) / head_size)
    angles = positions[:, None] * frequency[None, :]
    return (jnp.cos(angles)[:, None, :], jnp.sin(angles)[:, None, :])


def rotate(values, cosine, sine):
    half_size = values.shape[-1] // 2
    first_half = values[..., :half_size]
    second_half = values[..., half_size:]
    return jnp.concatenate(
        [first_half * cosine - second_half * sine, second_half * cosine + first_half * sine],
        axis=-1,
    )


def adam_update(weight, grad, first, second, rate, clip_scale):
    grad = grad * clip_scale
    first = BETA_ONE * first + (1.0 - BETA_ONE) * grad
    second = BETA_TWO * second + (1.0 - BETA_TWO) * grad * grad
    first_fix = first / (1.0 - BETA_ONE**STEP)
    second_fix = second / (1.0 - BETA_TWO**STEP)
    weight = weight - rate * (first_fix / (jnp.sqrt(second_fix) + ADAM_EPS) + DECAY * weight)
    return (weight, first, second)


def lane_squares(values):
    sums = jnp.sum(values * values, axis=tuple(range(values.ndim - 1)))
    return jnp.sum(jnp.pad(sums, (0, -sums.shape[0] % 128)).reshape(-1, 128), axis=0)


def tables_kernel(rate, clip, weight, grad, first, second, weight_out, first_out, second_out):
    new = adam_update(weight[...], grad[...], first[...], second[...], rate, clip[0, 0])
    weight_out[...], first_out[...], second_out[...] = new


def tables_update(weight, grad, first, second, rate, clip_scale):
    words, pair, width = weight.shape
    rows = max(count for count in range(1, 257) if words % count == 0)
    block = pl.BlockSpec((rows, pair, width), lambda i: (i, 0, 0))
    return pl.pallas_call(
        functools.partial(tables_kernel, rate),
        grid=(words // rows,),
        in_specs=[pl.BlockSpec(memory_space=pltpu.SMEM)] + [block] * 4,
        out_specs=[block] * 3,
        out_shape=[jax.ShapeDtypeStruct(weight.shape, jnp.float32)] * 3,
        compiler_params=pltpu.CompilerParams(vmem_limit_bytes=56 * 1024 * 1024),
        name="tables_update",
    )(clip_scale.reshape(1, 1), weight, grad, first, second)


def swap(value, number):
    return lax.ppermute(value, "expert", [(i, i ^ number) for i in range(32)])


def swap_group(value, number):
    return lax.ppermute(value, "dp", [(i, i ^ number) for i in range(4)])


def by_distance(values, index):
    shape = values.shape
    rest = shape[1:]
    for bit in range(shape[0].bit_length() - 1):
        halves = values.reshape((shape[0] >> (bit + 1), 2, 1 << bit) + rest)
        values = jnp.where(((index >> bit) & 1) == 1, halves[:, ::-1], halves)
    return values.reshape(shape)


def after(values, trigger):
    return lax.optimization_barrier((values, trigger))[0]


def add_low(left, right):
    return (left.astype(jnp.float32) + right.astype(jnp.float32)).astype(LOW)


def ring_sum(blocks, shift, other_way):
    near, far = (3, 1) if other_way else (1, 3)
    if other_way:
        sent = jnp.stack([blocks[3], blocks[2]])
        kept = blocks[0:2]
    else:
        sent = blocks[1:3]
        kept = jnp.stack([blocks[0], blocks[3]])
    kept = add_low(kept, swap(sent, near << shift))
    return add_low(kept[0], swap(kept[1], far << shift))


def ring_gather(block, shift, other_way):
    near, far = (3, 1) if other_way else (1, 3)
    pair = jnp.stack([block, swap(block, far << shift)])
    met = swap(pair, near << shift)
    if other_way:
        return jnp.stack([pair[0], pair[1], met[1], met[0]])
    return jnp.stack([pair[0], met[0], met[1], pair[1]])


ORDERS = ((0, 3, 1, 2), (0, 1, 3, 2))


def in_order(values, stream):
    if stream >= 2:
        values = jnp.swapaxes(values, 0, 1)
    values = jnp.stack([values[i] for i in ORDERS[stream % 2]])
    return jnp.stack([values[:, i] for i in ORDERS[stream // 2]], axis=1)


def rank_in_order(distance, way):
    return sum(jnp.where(distance == number, spot, 0) for spot, number in enumerate(ORDERS[way]))


def ring_steps(shift, way):
    return [number << shift for number in ((1, 3), (3, 1))[way]]


def halve(blocks, number):
    half = blocks.shape[0] // 2
    return add_low(blocks[:half], swap(blocks[half:], number))


def streams_sum(streams, between=lambda step, streams: streams, joined=True):
    streams = list(streams)
    for step in (0, 1):
        streams = between(step, streams)
        streams = [
            halve(blocks, ring_steps(3 if stream < 2 else 1, stream % 2)[step])
            for stream, blocks in enumerate(streams)
        ]
    if not joined:
        for step in (0, 1):
            streams = [
                halve(blocks, ring_steps(1 if stream < 2 else 3, stream // 2)[step])
                for stream, blocks in enumerate(streams)
            ]
        return [blocks[0] for blocks in streams]
    widths = [blocks.shape[-1] for blocks in streams]
    pairs = [jnp.concatenate(streams[pair : pair + 2], axis=-1) for pair in (0, 2)]
    for step in (0, 1):
        pairs = between(2 + step, pairs)
        pairs = [
            halve(blocks, ring_steps(1 if pair == 0 else 3, pair)[step])
            for pair, blocks in enumerate(pairs)
        ]
    return [
        part
        for pair, blocks in enumerate(pairs)
        for part in jnp.split(blocks[0], [widths[2 * pair]], axis=-1)
    ]


def planes_sum(streams):
    sums = []
    for pair, shifts in enumerate(((3, 1), (1, 3))):
        firsts = []
        for way in (0, 1):
            blocks = streams[2 * pair + way]
            blocks = blocks if pair == 0 else jnp.swapaxes(blocks, 0, 1)
            firsts.append(ring_sum(blocks, shifts[0], way == 1))
        sums.append(ring_sum(jnp.concatenate(firsts, axis=1), shifts[1], pair == 1))
    return jnp.concatenate(sums, axis=0)


def planes_gather(block):
    rows, width = block.shape
    halves = block.reshape(2, rows // 2, width)
    streams = []
    for pair, shifts in enumerate(((1, 3), (3, 1))):
        joined = ring_gather(halves[pair], shifts[0], pair == 1).reshape(4, 2, rows // 4, width)
        for way in (0, 1):
            met = ring_gather(joined[:, way], shifts[1], way == 1)
            streams.append(met if pair == 0 else jnp.swapaxes(met, 0, 1))
    return jnp.stack(streams, axis=2)


def expert_sum(blocks):
    _, rows, width = blocks.shape
    blocks = blocks.reshape(2, 4, 4, STREAMS, rows // STREAMS, width)
    mine = add_low(blocks[0], swap(blocks[1], 1))
    return planes_sum([mine[:, :, s] for s in range(STREAMS)])


def expert_gather(block):
    rows, width = block.shape
    mine = planes_gather(block).reshape(16, rows, width)
    return jnp.concatenate([mine, swap(mine, 1)], axis=0)


def core_first(values):
    return jnp.moveaxis(values.reshape((16, 2) + values.shape[1:]), 1, 0).reshape(values.shape)


def merge_kernel(numbers, rows, stats, *refs):
    others, merged = refs[:-1], refs[-1]
    top, total, target = stats[0:1, :], stats[1:2, :], stats[2:3, :]
    for number, other in zip(numbers, others, strict=True):
        values = other[...]
        kc, kx, ky = number & 1, number >> 3, (number >> 1) & 3
        pieces = []
        for block in range(32):
            source = ((block >> 4) ^ kc) * 16 + (((block >> 2) & 3) ^ kx) * 4 + ((block & 3) ^ ky)
            pieces.append(values[:, source * rows : (source + 1) * rows])
        values = jnp.concatenate(pieces, axis=1)
        other_top, other_total = values[0:1, :], values[1:2, :]
        new_top = jnp.maximum(top, other_top)
        total = total * jnp.exp(top - new_top) + other_total * jnp.exp(other_top - new_top)
        top, target = new_top, target + values[2:3, :]
    merged[...] = jnp.concatenate([top, total, target], axis=0)


def merge_stats(stats, others, numbers):
    return pl.pallas_call(
        functools.partial(merge_kernel, numbers, stats.shape[1] // 32),
        out_shape=jax.ShapeDtypeStruct(stats.shape, stats.dtype),
        name="merge_stats",
    )(stats, *others)


def meet_stats(stats, beside):
    for shift in (3, 1):
        numbers = [k << shift for k in (1, 2, 3)]
        others = [swap(stats, number) for number in numbers]
        if shift == 3:
            others = after(others, beside)
        stats = merge_stats(stats, others, numbers)
    return merge_stats(stats, [swap(stats, 1)], [1])


def hot(indices, count):
    return (indices[..., None] == jnp.arange(count, dtype=jnp.int32)).astype(LOW)


def attention_scores(query, key_rot, mask):
    scores = jnp.einsum("qhd,khd->hqk", query, key_rot, preferred_element_type=jnp.float32) * (
        1.0 / math.sqrt(HD)
    )
    return jnp.where(mask[None], scores, MASKED)


def body(
    ids,
    targets,
    documents,
    domains,
    loss_rows,
    routes,
    dense_rows,
    shared_down,
    gains,
    tables,
    expert_up,
    expert_down,
    dense_m,
    shared_m,
    gains_m,
    tables_m,
    up_m,
    down_m,
    dense_v,
    shared_v,
    gains_v,
    tables_v,
    up_v,
    down_v,
    expert_bias,
):
    f32 = jnp.float32
    groups = lax.axis_size("dp")
    axis_width = lax.axis_size("expert")
    expert_index = lax.axis_index("expert")
    group_index = lax.axis_index("dp")
    devices = groups * axis_width
    rows_dev = routes.shape[0]
    own_rows, dense_width = dense_rows.shape
    own_down, width_model = shared_down.shape
    hidden_shared = own_down * devices
    heads_count = width_model // HD
    experts = expert_bias.shape[0]
    slot_cap = min(rows_dev, rows_dev * TOP * 4 // (3 * experts))
    slots_all = experts * slot_cap
    vocab_part = tables.shape[1]
    part_width = tables.shape[2]
    vocab_start = expert_index * vocab_part
    hidden = expert_down.shape[1] * groups

    gap = -(dense_width + gains.shape[0]) % 128
    down_low = shared_down.astype(LOW)
    packed = jnp.concatenate(
        [
            dense_rows.astype(LOW),
            gains.astype(LOW).T,
            jnp.zeros((own_rows, gap), LOW),
            down_low[:own_rows],
            jnp.pad(down_low[own_rows:], ((0, 2 * own_rows - own_down), (0, 0))),
        ],
        axis=1,
    )
    packed_all = lax.all_gather(packed, BOTH, axis=0, tiled=True)
    start = dense_width + gains.shape[0] + gap
    router_start = 4 * width_model + 2 * hidden_shared
    w_qkv = packed_all[:, : 3 * width_model]
    w_out = packed_all[:, 3 * width_model : 4 * width_model]
    w_shared = packed_all[:, 4 * width_model : router_start]
    w_router = packed_all[:, router_start:dense_width]
    gain_full = packed_all[:, dense_width : dense_width + gains.shape[0]].T.astype(f32)
    down_first = packed_all[:, start : start + width_model]
    down_second = packed_all[:, start + width_model :]

    ids_all = by_distance(
        jnp.concatenate([ids] + [swap_group(ids, k) for k in range(1, groups)], axis=0), group_index
    ).reshape(groups, axis_width, rows_dev)
    table_words = tables[0].astype(LOW)
    token_shards = ids_all // vocab_part
    tokens_range = jnp.arange(rows_dev, dtype=jnp.int32)
    before = tokens_range[:, None] < tokens_range[None, :]
    held = token_shards == expert_index
    held_place = product(held.reshape(-1, rows_dev).astype(LOW), before.astype(LOW)).astype(jnp.int32)
    held_place = jnp.where(held, held_place.reshape(held.shape), -1).swapaxes(0, 1)
    held_words = (ids_all - vocab_start).swapaxes(0, 1)
    own_shards = lax.dynamic_index_in_dim(token_shards, expert_index, 1, False)
    same = own_shards[:, :, None] == own_shards[:, None, :]
    own_place = jnp.sum(jnp.where(same & before[None], 1, 0), axis=1)
    places = jnp.arange(ROUND_ROWS, dtype=jnp.int32)
    round_width = axis_width * ROUND_ROWS

    def words_of(start):
        wanted = jnp.where(
            held_place[:, :, None, :] == (start + places)[:, None], held_words[:, :, None, :] + 1, 0
        )
        return jnp.sum(wanted, axis=-1).reshape(-1) - 1

    def spots_of(start):
        spot = own_place - start
        return hot(
            jnp.where((spot >= 0) & (spot < ROUND_ROWS), own_shards * ROUND_ROWS + spot, -1),
            round_width,
        )

    def fetch_round(start):
        sent = product(hot(words_of(start), vocab_part), table_words).astype(LOW)
        got = lax.all_to_all(
            sent.reshape(axis_width, groups * ROUND_ROWS, part_width),
            "expert",
            split_axis=0,
            concat_axis=0,
            tiled=True,
        )
        got = got.reshape(axis_width, groups, ROUND_ROWS, part_width).swapaxes(0, 1)
        return jnp.einsum(
            "gtr,grd->gtd",
            spots_of(start),
            got.reshape(groups, round_width, part_width),
            preferred_element_type=f32,
        ), sent

    def further_rounds(turn, first):
        return lax.while_loop(
            lambda carry: carry[0] < most,
            lambda carry: (carry[0] + ROUND_ROWS, carry[1] + turn(carry[0])),
            (jnp.full((), ROUND_ROWS, jnp.int32), first),
        )[1]

    x_first, sent_first = fetch_round(0)
    routes, loss_rows, domains, targets, documents, token_shards = after(
        (routes, loss_rows, domains, targets, documents, token_shards), sent_first
    )
    shards = jnp.arange(axis_width, dtype=jnp.int32)
    most = jnp.max(jnp.sum((token_shards[..., None] == shards).astype(jnp.int32), axis=2))
    x_first = further_rounds(lambda start: fetch_round(start)[0], x_first).astype(LOW)
    x_first = lax.all_to_all(x_first, "dp", split_axis=0, concat_axis=0, tiled=True)
    x_first = x_first.swapaxes(0, 1).reshape(rows_dev, width_model).astype(f32)

    expert_part = jnp.concatenate(
        [expert_up[0].astype(LOW).swapaxes(1, 2), expert_down.astype(LOW)], axis=0
    )
    expert_all = lax.all_gather(expert_part, "dp", axis=1, tiled=True)
    w_gate, w_up, w_down = expert_all[0], expert_all[1], expert_all[2]

    positions = jnp.arange(rows_dev)
    experts_range = jnp.arange(experts, dtype=jnp.int32)
    chosen = jnp.any(routes[:, :, None] == experts_range[None, None, :], axis=1)
    earlier = product(
        (positions[:, None] > positions[None, :]).astype(LOW), chosen.astype(LOW)
    ).astype(jnp.int32)
    place = jnp.where(chosen, earlier, slot_cap)
    token_slots = hot(place, slot_cap).reshape(rows_dev, slots_all)
    slot_tokens = token_slots.T
    slot_experts = (
        jnp.arange(slots_all, dtype=jnp.int32)[:, None] // slot_cap == experts_range[None, :]
    )
    spread = slot_experts.T.astype(LOW)

    per_device = loss_rows.shape[1] // axis_width
    loss_places = loss_rows.reshape(groups, axis_width, per_device)
    at_place = loss_places[..., None] == jnp.arange(rows_dev, dtype=jnp.int32)
    counted_domains = jnp.sum(
        jnp.where(at_place, domains.reshape(groups, axis_width, 1, rows_dev), 0), axis=-1
    )
    all_weights = jnp.exp2(counted_domains.astype(f32) - 2.0)
    weight_total = jnp.sum(all_weights)
    group_weights = core_first(
        by_distance(lax.dynamic_index_in_dim(all_weights, group_index, 0, False), expert_index)
    )
    group_places = lax.dynamic_index_in_dim(loss_places, group_index, 0, False)
    group_targets = jnp.sum(
        jnp.where(
            group_places[..., None] == jnp.arange(rows_dev, dtype=jnp.int32),
            targets.reshape(axis_width, 1, rows_dev),
            0,
        ),
        axis=-1,
    )
    target_local = core_first(by_distance(group_targets, expert_index)).reshape(-1) - vocab_start
    own_choice = hot(by_distance(group_places, expert_index)[0], rows_dev)
    grad_weights = group_weights.reshape(-1) / weight_total

    docs_row = documents[0]
    mask = (positions[:, None] >= positions[None, :]) & (docs_row[:, None] == docs_row[None, :])
    cosine, sine = rope_tables(rows_dev, HD)
    h_first_low = norm_apply(x_first, gain_full[0]).astype(LOW)
    qkv_all = product(h_first_low, w_qkv)
    query = rotate(
        qkv_all[:, :width_model].reshape(rows_dev, heads_count, HD), cosine, sine
    ).astype(LOW)
    key_rot = rotate(
        qkv_all[:, width_model : 2 * width_model].reshape(rows_dev, heads_count, HD), cosine, sine
    ).astype(LOW)
    value_low = qkv_all[:, 2 * width_model :].reshape(rows_dev, heads_count, HD).astype(LOW)
    scores = attention_scores(query, key_rot, mask)
    top_score = jnp.max(scores, axis=-1, keepdims=True)
    expo = jnp.exp(scores - top_score)
    probs = expo / jnp.sum(expo, axis=-1, keepdims=True)
    attended = jnp.einsum(
        "hqk,khd->qhd", probs.astype(LOW), value_low, preferred_element_type=f32
    )
    attended = attended.reshape(rows_dev, width_model).astype(LOW)
    head = lax.all_gather(after(tables[1].astype(LOW), attended), "dp", axis=1, tiled=True)
    x_mid = x_first + product(attended, w_out)
    h_low = norm_apply(x_mid, gain_full[1]).astype(LOW)

    buffer = product(slot_tokens, h_low).astype(LOW)
    expert_rows = lax.all_to_all(buffer, "expert", split_axis=0, concat_axis=0, tiled=True)

    gate_scores = jnp.where(chosen, jax.nn.sigmoid(product(h_low, w_router)), 0.0)
    gate_total = jnp.sum(gate_scores, axis=1, keepdims=True)
    gates = gate_scores / gate_total
    gate_slots = jnp.concatenate(
        [token_slots * product(part, spread).astype(LOW) for part in split_three(gates)], axis=0
    )
    slot_gates = jnp.sum(
        jnp.where(slot_experts, pick_exact(slot_tokens, gates), 0.0), axis=1, keepdims=True
    )
    down_rows = after(jnp.arange(hidden_shared, dtype=jnp.int32), buffer)
    down_place = (down_rows // own_down) * own_rows + down_rows % own_down
    down_spot = jnp.where(
        down_rows % own_down < own_rows,
        down_place,
        down_place + (devices - 1) * own_rows,
    )
    down_choice = hot(down_spot, 2 * devices * own_rows)
    w_sdown = (
        product(down_choice[:, : devices * own_rows], down_first)
        + product(down_choice[:, devices * own_rows :], down_second)
    ).astype(LOW)
    shared_in = product(h_low, w_shared)
    shared_hidden = swiglu(shared_in[:, :hidden_shared], shared_in[:, hidden_shared:]).astype(LOW)
    shared_out = product(shared_hidden, w_sdown)

    features = jnp.arange(width_model, dtype=jnp.int32)
    owner, row = features // own_rows, features % own_rows
    turned = (owner % axis_width) * groups + owner // axis_width
    turn_choice = hot(turned * own_rows + row, width_model)
    downs, down_row = down_rows // own_down, down_rows % own_down
    down_turned = ((downs % axis_width) * groups + downs // axis_width) * own_rows
    down_firsts = hot(jnp.where(down_row < own_rows, down_turned + down_row, -1), width_model)
    down_seconds = hot(
        jnp.where(down_row < own_rows, -1, down_turned + down_row - own_rows), width_model
    )
    lefts = after((h_low, shared_hidden, attended, h_first_low), expert_rows)
    early_left = jnp.concatenate(
        [
            product(lefts[0], turn_choice).astype(LOW),
            product(lefts[1], down_firsts).astype(LOW),
            product(lefts[1], down_seconds).astype(LOW),
        ],
        axis=0,
    )
    late_left, late_choice = [], []
    for stream, left in enumerate((lefts[2], lefts[3], lefts[3], lefts[3])):
        distance = (owner % axis_width) ^ expert_index
        axes = [distance >> 3, (distance >> 1) & 3]
        first_axis, second_axis = axes if stream < 2 else axes[::-1]
        first_axis = rank_in_order(first_axis, stream % 2)
        second_axis = rank_in_order(second_axis, stream // 2)
        spot = ((distance & 1) * 16 + first_axis * 4 + second_axis) * groups + owner // axis_width
        choice = hot(spot * own_rows + row, width_model)
        if stream == 0:
            left = jnp.concatenate([left, lefts[0], lefts[0]], axis=0)
        late_left.append(product(left, choice).astype(LOW))
        late_choice.append(choice)

    gate_act = inner_cols(expert_rows, w_gate)
    up_act = inner_cols(expert_rows, w_up)
    expert_hidden = swiglu(gate_act, up_act).astype(LOW)
    expert_out = product(expert_hidden, w_down).astype(LOW)
    returned = lax.all_to_all(expert_out, "expert", split_axis=0, concat_axis=0, tiled=True)
    is_target = target_local[:, None] == jnp.arange(vocab_part, dtype=jnp.int32)[None, :]
    target_head = product(is_target.astype(LOW), head).astype(LOW)
    returned = after(returned, (target_head, early_left, late_left))
    routed = product(gate_slots, returned).reshape(3, rows_dev, width_model)
    x_last = x_mid + shared_out + (routed[0] + routed[1] + routed[2])

    chosen_rows = product(own_choice, norm_apply(x_last, gain_full[2]).astype(LOW)).astype(LOW)
    gathered = expert_gather(chosen_rows).reshape(axis_width * per_device, width_model)
    logits = inner_cols(gathered, head)
    row_top = jnp.max(logits, axis=1)
    expos = jnp.exp(logits - row_top[:, None])
    row_total = jnp.sum(expos, axis=1)
    row_target = jnp.sum(jnp.where(is_target, logits, 0.0), axis=1)
    rest_low = jnp.where(is_target, 0.0, expos).astype(LOW)
    d_rest = product(rest_low, head)
    stats = meet_stats(jnp.stack([row_top, row_total, row_target]), d_rest)
    log_norm = stats[0] + jnp.log(stats[1])
    entropy = log_norm[:per_device] - stats[2, :per_device]
    own_loss = jnp.sum(group_weights[0] * entropy)
    counts = jnp.sum(chosen.astype(f32), axis=0)
    terms = jnp.concatenate([own_loss[None], counts, jnp.zeros((127 - experts,), f32)])
    rest_scale = jnp.exp(row_top - log_norm) * grad_weights
    target_grad = (jnp.exp(stats[2] - log_norm) - 1.0) * grad_weights
    d_rows_all = d_rest * rest_scale[:, None] + target_grad[:, None] * target_head.astype(f32)
    d_rows_all = d_rows_all.astype(LOW)
    d_logits = jnp.where(
        is_target, target_grad[:, None], rest_low.astype(f32) * rest_scale[:, None]
    ).astype(LOW)
    d_chosen = expert_sum(d_rows_all.reshape(axis_width, per_device, width_model)).astype(f32)

    _, final_back = jax.vjp(norm_apply, x_last, gain_full[2])
    d_last, d_gain_last = final_back(pick_exact(own_choice.T, d_chosen))
    d_branch = d_last.astype(LOW)
    d_last_parts = split_three(d_last)

    d_buffer = (sum(product(slot_tokens, part) for part in d_last_parts) * slot_gates).astype(LOW)
    d_rows = lax.all_to_all(d_buffer, "expert", split_axis=0, concat_axis=0, tiled=True)

    _, shared_back = jax.vjp(swiglu, shared_in[:, :hidden_shared], shared_in[:, hidden_shared:])
    d_gate_shared, d_up_shared = shared_back(inner_cols(d_branch, w_sdown))
    d_shared_in = jnp.concatenate([d_gate_shared, d_up_shared], axis=1).astype(LOW)
    d_hmid = inner_cols(d_shared_in, w_shared)

    def spread_out(before, value, behind):
        return jnp.pad(value, ((0, 0), (before, behind)))

    right = jnp.concatenate(
        [
            spread_out(0, d_shared_in, 2 * width_model),
            spread_out(2 * hidden_shared, d_branch, width_model),
            spread_out(2 * hidden_shared + width_model, d_branch, 0),
        ],
        axis=0,
    )
    early = inner_rows(early_left, right).astype(LOW)
    d_logits, gathered = after((d_logits, gathered), d_buffer)
    d_head = inner_rows(d_logits, gathered).astype(LOW)

    def head_block(k):
        return lax.dynamic_slice_in_dim(
            d_head, (group_index ^ k) * part_width, part_width, axis=1
        )

    head_parts = [head_block(0), swap_group(head_block(1), 1), swap_group(head_block(3), 3)]
    d_rows = after(d_rows, (early, head_parts[1:]))
    early = lax.psum_scatter(early, "expert", scatter_dimension=0, tiled=True)

    d_expert_hidden = inner_cols(d_rows, w_down)
    _, expert_back = jax.vjp(swiglu, gate_act, up_act)
    d_gate_expert, d_up_expert = expert_back(d_expert_hidden)
    d_gate_expert = d_gate_expert.astype(LOW)
    d_up_expert = d_up_expert.astype(LOW)
    d_sent = (product(d_gate_expert, w_gate) + product(d_up_expert, w_up)).astype(LOW)
    d_returned = lax.all_to_all(d_sent, "expert", split_axis=0, concat_axis=0, tiled=True)
    d_last_late, returned = after((d_last_parts, returned), d_sent)
    d_slots = inner_cols(jnp.concatenate(d_last_late, axis=0), returned)
    d_slots = jnp.sum(d_slots.reshape(3, rows_dev, slots_all), axis=0) * token_slots.astype(f32)
    d_gates = sum(inner_cols(part, spread) for part in split_three(d_slots))
    d_scores = (d_gates - jnp.sum(gates * d_gates, axis=1, keepdims=True)) / gate_total
    d_router_logits = jnp.where(chosen, d_scores * gate_scores * (1.0 - gate_scores), 0.0)
    d_hmid = d_hmid + inner_cols(d_router_logits, w_router.astype(f32), HIGH)

    expert_rows, expert_hidden, d_rows = after((expert_rows, expert_hidden, d_rows), d_sent)
    d_experts = jnp.stack(
        [
            inner_rows(d_gate_expert, expert_rows).astype(LOW),
            inner_rows(d_up_expert, expert_rows).astype(LOW),
            inner_rows(expert_hidden, d_rows).astype(LOW),
        ]
    )
    d_experts = d_experts.reshape(3, groups, hidden // groups, width_model)

    def experts_block(k):
        return lax.dynamic_index_in_dim(d_experts, group_index ^ k, 1, False)

    expert_parts = [
        experts_block(0), swap_group(experts_block(1), 1), swap_group(experts_block(3), 3)
    ]

    d_hmid = d_hmid + product(token_slots, d_returned)
    _, mid_back = jax.vjp(norm_apply, x_mid, gain_full[1])
    d_mid_part, d_gain_mid = mid_back(d_hmid)
    d_mid = d_last + d_mid_part
    d_att_in = d_mid.astype(LOW)
    d_attended = inner_cols(d_att_in, w_out).astype(LOW).reshape(rows_dev, heads_count, HD)
    d_attended = after(d_attended, expert_parts[1:])
    d_value = jnp.einsum("hqk,qhd->khd", probs.astype(LOW), d_attended, preferred_element_type=f32)
    d_probs = jnp.einsum("qhd,khd->hqk", d_attended, value_low, preferred_element_type=f32)
    d_scores = (probs * (d_probs - jnp.sum(probs * d_probs, axis=-1, keepdims=True))).astype(LOW)
    scale_query = 1.0 / math.sqrt(HD)
    d_query = (
        jnp.einsum("hqk,khd->qhd", d_scores, key_rot, preferred_element_type=f32) * scale_query
    )
    d_key = jnp.einsum("hqk,qhd->khd", d_scores, query, preferred_element_type=f32) * scale_query
    d_qkv = jnp.concatenate(
        [
            rotate(d_query, cosine, -sine).reshape(rows_dev, width_model),
            rotate(d_key, cosine, -sine).reshape(rows_dev, width_model),
            d_value.reshape(rows_dev, width_model),
        ],
        axis=1,
    ).astype(LOW)
    _, first_back = jax.vjp(norm_apply, x_first, gain_full[0])
    d_first_part, d_gain_first = first_back(inner_cols(d_qkv, w_qkv))
    d_first = (d_mid + d_first_part).astype(LOW)

    d_first = d_first.reshape(rows_dev, groups, part_width).swapaxes(0, 1)
    d_qkv, d_att_in = after((d_qkv, d_att_in), d_first)
    d_first = lax.all_to_all(d_first, "dp", split_axis=0, concat_axis=0, tiled=True)
    d_tokens = lax.all_gather(
        d_first.reshape(groups * rows_dev, part_width), "expert", axis=0, tiled=True
    )
    token_words = (ids_all.swapaxes(0, 1) - vocab_start).reshape(1, -1)
    words = (token_words == jnp.arange(vocab_part, dtype=jnp.int32)[:, None]).astype(LOW)
    d_embed = product(words, d_tokens)

    gain_grad = split_three(jnp.stack([d_gain_first, d_gain_mid, d_gain_last]))
    router_parts = split_three(d_router_logits)
    units = jnp.eye(gains.shape[0], 128, dtype=LOW)
    late = []
    for stream, right in enumerate(
        (
            d_att_in,
            d_qkv[:, 2 * width_model :],
            d_qkv[:, width_model : 2 * width_model],
            d_qkv[:, :width_model],
        )
    ):
        left = late_left[stream]
        if stream == 0:
            right = jnp.concatenate(
                [
                    spread_out(0, right, 128),
                    spread_out(width_model, router_parts[0], 128 - experts),
                    spread_out(width_model, router_parts[1], 128 - experts),
                ],
                axis=0,
            )
        if stream == 3:
            gain_left = product(jnp.concatenate(gain_grad, axis=0), late_choice[3]).astype(LOW)
            left = jnp.concatenate([left, gain_left], axis=0)
            right = jnp.concatenate(
                [spread_out(0, right, 128)] + [spread_out(width_model, units, 0)] * 3, axis=0
            )
        half = width_model // 2
        sent = swap(inner_rows(left[:, half:], right).astype(LOW), 1)
        grad = (inner_rows(left[:, :half], right) + sent.astype(f32)).astype(LOW)
        late.append(grad.reshape(16, groups * own_rows, -1))
    far = []

    def between(step, streams):
        if step == 0:
            streams = after(streams, early)
        if step == 1:
            parts = after((head_block(2), experts_block(2)), streams)
            far.extend(swap_group(part, 2) for part in parts)
        return after(streams, (far, d_embed)) if step == 3 else streams

    late = streams_sum(late, between)
    d_head_part = sum(part.astype(f32) for part in head_parts + far[:1])
    experts_part = sum(part.astype(f32) for part in expert_parts + far[1:])
    late_width = sum(part.shape[1] for part in late)
    parts = lax.all_to_all(
        jnp.concatenate(late + [early], axis=1), "dp", split_axis=0, concat_axis=0, tiled=True
    )
    parts = jnp.sum(parts.reshape(groups, own_rows, -1).astype(f32), axis=0)
    late, early = parts[:, :late_width], parts[:, late_width:]
    behind = width_model + 128
    dense_part = jnp.concatenate(
        [
            late[:, 2 * width_model + behind : 3 * width_model + behind],
            late[:, width_model + behind : 2 * width_model + behind],
            late[:, behind : width_model + behind],
            late[:, :width_model],
            early[:, : 2 * hidden_shared],
            late[:, width_model : width_model + experts],
        ],
        axis=1,
    )
    start = 2 * hidden_shared
    shared_part = jnp.concatenate(
        [
            early[:, start : start + width_model],
            early[: own_down - own_rows, start + width_model :],
        ],
        axis=0,
    )
    start = 3 * width_model + behind
    gains_part = late[:, start : start + gains.shape[0]].T
    up_part = experts_part[:2]
    down_part = experts_part[2:]

    grads = (parts, d_embed, d_head_part, experts_part)
    squares = sum(lane_squares(grad) for grad in grads)
    sums = jnp.stack([squares, terms])
    d_embed, d_head_part, gains_part = after((d_embed, d_head_part, gains_part), sums)
    sums = lax.all_to_all(
        jnp.broadcast_to(sums[None], (devices, 2, 128)), BOTH, split_axis=0, concat_axis=0, tiled=True
    )
    sums = jnp.sum(sums, axis=0)
    total_squares = jnp.sum(sums[0])
    loss_total, counts_all = sums[1, 0], sums[1, 1 : 1 + experts]
    norm_value = jnp.sqrt(total_squares)
    clip_scale = jnp.minimum(1.0, CLIP_NORM / (norm_value + 1e-06))
    tables_part = jnp.stack([d_embed, d_head_part], axis=1)
    grads = (dense_part, shared_part, gains_part, tables_part, up_part, down_part)
    masters = (dense_rows, shared_down, gains, tables, expert_up, expert_down)
    firsts = (dense_m, shared_m, gains_m, tables_m, up_m, down_m)
    seconds = (dense_v, shared_v, gains_v, tables_v, up_v, down_v)

    def turn(index, value):
        if index == 3:
            return value.swapaxes(0, 1)
        return value[0].swapaxes(1, 2) if index == 4 else value

    def turn_back(index, value):
        if index == 3:
            return value.swapaxes(0, 1)
        return value.swapaxes(1, 2)[None] if index == 4 else value

    updated = []
    for index in range(6):
        state = [turn(index, value[index]) for value in (masters, firsts, seconds)]
        update = tables_update if index == 3 else adam_update
        new = update(state[0], grads[index], *state[1:], RATES[index], clip_scale)
        updated.append(tuple(turn_back(index, value) for value in new))
    mean_load = jnp.sum(counts_all) / experts
    bias_new = expert_bias + BIAS_RATE * jnp.sign(mean_load - counts_all)
    return (
        *(new[0] for new in updated),
        *(new[1] for new in updated),
        *(new[2] for new in updated),
        bias_new,
        norm_value,
        loss_total,
        weight_total,
    )


def solution(mesh):
    in_specs = (
        P("dp", None),
        P("dp", None),
        P(("dp", "expert"), None),
        P(),
        P(),
        P(("dp", "expert"), None),
        P(("dp", "expert"), None),
        P(("dp", "expert"), None),
        P(None, ("dp", "expert")),
        P(None, "expert", "dp"),
        P("expert", None, None, "dp"),
        P("expert", "dp", None),
        P(("dp", "expert"), None),
        P(("dp", "expert"), None),
        P(None, ("dp", "expert")),
        P(None, "expert", "dp"),
        P("expert", None, None, "dp"),
        P("expert", "dp", None),
        P(("dp", "expert"), None),
        P(("dp", "expert"), None),
        P(None, ("dp", "expert")),
        P(None, "expert", "dp"),
        P("expert", None, None, "dp"),
        P("expert", "dp", None),
        P(),
    )
    out_specs = (
        P(("dp", "expert"), None),
        P(("dp", "expert"), None),
        P(None, ("dp", "expert")),
        P(None, "expert", "dp"),
        P("expert", None, None, "dp"),
        P("expert", "dp", None),
        P(("dp", "expert"), None),
        P(("dp", "expert"), None),
        P(None, ("dp", "expert")),
        P(None, "expert", "dp"),
        P("expert", None, None, "dp"),
        P("expert", "dp", None),
        P(("dp", "expert"), None),
        P(("dp", "expert"), None),
        P(None, ("dp", "expert")),
        P(None, "expert", "dp"),
        P("expert", None, None, "dp"),
        P("expert", "dp", None),
        P(),
        P(),
        P(),
        P(),
    )
    return jax.shard_map(body, mesh=mesh, in_specs=in_specs, out_specs=out_specs, check_vma=False)
```

```python
import functools
import math

import jax
import jax.numpy as jnp
from jax import lax
from jax.experimental import pallas as pl
from jax.experimental.pallas import tpu as pltpu
from jax.sharding import PartitionSpec as P

HD = 128
TOP = 6
STEP = 10


NORM_EPS = 1e-06
HIGH = lax.Precision.HIGHEST
BETA_ONE = 0.9
BETA_TWO = 0.95
ADAM_EPS = 1e-08
DECAY = 0.1
CLIP_NORM = 0.02
BIAS_RATE = 0.05
ROPE_BASE = 10000.0
RATES = (0.03, 0.03, 0.5, 0.4, 0.03, 0.5)
MASKED = -1e30
LOW = jnp.bfloat16
BOTH = ("dp", "expert")
STREAMS = 4
ROUND_ROWS = 24


def product(left, right):
    return jnp.dot(left, right, preferred_element_type=jnp.float32)


def inner_rows(left, right, precision=None):
    return lax.dot_general(
        left,
        right,
        (((0,), (0,)), ((), ())),
        precision=precision,
        preferred_element_type=jnp.float32,
    )


def inner_cols(left, right, precision=None):
    return lax.dot_general(
        left,
        right,
        (((1,), (1,)), ((), ())),
        precision=precision,
        preferred_element_type=jnp.float32,
    )


def split_three(values):
    high = values.astype(LOW)
    rest = values - high.astype(jnp.float32)
    middle = rest.astype(LOW)
    last = (rest - middle.astype(jnp.float32)).astype(LOW)
    return high, middle, last


def pick_exact(choice, values):
    return sum(product(choice, part) for part in split_three(values))


def norm_apply(values, gain_row):
    return (
        values * lax.rsqrt(jnp.mean(values * values, axis=-1, keepdims=True) + NORM_EPS) * gain_row
    )


def swiglu(gate_act, up_act):
    return jax.nn.silu(gate_act) * up_act


def rope_tables(length, head_size):
    positions = jnp.arange(length, dtype=jnp.float32)
    frequency = ROPE_BASE ** (-2.0 * jnp.arange(head_size // 2, dtype=jnp.float32) / head_size)
    angles = positions[:, None] * frequency[None, :]
    return (jnp.cos(angles)[:, None, :], jnp.sin(angles)[:, None, :])


def rotate(values, cosine, sine):
    half_size = values.shape[-1] // 2
    first_half = values[..., :half_size]
    second_half = values[..., half_size:]
    return jnp.concatenate(
        [first_half * cosine - second_half * sine, second_half * cosine + first_half * sine],
        axis=-1,
    )


def adam_update(weight, grad, first, second, rate, clip_scale):
    grad = grad * clip_scale
    first = BETA_ONE * first + (1.0 - BETA_ONE) * grad
    second = BETA_TWO * second + (1.0 - BETA_TWO) * grad * grad
    first_fix = first / (1.0 - BETA_ONE**STEP)
    second_fix = second / (1.0 - BETA_TWO**STEP)
    weight = weight - rate * (first_fix / (jnp.sqrt(second_fix) + ADAM_EPS) + DECAY * weight)
    return (weight, first, second)


def lane_squares(values):
    sums = jnp.sum(values * values, axis=tuple(range(values.ndim - 1)))
    return jnp.sum(jnp.pad(sums, (0, -sums.shape[0] % 128)).reshape(-1, 128), axis=0)


def tables_kernel(rate, clip, weight, grad, first, second, weight_out, first_out, second_out):
    new = adam_update(weight[...], grad[...], first[...], second[...], rate, clip[0, 0])
    weight_out[...], first_out[...], second_out[...] = new


def tables_update(weight, grad, first, second, rate, clip_scale):
    words, pair, width = weight.shape
    rows = max(count for count in range(1, 257) if words % count == 0)
    block = pl.BlockSpec((rows, pair, width), lambda i: (i, 0, 0))
    return pl.pallas_call(
        functools.partial(tables_kernel, rate),
        grid=(words // rows,),
        in_specs=[pl.BlockSpec(memory_space=pltpu.SMEM)] + [block] * 4,
        out_specs=[block] * 3,
        out_shape=[jax.ShapeDtypeStruct(weight.shape, jnp.float32)] * 3,
        compiler_params=pltpu.CompilerParams(vmem_limit_bytes=56 * 1024 * 1024),
        name="tables_update",
    )(clip_scale.reshape(1, 1), weight, grad, first, second)


def swap(value, number):
    return lax.ppermute(value, "expert", [(i, i ^ number) for i in range(32)])


def swap_group(value, number):
    return lax.ppermute(value, "dp", [(i, i ^ number) for i in range(4)])


def by_distance(values, index):
    shape = values.shape
    rest = shape[1:]
    for bit in range(shape[0].bit_length() - 1):
        halves = values.reshape((shape[0] >> (bit + 1), 2, 1 << bit) + rest)
        values = jnp.where(((index >> bit) & 1) == 1, halves[:, ::-1], halves)
    return values.reshape(shape)


def after(values, trigger):
    return lax.optimization_barrier((values, trigger))[0]


def add_low(left, right):
    return (left.astype(jnp.float32) + right.astype(jnp.float32)).astype(LOW)


def ring_sum(blocks, shift, other_way):
    near, far = (3, 1) if other_way else (1, 3)
    if other_way:
        sent = jnp.stack([blocks[3], blocks[2]])
        kept = blocks[0:2]
    else:
        sent = blocks[1:3]
        kept = jnp.stack([blocks[0], blocks[3]])
    kept = add_low(kept, swap(sent, near << shift))
    return add_low(kept[0], swap(kept[1], far << shift))


def ring_gather(block, shift, other_way):
    near, far = (3, 1) if other_way else (1, 3)
    pair = jnp.stack([block, swap(block, far << shift)])
    met = swap(pair, near << shift)
    if other_way:
        return jnp.stack([pair[0], pair[1], met[1], met[0]])
    return jnp.stack([pair[0], met[0], met[1], pair[1]])


ORDERS = ((0, 3, 1, 2), (0, 1, 3, 2))


def in_order(values, stream):
    if stream >= 2:
        values = jnp.swapaxes(values, 0, 1)
    values = jnp.stack([values[i] for i in ORDERS[stream % 2]])
    return jnp.stack([values[:, i] for i in ORDERS[stream // 2]], axis=1)


def rank_in_order(distance, way):
    return sum(jnp.where(distance == number, spot, 0) for spot, number in enumerate(ORDERS[way]))


def ring_steps(shift, way):
    return [number << shift for number in ((1, 3), (3, 1))[way]]


def halve(blocks, number):
    half = blocks.shape[0] // 2
    return add_low(blocks[:half], swap(blocks[half:], number))


def streams_sum(streams, between=lambda step, streams: streams, joined=True):
    streams = list(streams)
    for step in (0, 1):
        streams = between(step, streams)
        streams = [
            halve(blocks, ring_steps(3 if stream < 2 else 1, stream % 2)[step])
            for stream, blocks in enumerate(streams)
        ]
    if not joined:
        for step in (0, 1):
            streams = [
                halve(blocks, ring_steps(1 if stream < 2 else 3, stream // 2)[step])
                for stream, blocks in enumerate(streams)
            ]
        return [blocks[0] for blocks in streams]
    widths = [blocks.shape[-1] for blocks in streams]
    pairs = [jnp.concatenate(streams[pair : pair + 2], axis=-1) for pair in (0, 2)]
    for step in (0, 1):
        pairs = between(2 + step, pairs)
        pairs = [
            halve(blocks, ring_steps(1 if pair == 0 else 3, pair)[step])
            for pair, blocks in enumerate(pairs)
        ]
    return [
        part
        for pair, blocks in enumerate(pairs)
        for part in jnp.split(blocks[0], [widths[2 * pair]], axis=-1)
    ]


def planes_sum(streams):
    sums = []
    for pair, shifts in enumerate(((3, 1), (1, 3))):
        firsts = []
        for way in (0, 1):
            blocks = streams[2 * pair + way]
            blocks = blocks if pair == 0 else jnp.swapaxes(blocks, 0, 1)
            firsts.append(ring_sum(blocks, shifts[0], way == 1))
        sums.append(ring_sum(jnp.concatenate(firsts, axis=1), shifts[1], pair == 1))
    return jnp.concatenate(sums, axis=0)


def planes_gather(block):
    rows, width = block.shape
    halves = block.reshape(2, rows // 2, width)
    streams = []
    for pair, shifts in enumerate(((1, 3), (3, 1))):
        joined = ring_gather(halves[pair], shifts[0], pair == 1).reshape(4, 2, rows // 4, width)
        for way in (0, 1):
            met = ring_gather(joined[:, way], shifts[1], way == 1)
            streams.append(met if pair == 0 else jnp.swapaxes(met, 0, 1))
    return jnp.stack(streams, axis=2)


def expert_sum(blocks):
    _, rows, width = blocks.shape
    blocks = blocks.reshape(2, 4, 4, STREAMS, rows // STREAMS, width)
    mine = add_low(blocks[0], swap(blocks[1], 1))
    return planes_sum([mine[:, :, s] for s in range(STREAMS)])


def expert_gather(block):
    rows, width = block.shape
    mine = planes_gather(block).reshape(16, rows, width)
    return jnp.concatenate([mine, swap(mine, 1)], axis=0)


def core_first(values):
    return jnp.moveaxis(values.reshape((16, 2) + values.shape[1:]), 1, 0).reshape(values.shape)


def merge_kernel(numbers, rows, stats, *refs):
    others, merged = refs[:-1], refs[-1]
    top, total, target = stats[0:1, :], stats[1:2, :], stats[2:3, :]
    for number, other in zip(numbers, others, strict=True):
        values = other[...]
        kc, kx, ky = number & 1, number >> 3, (number >> 1) & 3
        pieces = []
        for block in range(32):
            source = ((block >> 4) ^ kc) * 16 + (((block >> 2) & 3) ^ kx) * 4 + ((block & 3) ^ ky)
            pieces.append(values[:, source * rows : (source + 1) * rows])
        values = jnp.concatenate(pieces, axis=1)
        other_top, other_total = values[0:1, :], values[1:2, :]
        new_top = jnp.maximum(top, other_top)
        total = total * jnp.exp(top - new_top) + other_total * jnp.exp(other_top - new_top)
        top, target = new_top, target + values[2:3, :]
    merged[...] = jnp.concatenate([top, total, target], axis=0)


def merge_stats(stats, others, numbers):
    return pl.pallas_call(
        functools.partial(merge_kernel, numbers, stats.shape[1] // 32),
        out_shape=jax.ShapeDtypeStruct(stats.shape, stats.dtype),
        name="merge_stats",
    )(stats, *others)


def meet_stats(stats, beside):
    for shift in (3, 1):
        numbers = [k << shift for k in (1, 2, 3)]
        others = [swap(stats, number) for number in numbers]
        if shift == 3:
            others = after(others, beside)
        stats = merge_stats(stats, others, numbers)
    return merge_stats(stats, [swap(stats, 1)], [1])


def hot(indices, count):
    return (indices[..., None] == jnp.arange(count, dtype=jnp.int32)).astype(LOW)


def attention_scores(query, key_rot, mask):
    scores = jnp.einsum("qhd,khd->hqk", query, key_rot, preferred_element_type=jnp.float32) * (
        1.0 / math.sqrt(HD)
    )
    return jnp.where(mask[None], scores, MASKED)


def body(
    ids,
    targets,
    documents,
    domains,
    loss_rows,
    routes,
    dense_rows,
    shared_down,
    gains,
    tables,
    expert_up,
    expert_down,
    dense_m,
    shared_m,
    gains_m,
    tables_m,
    up_m,
    down_m,
    dense_v,
    shared_v,
    gains_v,
    tables_v,
    up_v,
    down_v,
    expert_bias,
):
    f32 = jnp.float32
    groups = lax.axis_size("dp")
    axis_width = lax.axis_size("expert")
    expert_index = lax.axis_index("expert")
    group_index = lax.axis_index("dp")
    devices = groups * axis_width
    rows_dev = routes.shape[0]
    own_rows, dense_width = dense_rows.shape
    own_down, width_model = shared_down.shape
    hidden_shared = own_down * devices
    heads_count = width_model // HD
    experts = expert_bias.shape[0]
    slot_cap = min(rows_dev, rows_dev * TOP * 4 // (3 * experts))
    slots_all = experts * slot_cap
    vocab_part = tables.shape[1]
    part_width = tables.shape[2]
    vocab_start = expert_index * vocab_part
    hidden = expert_down.shape[1] * groups

    gap = -(dense_width + gains.shape[0]) % 128
    down_low = shared_down.astype(LOW)
    packed = jnp.concatenate(
        [
            dense_rows.astype(LOW),
            gains.astype(LOW).T,
            jnp.zeros((own_rows, gap), LOW),
            down_low[:own_rows],
            jnp.pad(down_low[own_rows:], ((0, 2 * own_rows - own_down), (0, 0))),
        ],
        axis=1,
    )
    packed_all = lax.all_gather(packed, BOTH, axis=0, tiled=True)
    start = dense_width + gains.shape[0] + gap
    router_start = 4 * width_model + 2 * hidden_shared
    w_qkv = packed_all[:, : 3 * width_model]
    w_out = packed_all[:, 3 * width_model : 4 * width_model]
    w_shared = packed_all[:, 4 * width_model : router_start]
    w_router = packed_all[:, router_start:dense_width]
    gain_full = packed_all[:, dense_width : dense_width + gains.shape[0]].T.astype(f32)
    down_first = packed_all[:, start : start + width_model]
    down_second = packed_all[:, start + width_model :]

    ids_all = by_distance(
        jnp.concatenate([ids] + [swap_group(ids, k) for k in range(1, groups)], axis=0), group_index
    ).reshape(groups, axis_width, rows_dev)
    table_words = tables[0].astype(LOW)
    token_shards = ids_all // vocab_part
    tokens_range = jnp.arange(rows_dev, dtype=jnp.int32)
    before = tokens_range[:, None] < tokens_range[None, :]
    held = token_shards == expert_index
    held_place = product(held.reshape(-1, rows_dev).astype(LOW), before.astype(LOW)).astype(jnp.int32)
    held_place = jnp.where(held, held_place.reshape(held.shape), -1).swapaxes(0, 1)
    held_words = (ids_all - vocab_start).swapaxes(0, 1)
    own_shards = lax.dynamic_index_in_dim(token_shards, expert_index, 1, False)
    same = own_shards[:, :, None] == own_shards[:, None, :]
    own_place = jnp.sum(jnp.where(same & before[None], 1, 0), axis=1)
    places = jnp.arange(ROUND_ROWS, dtype=jnp.int32)
    round_width = axis_width * ROUND_ROWS

    def words_of(start):
        wanted = jnp.where(
            held_place[:, :, None, :] == (start + places)[:, None], held_words[:, :, None, :] + 1, 0
        )
        return jnp.sum(wanted, axis=-1).reshape(-1) - 1

    def spots_of(start):
        spot = own_place - start
        return hot(
            jnp.where((spot >= 0) & (spot < ROUND_ROWS), own_shards * ROUND_ROWS + spot, -1),
            round_width,
        )

    def fetch_round(start):
        sent = product(hot(words_of(start), vocab_part), table_words).astype(LOW)
        got = lax.all_to_all(
            sent.reshape(axis_width, groups * ROUND_ROWS, part_width),
            "expert",
            split_axis=0,
            concat_axis=0,
            tiled=True,
        )
        got = got.reshape(axis_width, groups, ROUND_ROWS, part_width).swapaxes(0, 1)
        return jnp.einsum(
            "gtr,grd->gtd",
            spots_of(start),
            got.reshape(groups, round_width, part_width),
            preferred_element_type=f32,
        ), sent

    def further_rounds(turn, first):
        return lax.while_loop(
            lambda carry: carry[0] < most,
            lambda carry: (carry[0] + ROUND_ROWS, carry[1] + turn(carry[0])),
            (jnp.full((), ROUND_ROWS, jnp.int32), first),
        )[1]

    x_first, sent_first = fetch_round(0)
    routes, loss_rows, domains, targets, documents, token_shards = after(
        (routes, loss_rows, domains, targets, documents, token_shards), sent_first
    )
    shards = jnp.arange(axis_width, dtype=jnp.int32)
    most = jnp.max(jnp.sum((token_shards[..., None] == shards).astype(jnp.int32), axis=2))
    x_first = further_rounds(lambda start: fetch_round(start)[0], x_first).astype(LOW)
    x_first = lax.all_to_all(x_first, "dp", split_axis=0, concat_axis=0, tiled=True)
    x_first = x_first.swapaxes(0, 1).reshape(rows_dev, width_model).astype(f32)

    expert_part = jnp.concatenate(
        [expert_up[0].astype(LOW).swapaxes(1, 2), expert_down.astype(LOW)], axis=0
    )
    expert_all = lax.all_gather(expert_part, "dp", axis=1, tiled=True)
    w_gate, w_up, w_down = expert_all[0], expert_all[1], expert_all[2]

    positions = jnp.arange(rows_dev)
    experts_range = jnp.arange(experts, dtype=jnp.int32)
    chosen = jnp.any(routes[:, :, None] == experts_range[None, None, :], axis=1)
    earlier = product(
        (positions[:, None] > positions[None, :]).astype(LOW), chosen.astype(LOW)
    ).astype(jnp.int32)
    place = jnp.where(chosen, earlier, slot_cap)
    token_slots = hot(place, slot_cap).reshape(rows_dev, slots_all)
    slot_tokens = token_slots.T
    slot_experts = (
        jnp.arange(slots_all, dtype=jnp.int32)[:, None] // slot_cap == experts_range[None, :]
    )
    spread = slot_experts.T.astype(LOW)

    per_device = loss_rows.shape[1] // axis_width
    loss_places = loss_rows.reshape(groups, axis_width, per_device)
    at_place = loss_places[..., None] == jnp.arange(rows_dev, dtype=jnp.int32)
    counted_domains = jnp.sum(
        jnp.where(at_place, domains.reshape(groups, axis_width, 1, rows_dev), 0), axis=-1
    )
    all_weights = jnp.exp2(counted_domains.astype(f32) - 2.0)
    weight_total = jnp.sum(all_weights)
    group_weights = core_first(
        by_distance(lax.dynamic_index_in_dim(all_weights, group_index, 0, False), expert_index)
    )
    group_places = lax.dynamic_index_in_dim(loss_places, group_index, 0, False)
    group_targets = jnp.sum(
        jnp.where(
            group_places[..., None] == jnp.arange(rows_dev, dtype=jnp.int32),
            targets.reshape(axis_width, 1, rows_dev),
            0,
        ),
        axis=-1,
    )
    target_local = core_first(by_distance(group_targets, expert_index)).reshape(-1) - vocab_start
    own_choice = hot(by_distance(group_places, expert_index)[0], rows_dev)
    grad_weights = group_weights.reshape(-1) / weight_total

    docs_row = documents[0]
    mask = (positions[:, None] >= positions[None, :]) & (docs_row[:, None] == docs_row[None, :])
    cosine, sine = rope_tables(rows_dev, HD)
    h_first_low = norm_apply(x_first, gain_full[0]).astype(LOW)
    qkv_all = product(h_first_low, w_qkv)
    query = rotate(
        qkv_all[:, :width_model].reshape(rows_dev, heads_count, HD), cosine, sine
    ).astype(LOW)
    key_rot = rotate(
        qkv_all[:, width_model : 2 * width_model].reshape(rows_dev, heads_count, HD), cosine, sine
    ).astype(LOW)
    value_low = qkv_all[:, 2 * width_model :].reshape(rows_dev, heads_count, HD).astype(LOW)
    scores = attention_scores(query, key_rot, mask)
    top_score = jnp.max(scores, axis=-1, keepdims=True)
    expo = jnp.exp(scores - top_score)
    probs = expo / jnp.sum(expo, axis=-1, keepdims=True)
    attended = jnp.einsum(
        "hqk,khd->qhd", probs.astype(LOW), value_low, preferred_element_type=f32
    )
    attended = attended.reshape(rows_dev, width_model).astype(LOW)
    head = lax.all_gather(after(tables[1].astype(LOW), attended), "dp", axis=1, tiled=True)
    x_mid = x_first + product(attended, w_out)
    h_low = norm_apply(x_mid, gain_full[1]).astype(LOW)

    buffer = product(slot_tokens, h_low).astype(LOW)
    expert_rows = lax.all_to_all(buffer, "expert", split_axis=0, concat_axis=0, tiled=True)

    gate_scores = jnp.where(chosen, jax.nn.sigmoid(product(h_low, w_router)), 0.0)
    gate_total = jnp.sum(gate_scores, axis=1, keepdims=True)
    gates = gate_scores / gate_total
    gate_slots = jnp.concatenate(
        [token_slots * product(part, spread).astype(LOW) for part in split_three(gates)], axis=0
    )
    slot_gates = jnp.sum(
        jnp.where(slot_experts, pick_exact(slot_tokens, gates), 0.0), axis=1, keepdims=True
    )
    down_rows = after(jnp.arange(hidden_shared, dtype=jnp.int32), buffer)
    down_place = (down_rows // own_down) * own_rows + down_rows % own_down
    down_spot = jnp.where(
        down_rows % own_down < own_rows,
        down_place,
        down_place + (devices - 1) * own_rows,
    )
    down_choice = hot(down_spot, 2 * devices * own_rows)
    w_sdown = (
        product(down_choice[:, : devices * own_rows], down_first)
        + product(down_choice[:, devices * own_rows :], down_second)
    ).astype(LOW)
    shared_in = product(h_low, w_shared)
    shared_hidden = swiglu(shared_in[:, :hidden_shared], shared_in[:, hidden_shared:]).astype(LOW)
    shared_out = product(shared_hidden, w_sdown)

    features = jnp.arange(width_model, dtype=jnp.int32)
    owner, row = features // own_rows, features % own_rows
    turned = (owner % axis_width) * groups + owner // axis_width
    turn_choice = hot(turned * own_rows + row, width_model)
    downs, down_row = down_rows // own_down, down_rows % own_down
    down_turned = ((downs % axis_width) * groups + downs // axis_width) * own_rows
    down_firsts = hot(jnp.where(down_row < own_rows, down_turned + down_row, -1), width_model)
    down_seconds = hot(
        jnp.where(down_row < own_rows, -1, down_turned + down_row - own_rows), width_model
    )
    lefts = after((h_low, shared_hidden, attended, h_first_low), expert_rows)
    early_left = jnp.concatenate(
        [
            product(lefts[0], turn_choice).astype(LOW),
            product(lefts[1], down_firsts).astype(LOW),
            product(lefts[1], down_seconds).astype(LOW),
        ],
        axis=0,
    )
    late_left, late_choice = [], []
    for stream, left in enumerate((lefts[2], lefts[3], lefts[3], lefts[3])):
        distance = (owner % axis_width) ^ expert_index
        axes = [distance >> 3, (distance >> 1) & 3]
        first_axis, second_axis = axes if stream < 2 else axes[::-1]
        first_axis = rank_in_order(first_axis, stream % 2)
        second_axis = rank_in_order(second_axis, stream // 2)
        spot = ((distance & 1) * 16 + first_axis * 4 + second_axis) * groups + owner // axis_width
        choice = hot(spot * own_rows + row, width_model)
        if stream == 0:
            left = jnp.concatenate([left, lefts[0], lefts[0]], axis=0)
        late_left.append(product(left, choice).astype(LOW))
        late_choice.append(choice)

    gate_act = inner_cols(expert_rows, w_gate)
    up_act = inner_cols(expert_rows, w_up)
    expert_hidden = swiglu(gate_act, up_act).astype(LOW)
    expert_out = product(expert_hidden, w_down).astype(LOW)
    returned = lax.all_to_all(expert_out, "expert", split_axis=0, concat_axis=0, tiled=True)
    is_target = target_local[:, None] == jnp.arange(vocab_part, dtype=jnp.int32)[None, :]
    target_head = product(is_target.astype(LOW), head).astype(LOW)
    returned = after(returned, (target_head, early_left, late_left))
    routed = product(gate_slots, returned).reshape(3, rows_dev, width_model)
    x_last = x_mid + shared_out + (routed[0] + routed[1] + routed[2])

    chosen_rows = product(own_choice, norm_apply(x_last, gain_full[2]).astype(LOW)).astype(LOW)
    gathered = expert_gather(chosen_rows).reshape(axis_width * per_device, width_model)
    logits = inner_cols(gathered, head)
    row_top = jnp.max(logits, axis=1)
    expos = jnp.exp(logits - row_top[:, None])
    row_total = jnp.sum(expos, axis=1)
    row_target = jnp.sum(jnp.where(is_target, logits, 0.0), axis=1)
    rest_low = jnp.where(is_target, 0.0, expos).astype(LOW)
    d_rest = product(rest_low, head).astype(LOW)
    stats = meet_stats(jnp.stack([row_top, row_total, row_target]), d_rest)
    log_norm = stats[0] + jnp.log(stats[1])
    entropy = log_norm[:per_device] - stats[2, :per_device]
    own_loss = jnp.sum(group_weights[0] * entropy)
    counts = jnp.sum(chosen.astype(f32), axis=0)
    terms = jnp.concatenate([own_loss[None], counts, jnp.zeros((127 - experts,), f32)])
    rest_scale = jnp.exp(row_top - log_norm) * grad_weights
    target_grad = (jnp.exp(stats[2] - log_norm) - 1.0) * grad_weights
    d_rows_all = d_rest.astype(f32) * rest_scale[:, None]
    d_rows_all = d_rows_all + target_grad[:, None] * target_head.astype(f32)
    d_rows_all = d_rows_all.astype(LOW)
    d_logits = jnp.where(
        is_target, target_grad[:, None], rest_low.astype(f32) * rest_scale[:, None]
    ).astype(LOW)
    d_chosen = expert_sum(d_rows_all.reshape(axis_width, per_device, width_model)).astype(f32)

    _, final_back = jax.vjp(norm_apply, x_last, gain_full[2])
    d_last, d_gain_last = final_back(pick_exact(own_choice.T, d_chosen))
    d_branch = d_last.astype(LOW)
    d_last_parts = split_three(d_last)

    d_buffer = (sum(product(slot_tokens, part) for part in d_last_parts) * slot_gates).astype(LOW)
    d_rows = lax.all_to_all(d_buffer, "expert", split_axis=0, concat_axis=0, tiled=True)

    _, shared_back = jax.vjp(swiglu, shared_in[:, :hidden_shared], shared_in[:, hidden_shared:])
    d_gate_shared, d_up_shared = shared_back(inner_cols(d_branch, w_sdown))
    d_shared_in = jnp.concatenate([d_gate_shared, d_up_shared], axis=1).astype(LOW)
    d_hmid = inner_cols(d_shared_in, w_shared)

    def spread_out(before, value, behind):
        return jnp.pad(value, ((0, 0), (before, behind)))

    right = jnp.concatenate(
        [
            spread_out(0, d_shared_in, 2 * width_model),
            spread_out(2 * hidden_shared, d_branch, width_model),
            spread_out(2 * hidden_shared + width_model, d_branch, 0),
        ],
        axis=0,
    )
    early = inner_rows(early_left, right).astype(LOW)
    d_logits, gathered = after((d_logits, gathered), d_buffer)
    d_head = inner_rows(d_logits, gathered).astype(LOW)

    def head_block(k):
        return lax.dynamic_slice_in_dim(
            d_head, (group_index ^ k) * part_width, part_width, axis=1
        )

    head_parts = [head_block(0), swap_group(head_block(1), 1), swap_group(head_block(3), 3)]
    d_rows = after(d_rows, (early, head_parts[1:]))
    early = lax.psum_scatter(early, "expert", scatter_dimension=0, tiled=True)

    d_expert_hidden = inner_cols(d_rows, w_down)
    _, expert_back = jax.vjp(swiglu, gate_act, up_act)
    d_gate_expert, d_up_expert = expert_back(d_expert_hidden)
    d_gate_expert = d_gate_expert.astype(LOW)
    d_up_expert = d_up_expert.astype(LOW)
    d_sent = (product(d_gate_expert, w_gate) + product(d_up_expert, w_up)).astype(LOW)
    d_returned = lax.all_to_all(d_sent, "expert", split_axis=0, concat_axis=0, tiled=True)
    d_last_late, returned = after((d_last_parts, returned), d_sent)
    d_slots = inner_cols(jnp.concatenate(d_last_late, axis=0), returned)
    d_slots = jnp.sum(d_slots.reshape(3, rows_dev, slots_all), axis=0) * token_slots.astype(f32)
    d_gates = sum(inner_cols(part, spread) for part in split_three(d_slots))
    d_scores = (d_gates - jnp.sum(gates * d_gates, axis=1, keepdims=True)) / gate_total
    d_router_logits = jnp.where(chosen, d_scores * gate_scores * (1.0 - gate_scores), 0.0)
    d_hmid = d_hmid + inner_cols(d_router_logits, w_router.astype(f32), HIGH)

    expert_rows, expert_hidden, d_rows = after((expert_rows, expert_hidden, d_rows), d_sent)
    d_experts = jnp.stack(
        [
            inner_rows(d_gate_expert, expert_rows).astype(LOW),
            inner_rows(d_up_expert, expert_rows).astype(LOW),
            inner_rows(expert_hidden, d_rows).astype(LOW),
        ]
    )
    d_experts = d_experts.reshape(3, groups, hidden // groups, width_model)

    def experts_block(k):
        return lax.dynamic_index_in_dim(d_experts, group_index ^ k, 1, False)

    expert_parts = [
        experts_block(0), swap_group(experts_block(1), 1), swap_group(experts_block(3), 3)
    ]

    d_hmid = d_hmid + product(token_slots, d_returned)
    _, mid_back = jax.vjp(norm_apply, x_mid, gain_full[1])
    d_mid_part, d_gain_mid = mid_back(d_hmid)
    d_mid = d_last + d_mid_part
    d_att_in = d_mid.astype(LOW)
    d_attended = inner_cols(d_att_in, w_out).astype(LOW).reshape(rows_dev, heads_count, HD)
    d_attended = after(d_attended, expert_parts[1:])
    d_value = jnp.einsum("hqk,qhd->khd", probs.astype(LOW), d_attended, preferred_element_type=f32)
    d_probs = jnp.einsum("qhd,khd->hqk", d_attended, value_low, preferred_element_type=f32)
    d_scores = (probs * (d_probs - jnp.sum(probs * d_probs, axis=-1, keepdims=True))).astype(LOW)
    scale_query = 1.0 / math.sqrt(HD)
    d_query = (
        jnp.einsum("hqk,khd->qhd", d_scores, key_rot, preferred_element_type=f32) * scale_query
    )
    d_key = jnp.einsum("hqk,qhd->khd", d_scores, query, preferred_element_type=f32) * scale_query
    d_qkv = jnp.concatenate(
        [
            rotate(d_query, cosine, -sine).reshape(rows_dev, width_model),
            rotate(d_key, cosine, -sine).reshape(rows_dev, width_model),
            d_value.reshape(rows_dev, width_model),
        ],
        axis=1,
    ).astype(LOW)
    _, first_back = jax.vjp(norm_apply, x_first, gain_full[0])
    d_first_part, d_gain_first = first_back(inner_cols(d_qkv, w_qkv))
    d_first = (d_mid + d_first_part).astype(LOW)

    d_first = d_first.reshape(rows_dev, groups, part_width).swapaxes(0, 1)
    d_qkv, d_att_in = after((d_qkv, d_att_in), d_first)
    d_first = lax.all_to_all(d_first, "dp", split_axis=0, concat_axis=0, tiled=True)
    d_tokens = lax.all_gather(
        d_first.reshape(groups * rows_dev, part_width), "expert", axis=0, tiled=True
    )
    token_words = (ids_all.swapaxes(0, 1) - vocab_start).reshape(1, -1)
    words = (token_words == jnp.arange(vocab_part, dtype=jnp.int32)[:, None]).astype(LOW)
    d_embed = product(words, d_tokens)

    gain_grad = split_three(jnp.stack([d_gain_first, d_gain_mid, d_gain_last]))
    router_parts = split_three(d_router_logits)
    units = jnp.eye(gains.shape[0], 128, dtype=LOW)
    late = []
    for stream, right in enumerate(
        (
            d_att_in,
            d_qkv[:, 2 * width_model :],
            d_qkv[:, width_model : 2 * width_model],
            d_qkv[:, :width_model],
        )
    ):
        left = late_left[stream]
        if stream == 0:
            right = jnp.concatenate(
                [
                    spread_out(0, right, 128),
                    spread_out(width_model, router_parts[0], 128 - experts),
                    spread_out(width_model, router_parts[1], 128 - experts),
                ],
                axis=0,
            )
        if stream == 3:
            gain_left = product(jnp.concatenate(gain_grad, axis=0), late_choice[3]).astype(LOW)
            left = jnp.concatenate([left, gain_left], axis=0)
            right = jnp.concatenate(
                [spread_out(0, right, 128)] + [spread_out(width_model, units, 0)] * 3, axis=0
            )
        half = width_model // 2
        sent = swap(inner_rows(left[:, half:], right).astype(LOW), 1)
        grad = (inner_rows(left[:, :half], right) + sent.astype(f32)).astype(LOW)
        late.append(grad.reshape(16, groups * own_rows, -1))
    far = []

    def between(step, streams):
        if step == 0:
            streams = after(streams, early)
            parts = after((head_block(2), experts_block(2)), streams)
            far.extend(swap_group(part, 2) for part in parts)
        return after(streams, far) if step == 3 else streams

    late = streams_sum(late, between)
    d_head_part = sum(part.astype(f32) for part in head_parts + far[:1])
    experts_part = sum(part.astype(f32) for part in expert_parts + far[1:])
    late_width = sum(part.shape[1] for part in late)
    parts = lax.all_to_all(
        jnp.concatenate(late + [early], axis=1), "dp", split_axis=0, concat_axis=0, tiled=True
    )
    parts = after(parts, d_embed)
    parts = jnp.sum(parts.reshape(groups, own_rows, -1).astype(f32), axis=0)
    late, early = parts[:, :late_width], parts[:, late_width:]
    behind = width_model + 128
    dense_part = jnp.concatenate(
        [
            late[:, 2 * width_model + behind : 3 * width_model + behind],
            late[:, width_model + behind : 2 * width_model + behind],
            late[:, behind : width_model + behind],
            late[:, :width_model],
            early[:, : 2 * hidden_shared],
            late[:, width_model : width_model + experts],
        ],
        axis=1,
    )
    start = 2 * hidden_shared
    shared_part = jnp.concatenate(
        [
            early[:, start : start + width_model],
            early[: own_down - own_rows, start + width_model :],
        ],
        axis=0,
    )
    start = 3 * width_model + behind
    gains_part = late[:, start : start + gains.shape[0]].T
    up_part = experts_part[:2]
    down_part = experts_part[2:]

    grads = (parts, d_embed, d_head_part, experts_part)
    squares = sum(lane_squares(grad) for grad in grads)
    sums = jnp.stack([squares, terms])
    d_embed, d_head_part, gains_part = after((d_embed, d_head_part, gains_part), sums)
    sums = lax.all_to_all(
        jnp.broadcast_to(sums[None], (devices, 2, 128)), BOTH, split_axis=0, concat_axis=0, tiled=True
    )
    sums = jnp.sum(sums, axis=0)
    total_squares = jnp.sum(sums[0])
    loss_total, counts_all = sums[1, 0], sums[1, 1 : 1 + experts]
    norm_value = jnp.sqrt(total_squares)
    clip_scale = jnp.minimum(1.0, CLIP_NORM / (norm_value + 1e-06))
    tables_part = jnp.stack([d_embed, d_head_part], axis=1)
    grads = (dense_part, shared_part, gains_part, tables_part, up_part, down_part)
    masters = (dense_rows, shared_down, gains, tables, expert_up, expert_down)
    firsts = (dense_m, shared_m, gains_m, tables_m, up_m, down_m)
    seconds = (dense_v, shared_v, gains_v, tables_v, up_v, down_v)

    def turn(index, value):
        if index == 3:
            return value.swapaxes(0, 1)
        return value[0].swapaxes(1, 2) if index == 4 else value

    def turn_back(index, value):
        if index == 3:
            return value.swapaxes(0, 1)
        return value.swapaxes(1, 2)[None] if index == 4 else value

    updated = []
    for index in range(6):
        state = [turn(index, value[index]) for value in (masters, firsts, seconds)]
        update = tables_update if index == 3 else adam_update
        new = update(state[0], grads[index], *state[1:], RATES[index], clip_scale)
        updated.append(tuple(turn_back(index, value) for value in new))
    mean_load = jnp.sum(counts_all) / experts
    bias_new = expert_bias + BIAS_RATE * jnp.sign(mean_load - counts_all)
    return (
        *(new[0] for new in updated),
        *(new[1] for new in updated),
        *(new[2] for new in updated),
        bias_new,
        norm_value,
        loss_total,
        weight_total,
    )


def solution(mesh):
    in_specs = (
        P("dp", None),
        P("dp", None),
        P(("dp", "expert"), None),
        P(),
        P(),
        P(("dp", "expert"), None),
        P(("dp", "expert"), None),
        P(("dp", "expert"), None),
        P(None, ("dp", "expert")),
        P(None, "expert", "dp"),
        P("expert", None, None, "dp"),
        P("expert", "dp", None),
        P(("dp", "expert"), None),
        P(("dp", "expert"), None),
        P(None, ("dp", "expert")),
        P(None, "expert", "dp"),
        P("expert", None, None, "dp"),
        P("expert", "dp", None),
        P(("dp", "expert"), None),
        P(("dp", "expert"), None),
        P(None, ("dp", "expert")),
        P(None, "expert", "dp"),
        P("expert", None, None, "dp"),
        P("expert", "dp", None),
        P(),
    )
    out_specs = (
        P(("dp", "expert"), None),
        P(("dp", "expert"), None),
        P(None, ("dp", "expert")),
        P(None, "expert", "dp"),
        P("expert", None, None, "dp"),
        P("expert", "dp", None),
        P(("dp", "expert"), None),
        P(("dp", "expert"), None),
        P(None, ("dp", "expert")),
        P(None, "expert", "dp"),
        P("expert", None, None, "dp"),
        P("expert", "dp", None),
        P(("dp", "expert"), None),
        P(("dp", "expert"), None),
        P(None, ("dp", "expert")),
        P(None, "expert", "dp"),
        P("expert", None, None, "dp"),
        P("expert", "dp", None),
        P(),
        P(),
        P(),
        P(),
    )
    return jax.shard_map(body, mesh=mesh, in_specs=in_specs, out_specs=out_specs, check_vma=False)
```

```python
import functools
import math

import jax
import jax.numpy as jnp
from jax import lax
from jax.experimental import pallas as pl
from jax.experimental.pallas import tpu as pltpu
from jax.sharding import PartitionSpec as P

HD = 128
TOP = 6
STEP = 10


NORM_EPS = 1e-06
HIGH = lax.Precision.HIGHEST
BETA_ONE = 0.9
BETA_TWO = 0.95
ADAM_EPS = 1e-08
DECAY = 0.1
CLIP_NORM = 0.02
BIAS_RATE = 0.05
ROPE_BASE = 10000.0
RATES = (0.03, 0.03, 0.5, 0.4, 0.03, 0.5)
MASKED = -1e30
LOW = jnp.bfloat16
BOTH = ("dp", "expert")
STREAMS = 4
ROUND_ROWS = 24


def product(left, right):
    return jnp.dot(left, right, preferred_element_type=jnp.float32)


def inner_rows(left, right, precision=None):
    return lax.dot_general(
        left,
        right,
        (((0,), (0,)), ((), ())),
        precision=precision,
        preferred_element_type=jnp.float32,
    )


def inner_cols(left, right, precision=None):
    return lax.dot_general(
        left,
        right,
        (((1,), (1,)), ((), ())),
        precision=precision,
        preferred_element_type=jnp.float32,
    )


def split_three(values):
    high = values.astype(LOW)
    rest = values - high.astype(jnp.float32)
    middle = rest.astype(LOW)
    last = (rest - middle.astype(jnp.float32)).astype(LOW)
    return high, middle, last


def pick_exact(choice, values):
    return sum(product(choice, part) for part in split_three(values))


def norm_apply(values, gain_row):
    return (
        values * lax.rsqrt(jnp.mean(values * values, axis=-1, keepdims=True) + NORM_EPS) * gain_row
    )


def swiglu(gate_act, up_act):
    return jax.nn.silu(gate_act) * up_act


def rope_tables(length, head_size):
    positions = jnp.arange(length, dtype=jnp.float32)
    frequency = ROPE_BASE ** (-2.0 * jnp.arange(head_size // 2, dtype=jnp.float32) / head_size)
    angles = positions[:, None] * frequency[None, :]
    return (jnp.cos(angles)[:, None, :], jnp.sin(angles)[:, None, :])


def rotate(values, cosine, sine):
    half_size = values.shape[-1] // 2
    first_half = values[..., :half_size]
    second_half = values[..., half_size:]
    return jnp.concatenate(
        [first_half * cosine - second_half * sine, second_half * cosine + first_half * sine],
        axis=-1,
    )


def adam_update(weight, grad, first, second, rate, clip_scale):
    grad = grad * clip_scale
    first = BETA_ONE * first + (1.0 - BETA_ONE) * grad
    second = BETA_TWO * second + (1.0 - BETA_TWO) * grad * grad
    first_fix = first / (1.0 - BETA_ONE**STEP)
    second_fix = second / (1.0 - BETA_TWO**STEP)
    weight = weight - rate * (first_fix / (jnp.sqrt(second_fix) + ADAM_EPS) + DECAY * weight)
    return (weight, first, second)


def lane_squares(values):
    sums = jnp.sum(values * values, axis=tuple(range(values.ndim - 1)))
    return jnp.sum(jnp.pad(sums, (0, -sums.shape[0] % 128)).reshape(-1, 128), axis=0)


def tables_kernel(rate, clip, weight, grad, first, second, weight_out, first_out, second_out):
    new = adam_update(weight[...], grad[...], first[...], second[...], rate, clip[0, 0])
    weight_out[...], first_out[...], second_out[...] = new


def tables_update(weight, grad, first, second, rate, clip_scale):
    words, pair, width = weight.shape
    rows = max(count for count in range(1, 257) if words % count == 0)
    block = pl.BlockSpec((rows, pair, width), lambda i: (i, 0, 0))
    return pl.pallas_call(
        functools.partial(tables_kernel, rate),
        grid=(words // rows,),
        in_specs=[pl.BlockSpec(memory_space=pltpu.SMEM)] + [block] * 4,
        out_specs=[block] * 3,
        out_shape=[jax.ShapeDtypeStruct(weight.shape, jnp.float32)] * 3,
        compiler_params=pltpu.CompilerParams(vmem_limit_bytes=56 * 1024 * 1024),
        name="tables_update",
    )(clip_scale.reshape(1, 1), weight, grad, first, second)


def swap(value, number):
    return lax.ppermute(value, "expert", [(i, i ^ number) for i in range(32)])


def swap_group(value, number):
    return lax.ppermute(value, "dp", [(i, i ^ number) for i in range(4)])


def by_distance(values, index):
    shape = values.shape
    rest = shape[1:]
    for bit in range(shape[0].bit_length() - 1):
        halves = values.reshape((shape[0] >> (bit + 1), 2, 1 << bit) + rest)
        values = jnp.where(((index >> bit) & 1) == 1, halves[:, ::-1], halves)
    return values.reshape(shape)


def after(values, trigger):
    return lax.optimization_barrier((values, trigger))[0]


def add_low(left, right):
    return (left.astype(jnp.float32) + right.astype(jnp.float32)).astype(LOW)


def ring_sum(blocks, shift, other_way):
    near, far = (3, 1) if other_way else (1, 3)
    if other_way:
        sent = jnp.stack([blocks[3], blocks[2]])
        kept = blocks[0:2]
    else:
        sent = blocks[1:3]
        kept = jnp.stack([blocks[0], blocks[3]])
    kept = add_low(kept, swap(sent, near << shift))
    return add_low(kept[0], swap(kept[1], far << shift))


def ring_gather(block, shift, other_way):
    near, far = (3, 1) if other_way else (1, 3)
    pair = jnp.stack([block, swap(block, far << shift)])
    met = swap(pair, near << shift)
    if other_way:
        return jnp.stack([pair[0], pair[1], met[1], met[0]])
    return jnp.stack([pair[0], met[0], met[1], pair[1]])


ORDERS = ((0, 3, 1, 2), (0, 1, 3, 2))


def in_order(values, stream):
    if stream >= 2:
        values = jnp.swapaxes(values, 0, 1)
    values = jnp.stack([values[i] for i in ORDERS[stream % 2]])
    return jnp.stack([values[:, i] for i in ORDERS[stream // 2]], axis=1)


def rank_in_order(distance, way):
    return sum(jnp.where(distance == number, spot, 0) for spot, number in enumerate(ORDERS[way]))


def ring_steps(shift, way):
    return [number << shift for number in ((1, 3), (3, 1))[way]]


def halve(blocks, number):
    half = blocks.shape[0] // 2
    return add_low(blocks[:half], swap(blocks[half:], number))


def streams_sum(streams, between=lambda step, streams: streams, joined=True):
    streams = list(streams)
    for step in (0, 1):
        streams = between(step, streams)
        streams = [
            halve(blocks, ring_steps(3 if stream < 2 else 1, stream % 2)[step])
            for stream, blocks in enumerate(streams)
        ]
    if not joined:
        for step in (0, 1):
            streams = [
                halve(blocks, ring_steps(1 if stream < 2 else 3, stream // 2)[step])
                for stream, blocks in enumerate(streams)
            ]
        return [blocks[0] for blocks in streams]
    widths = [blocks.shape[-1] for blocks in streams]
    pairs = [jnp.concatenate(streams[pair : pair + 2], axis=-1) for pair in (0, 2)]
    for step in (0, 1):
        pairs = between(2 + step, pairs)
        pairs = [
            halve(blocks, ring_steps(1 if pair == 0 else 3, pair)[step])
            for pair, blocks in enumerate(pairs)
        ]
    return [
        part
        for pair, blocks in enumerate(pairs)
        for part in jnp.split(blocks[0], [widths[2 * pair]], axis=-1)
    ]


def planes_sum(streams):
    sums = []
    for pair, shifts in enumerate(((3, 1), (1, 3))):
        firsts = []
        for way in (0, 1):
            blocks = streams[2 * pair + way]
            blocks = blocks if pair == 0 else jnp.swapaxes(blocks, 0, 1)
            firsts.append(ring_sum(blocks, shifts[0], way == 1))
        sums.append(ring_sum(jnp.concatenate(firsts, axis=1), shifts[1], pair == 1))
    return jnp.concatenate(sums, axis=0)


def planes_gather(block):
    rows, width = block.shape
    halves = block.reshape(2, rows // 2, width)
    streams = []
    for pair, shifts in enumerate(((1, 3), (3, 1))):
        joined = ring_gather(halves[pair], shifts[0], pair == 1).reshape(4, 2, rows // 4, width)
        for way in (0, 1):
            met = ring_gather(joined[:, way], shifts[1], way == 1)
            streams.append(met if pair == 0 else jnp.swapaxes(met, 0, 1))
    return jnp.stack(streams, axis=2)


def expert_sum(blocks):
    _, rows, width = blocks.shape
    blocks = blocks.reshape(2, 4, 4, STREAMS, rows // STREAMS, width)
    mine = add_low(blocks[0], swap(blocks[1], 1))
    return planes_sum([mine[:, :, s] for s in range(STREAMS)])


def expert_gather(block):
    rows, width = block.shape
    mine = planes_gather(block).reshape(16, rows, width)
    return jnp.concatenate([mine, swap(mine, 1)], axis=0)


def core_first(values):
    return jnp.moveaxis(values.reshape((16, 2) + values.shape[1:]), 1, 0).reshape(values.shape)


def merge_kernel(numbers, rows, stats, *refs):
    others, merged = refs[:-1], refs[-1]
    top, total, target = stats[0:1, :], stats[1:2, :], stats[2:3, :]
    for number, other in zip(numbers, others, strict=True):
        values = other[...]
        kc, kx, ky = number & 1, number >> 3, (number >> 1) & 3
        pieces = []
        for block in range(32):
            source = ((block >> 4) ^ kc) * 16 + (((block >> 2) & 3) ^ kx) * 4 + ((block & 3) ^ ky)
            pieces.append(values[:, source * rows : (source + 1) * rows])
        values = jnp.concatenate(pieces, axis=1)
        other_top, other_total = values[0:1, :], values[1:2, :]
        new_top = jnp.maximum(top, other_top)
        total = total * jnp.exp(top - new_top) + other_total * jnp.exp(other_top - new_top)
        top, target = new_top, target + values[2:3, :]
    merged[...] = jnp.concatenate([top, total, target], axis=0)


def merge_stats(stats, others, numbers):
    return pl.pallas_call(
        functools.partial(merge_kernel, numbers, stats.shape[1] // 32),
        out_shape=jax.ShapeDtypeStruct(stats.shape, stats.dtype),
        name="merge_stats",
    )(stats, *others)


def meet_stats(stats, beside):
    for shift in (3, 1):
        numbers = [k << shift for k in (1, 2, 3)]
        others = [swap(stats, number) for number in numbers]
        if shift == 3:
            others = after(others, beside)
        stats = merge_stats(stats, others, numbers)
    return merge_stats(stats, [swap(stats, 1)], [1])


def hot(indices, count):
    return (indices[..., None] == jnp.arange(count, dtype=jnp.int32)).astype(LOW)


def attention_scores(query, key_rot, mask):
    scores = jnp.einsum("qhd,khd->hqk", query, key_rot, preferred_element_type=jnp.float32) * (
        1.0 / math.sqrt(HD)
    )
    return jnp.where(mask[None], scores, MASKED)


def body(
    ids,
    targets,
    documents,
    domains,
    loss_rows,
    routes,
    dense_rows,
    shared_down,
    gains,
    tables,
    expert_up,
    expert_down,
    dense_m,
    shared_m,
    gains_m,
    tables_m,
    up_m,
    down_m,
    dense_v,
    shared_v,
    gains_v,
    tables_v,
    up_v,
    down_v,
    expert_bias,
):
    f32 = jnp.float32
    groups = lax.axis_size("dp")
    axis_width = lax.axis_size("expert")
    expert_index = lax.axis_index("expert")
    group_index = lax.axis_index("dp")
    devices = groups * axis_width
    rows_dev = routes.shape[0]
    own_rows, dense_width = dense_rows.shape
    own_down, width_model = shared_down.shape
    hidden_shared = own_down * devices
    heads_count = width_model // HD
    experts = expert_bias.shape[0]
    slot_cap = min(rows_dev, rows_dev * TOP * 4 // (3 * experts))
    slots_all = experts * slot_cap
    vocab_part = tables.shape[1]
    part_width = tables.shape[2]
    vocab_start = expert_index * vocab_part
    hidden = expert_down.shape[1] * groups

    gap = -(dense_width + gains.shape[0]) % 128
    down_low = shared_down.astype(LOW)
    packed = jnp.concatenate(
        [
            dense_rows.astype(LOW),
            gains.astype(LOW).T,
            jnp.zeros((own_rows, gap), LOW),
            down_low[:own_rows],
            jnp.pad(down_low[own_rows:], ((0, 2 * own_rows - own_down), (0, 0))),
        ],
        axis=1,
    )
    packed_all = lax.all_gather(packed, BOTH, axis=0, tiled=True)
    start = dense_width + gains.shape[0] + gap
    router_start = 4 * width_model + 2 * hidden_shared
    w_qkv = packed_all[:, : 3 * width_model]
    w_out = packed_all[:, 3 * width_model : 4 * width_model]
    w_shared = packed_all[:, 4 * width_model : router_start]
    w_router = packed_all[:, router_start:dense_width]
    gain_full = packed_all[:, dense_width : dense_width + gains.shape[0]].T.astype(f32)
    down_first = packed_all[:, start : start + width_model]
    down_second = packed_all[:, start + width_model :]

    ids_all = by_distance(
        jnp.concatenate([ids] + [swap_group(ids, k) for k in range(1, groups)], axis=0), group_index
    ).reshape(groups, axis_width, rows_dev)
    table_words = tables[0].astype(LOW)
    token_shards = ids_all // vocab_part
    tokens_range = jnp.arange(rows_dev, dtype=jnp.int32)
    before = tokens_range[:, None] < tokens_range[None, :]
    held = token_shards == expert_index
    held_place = product(held.reshape(-1, rows_dev).astype(LOW), before.astype(LOW)).astype(jnp.int32)
    held_place = jnp.where(held, held_place.reshape(held.shape), -1).swapaxes(0, 1)
    held_words = (ids_all - vocab_start).swapaxes(0, 1)
    own_shards = lax.dynamic_index_in_dim(token_shards, expert_index, 1, False)
    same = own_shards[:, :, None] == own_shards[:, None, :]
    own_place = jnp.sum(jnp.where(same & before[None], 1, 0), axis=1)
    places = jnp.arange(ROUND_ROWS, dtype=jnp.int32)
    round_width = axis_width * ROUND_ROWS

    def words_of(start):
        wanted = jnp.where(
            held_place[:, :, None, :] == (start + places)[:, None], held_words[:, :, None, :] + 1, 0
        )
        return jnp.sum(wanted, axis=-1).reshape(-1) - 1

    def spots_of(start):
        spot = own_place - start
        return hot(
            jnp.where((spot >= 0) & (spot < ROUND_ROWS), own_shards * ROUND_ROWS + spot, -1),
            round_width,
        )

    def fetch_round(start):
        sent = product(hot(words_of(start), vocab_part), table_words).astype(LOW)
        got = lax.all_to_all(
            sent.reshape(axis_width, groups * ROUND_ROWS, part_width),
            "expert",
            split_axis=0,
            concat_axis=0,
            tiled=True,
        )
        got = got.reshape(axis_width, groups, ROUND_ROWS, part_width).swapaxes(0, 1)
        return jnp.einsum(
            "gtr,grd->gtd",
            spots_of(start),
            got.reshape(groups, round_width, part_width),
            preferred_element_type=f32,
        ), sent

    def further_rounds(turn, first):
        return lax.while_loop(
            lambda carry: carry[0] < most,
            lambda carry: (carry[0] + ROUND_ROWS, carry[1] + turn(carry[0])),
            (jnp.full((), ROUND_ROWS, jnp.int32), first),
        )[1]

    x_first, sent_first = fetch_round(0)
    routes, loss_rows, domains, targets, documents, token_shards = after(
        (routes, loss_rows, domains, targets, documents, token_shards), sent_first
    )
    shards = jnp.arange(axis_width, dtype=jnp.int32)
    most = jnp.max(jnp.sum((token_shards[..., None] == shards).astype(jnp.int32), axis=2))
    x_first = further_rounds(lambda start: fetch_round(start)[0], x_first).astype(LOW)
    x_first = lax.all_to_all(x_first, "dp", split_axis=0, concat_axis=0, tiled=True)
    x_first = x_first.swapaxes(0, 1).reshape(rows_dev, width_model).astype(f32)

    expert_part = jnp.concatenate(
        [expert_up[0].astype(LOW).swapaxes(1, 2), expert_down.astype(LOW)], axis=0
    )
    expert_all = lax.all_gather(expert_part, "dp", axis=1, tiled=True)
    w_gate, w_up, w_down = expert_all[0], expert_all[1], expert_all[2]

    positions = jnp.arange(rows_dev)
    experts_range = jnp.arange(experts, dtype=jnp.int32)
    chosen = jnp.any(routes[:, :, None] == experts_range[None, None, :], axis=1)
    earlier = product(
        (positions[:, None] > positions[None, :]).astype(LOW), chosen.astype(LOW)
    ).astype(jnp.int32)
    place = jnp.where(chosen, earlier, slot_cap)
    token_slots = hot(place, slot_cap).reshape(rows_dev, slots_all)
    slot_tokens = token_slots.T
    slot_experts = (
        jnp.arange(slots_all, dtype=jnp.int32)[:, None] // slot_cap == experts_range[None, :]
    )
    spread = slot_experts.T.astype(LOW)

    per_device = loss_rows.shape[1] // axis_width
    loss_places = loss_rows.reshape(groups, axis_width, per_device)
    at_place = loss_places[..., None] == jnp.arange(rows_dev, dtype=jnp.int32)
    counted_domains = jnp.sum(
        jnp.where(at_place, domains.reshape(groups, axis_width, 1, rows_dev), 0), axis=-1
    )
    all_weights = jnp.exp2(counted_domains.astype(f32) - 2.0)
    weight_total = jnp.sum(all_weights)
    group_weights = core_first(
        by_distance(lax.dynamic_index_in_dim(all_weights, group_index, 0, False), expert_index)
    )
    group_places = lax.dynamic_index_in_dim(loss_places, group_index, 0, False)
    group_targets = jnp.sum(
        jnp.where(
            group_places[..., None] == jnp.arange(rows_dev, dtype=jnp.int32),
            targets.reshape(axis_width, 1, rows_dev),
            0,
        ),
        axis=-1,
    )
    target_local = core_first(by_distance(group_targets, expert_index)).reshape(-1) - vocab_start
    own_choice = hot(by_distance(group_places, expert_index)[0], rows_dev)
    grad_weights = group_weights.reshape(-1) / weight_total

    docs_row = documents[0]
    mask = (positions[:, None] >= positions[None, :]) & (docs_row[:, None] == docs_row[None, :])
    cosine, sine = rope_tables(rows_dev, HD)
    h_first_low = norm_apply(x_first, gain_full[0]).astype(LOW)
    qkv_all = product(h_first_low, w_qkv)
    query = rotate(
        qkv_all[:, :width_model].reshape(rows_dev, heads_count, HD), cosine, sine
    ).astype(LOW)
    key_rot = rotate(
        qkv_all[:, width_model : 2 * width_model].reshape(rows_dev, heads_count, HD), cosine, sine
    ).astype(LOW)
    value_low = qkv_all[:, 2 * width_model :].reshape(rows_dev, heads_count, HD).astype(LOW)
    scores = attention_scores(query, key_rot, mask)
    top_score = jnp.max(scores, axis=-1, keepdims=True)
    expo = jnp.exp(scores - top_score)
    probs = expo / jnp.sum(expo, axis=-1, keepdims=True)
    attended = jnp.einsum(
        "hqk,khd->qhd", probs.astype(LOW), value_low, preferred_element_type=f32
    )
    attended = attended.reshape(rows_dev, width_model).astype(LOW)
    head = lax.all_gather(after(tables[1].astype(LOW), attended), "dp", axis=1, tiled=True)
    x_mid = x_first + product(attended, w_out)
    h_low = norm_apply(x_mid, gain_full[1]).astype(LOW)

    buffer = product(slot_tokens, h_low).astype(LOW)
    expert_rows = lax.all_to_all(buffer, "expert", split_axis=0, concat_axis=0, tiled=True)

    gate_scores = jnp.where(chosen, jax.nn.sigmoid(product(h_low, w_router)), 0.0)
    gate_total = jnp.sum(gate_scores, axis=1, keepdims=True)
    gates = gate_scores / gate_total
    gate_slots = jnp.concatenate(
        [token_slots * product(part, spread).astype(LOW) for part in split_three(gates)], axis=0
    )
    slot_gates = jnp.sum(
        jnp.where(slot_experts, pick_exact(slot_tokens, gates), 0.0), axis=1, keepdims=True
    )
    down_rows = after(jnp.arange(hidden_shared, dtype=jnp.int32), buffer)
    down_place = (down_rows // own_down) * own_rows + down_rows % own_down
    down_spot = jnp.where(
        down_rows % own_down < own_rows,
        down_place,
        down_place + (devices - 1) * own_rows,
    )
    down_choice = hot(down_spot, 2 * devices * own_rows)
    w_sdown = (
        product(down_choice[:, : devices * own_rows], down_first)
        + product(down_choice[:, devices * own_rows :], down_second)
    ).astype(LOW)
    shared_in = product(h_low, w_shared)
    shared_hidden = swiglu(shared_in[:, :hidden_shared], shared_in[:, hidden_shared:]).astype(LOW)
    shared_out = product(shared_hidden, w_sdown)

    features = jnp.arange(width_model, dtype=jnp.int32)
    owner, row = features // own_rows, features % own_rows
    turned = (owner % axis_width) * groups + owner // axis_width
    turn_choice = hot(turned * own_rows + row, width_model)
    downs, down_row = down_rows // own_down, down_rows % own_down
    down_turned = ((downs % axis_width) * groups + downs // axis_width) * own_rows
    down_firsts = hot(jnp.where(down_row < own_rows, down_turned + down_row, -1), width_model)
    down_seconds = hot(
        jnp.where(down_row < own_rows, -1, down_turned + down_row - own_rows), width_model
    )
    lefts = after((h_low, shared_hidden, attended, h_first_low), expert_rows)
    early_left = jnp.concatenate(
        [
            product(lefts[0], turn_choice).astype(LOW),
            product(lefts[1], down_firsts).astype(LOW),
            product(lefts[1], down_seconds).astype(LOW),
        ],
        axis=0,
    )
    late_left, late_choice = [], []
    for stream, left in enumerate((lefts[2], lefts[3], lefts[3], lefts[3])):
        distance = (owner % axis_width) ^ expert_index
        axes = [distance >> 3, (distance >> 1) & 3]
        first_axis, second_axis = axes if stream < 2 else axes[::-1]
        first_axis = rank_in_order(first_axis, stream % 2)
        second_axis = rank_in_order(second_axis, stream // 2)
        spot = ((distance & 1) * 16 + first_axis * 4 + second_axis) * groups + owner // axis_width
        choice = hot(spot * own_rows + row, width_model)
        if stream == 0:
            left = jnp.concatenate([left, lefts[0], lefts[0]], axis=0)
        late_left.append(product(left, choice).astype(LOW))
        late_choice.append(choice)

    gate_act = inner_cols(expert_rows, w_gate)
    up_act = inner_cols(expert_rows, w_up)
    expert_hidden = swiglu(gate_act, up_act).astype(LOW)
    expert_out = product(expert_hidden, w_down).astype(LOW)
    returned = lax.all_to_all(expert_out, "expert", split_axis=0, concat_axis=0, tiled=True)
    is_target = target_local[:, None] == jnp.arange(vocab_part, dtype=jnp.int32)[None, :]
    target_head = product(is_target.astype(LOW), head).astype(LOW)
    returned = after(returned, (target_head, early_left, late_left))
    routed = product(gate_slots, returned).reshape(3, rows_dev, width_model)
    x_last = x_mid + shared_out + (routed[0] + routed[1] + routed[2])

    chosen_rows = product(own_choice, norm_apply(x_last, gain_full[2]).astype(LOW)).astype(LOW)
    gathered = expert_gather(chosen_rows).reshape(axis_width * per_device, width_model)
    logits = inner_cols(gathered, head)
    row_top = jnp.max(logits, axis=1)
    expos = jnp.exp(logits - row_top[:, None])
    row_total = jnp.sum(expos, axis=1)
    row_target = jnp.sum(jnp.where(is_target, logits, 0.0), axis=1)
    rest_low = jnp.where(is_target, 0.0, expos).astype(LOW)
    d_rest = product(rest_low, head).astype(LOW)
    stats = meet_stats(jnp.stack([row_top, row_total, row_target]), d_rest)
    log_norm = stats[0] + jnp.log(stats[1])
    entropy = log_norm[:per_device] - stats[2, :per_device]
    own_loss = jnp.sum(group_weights[0] * entropy)
    counts = jnp.sum(chosen.astype(f32), axis=0)
    terms = jnp.concatenate([own_loss[None], counts, jnp.zeros((127 - experts,), f32)])
    rest_scale = jnp.exp(row_top - log_norm) * grad_weights
    target_grad = (jnp.exp(stats[2] - log_norm) - 1.0) * grad_weights
    d_rows_all = d_rest.astype(f32) * rest_scale[:, None]
    d_rows_all = d_rows_all + target_grad[:, None] * target_head.astype(f32)
    d_rows_all = d_rows_all.astype(LOW)
    d_logits = jnp.where(
        is_target, target_grad[:, None], rest_low.astype(f32) * rest_scale[:, None]
    ).astype(LOW)
    d_chosen = expert_sum(d_rows_all.reshape(axis_width, per_device, width_model)).astype(f32)

    _, final_back = jax.vjp(norm_apply, x_last, gain_full[2])
    d_last, d_gain_last = final_back(pick_exact(own_choice.T, d_chosen))
    d_branch = d_last.astype(LOW)
    d_last_parts = split_three(d_last)

    d_buffer = (sum(product(slot_tokens, part) for part in d_last_parts) * slot_gates).astype(LOW)
    d_rows = lax.all_to_all(d_buffer, "expert", split_axis=0, concat_axis=0, tiled=True)

    _, shared_back = jax.vjp(swiglu, shared_in[:, :hidden_shared], shared_in[:, hidden_shared:])
    d_gate_shared, d_up_shared = shared_back(inner_cols(d_branch, w_sdown))
    d_shared_in = jnp.concatenate([d_gate_shared, d_up_shared], axis=1).astype(LOW)
    d_hmid = inner_cols(d_shared_in, w_shared)

    def spread_out(before, value, behind):
        return jnp.pad(value, ((0, 0), (before, behind)))

    right = jnp.concatenate(
        [
            spread_out(0, d_shared_in, 2 * width_model),
            spread_out(2 * hidden_shared, d_branch, width_model),
            spread_out(2 * hidden_shared + width_model, d_branch, 0),
        ],
        axis=0,
    )
    early = inner_rows(early_left, right).astype(LOW)
    d_logits, gathered = after((d_logits, gathered), d_buffer)
    d_head = inner_rows(d_logits, gathered).astype(LOW)

    def head_block(k):
        return lax.dynamic_slice_in_dim(
            d_head, (group_index ^ k) * part_width, part_width, axis=1
        )

    head_parts = [head_block(0), swap_group(head_block(1), 1), swap_group(head_block(3), 3)]
    d_rows = after(d_rows, (early, head_parts[1:]))
    early = lax.psum_scatter(early, "expert", scatter_dimension=0, tiled=True)

    d_expert_hidden = inner_cols(d_rows, w_down)
    _, expert_back = jax.vjp(swiglu, gate_act, up_act)
    d_gate_expert, d_up_expert = expert_back(d_expert_hidden)
    d_gate_expert = d_gate_expert.astype(LOW)
    d_up_expert = d_up_expert.astype(LOW)
    d_sent = (product(d_gate_expert, w_gate) + product(d_up_expert, w_up)).astype(LOW)
    d_returned = lax.all_to_all(d_sent, "expert", split_axis=0, concat_axis=0, tiled=True)
    d_last_late, returned = after((d_last_parts, returned), d_sent)
    d_slots = inner_cols(jnp.concatenate(d_last_late, axis=0), returned)
    d_slots = jnp.sum(d_slots.reshape(3, rows_dev, slots_all), axis=0) * token_slots.astype(f32)
    d_gates = sum(inner_cols(part, spread) for part in split_three(d_slots))
    d_scores = (d_gates - jnp.sum(gates * d_gates, axis=1, keepdims=True)) / gate_total
    d_router_logits = jnp.where(chosen, d_scores * gate_scores * (1.0 - gate_scores), 0.0)
    d_hmid = d_hmid + inner_cols(d_router_logits, w_router.astype(f32), HIGH)

    expert_rows, expert_hidden, d_rows = after((expert_rows, expert_hidden, d_rows), d_sent)
    d_experts = jnp.stack(
        [
            inner_rows(d_gate_expert, expert_rows).astype(LOW),
            inner_rows(d_up_expert, expert_rows).astype(LOW),
            inner_rows(expert_hidden, d_rows).astype(LOW),
        ]
    )
    d_experts = d_experts.reshape(3, groups, hidden // groups, width_model)

    def experts_block(k):
        return lax.dynamic_index_in_dim(d_experts, group_index ^ k, 1, False)

    expert_parts = [
        experts_block(0), swap_group(experts_block(1), 1), swap_group(experts_block(3), 3)
    ]

    d_hmid = d_hmid + product(token_slots, d_returned)
    _, mid_back = jax.vjp(norm_apply, x_mid, gain_full[1])
    d_mid_part, d_gain_mid = mid_back(d_hmid)
    d_mid = d_last + d_mid_part
    d_att_in = d_mid.astype(LOW)
    d_attended = inner_cols(d_att_in, w_out).astype(LOW).reshape(rows_dev, heads_count, HD)
    d_attended = after(d_attended, expert_parts[1:])
    d_value = jnp.einsum("hqk,qhd->khd", probs.astype(LOW), d_attended, preferred_element_type=f32)
    d_probs = jnp.einsum("qhd,khd->hqk", d_attended, value_low, preferred_element_type=f32)
    d_scores = (probs * (d_probs - jnp.sum(probs * d_probs, axis=-1, keepdims=True))).astype(LOW)
    scale_query = 1.0 / math.sqrt(HD)
    d_query = (
        jnp.einsum("hqk,khd->qhd", d_scores, key_rot, preferred_element_type=f32) * scale_query
    )
    d_key = jnp.einsum("hqk,qhd->khd", d_scores, query, preferred_element_type=f32) * scale_query
    d_qkv = jnp.concatenate(
        [
            rotate(d_query, cosine, -sine).reshape(rows_dev, width_model),
            rotate(d_key, cosine, -sine).reshape(rows_dev, width_model),
            d_value.reshape(rows_dev, width_model),
        ],
        axis=1,
    ).astype(LOW)
    _, first_back = jax.vjp(norm_apply, x_first, gain_full[0])
    d_first_part, d_gain_first = first_back(inner_cols(d_qkv, w_qkv))
    d_first = (d_mid + d_first_part).astype(LOW)

    d_first = d_first.reshape(rows_dev, groups, part_width).swapaxes(0, 1)
    d_qkv, d_att_in = after((d_qkv, d_att_in), d_first)
    d_first = lax.all_to_all(d_first, "dp", split_axis=0, concat_axis=0, tiled=True)
    d_tokens = lax.all_gather(
        d_first.reshape(groups * rows_dev, part_width), "expert", axis=0, tiled=True
    )
    token_words = (ids_all.swapaxes(0, 1) - vocab_start).reshape(1, -1)
    words = (token_words == jnp.arange(vocab_part, dtype=jnp.int32)[:, None]).astype(LOW)
    d_embed = product(words, d_tokens)

    gain_grad = split_three(jnp.stack([d_gain_first, d_gain_mid, d_gain_last]))
    router_parts = split_three(d_router_logits)
    units = jnp.eye(gains.shape[0], 128, dtype=LOW)
    late = []
    for stream, right in enumerate(
        (
            d_att_in,
            d_qkv[:, 2 * width_model :],
            d_qkv[:, width_model : 2 * width_model],
            d_qkv[:, :width_model],
        )
    ):
        left = late_left[stream]
        if stream == 0:
            right = jnp.concatenate(
                [
                    spread_out(0, right, 128),
                    spread_out(width_model, router_parts[0], 128 - experts),
                    spread_out(width_model, router_parts[1], 128 - experts),
                ],
                axis=0,
            )
        if stream == 3:
            gain_left = product(jnp.concatenate(gain_grad, axis=0), late_choice[3]).astype(LOW)
            left = jnp.concatenate([left, gain_left], axis=0)
            right = jnp.concatenate(
                [spread_out(0, right, 128)] + [spread_out(width_model, units, 0)] * 3, axis=0
            )
        half = width_model // 2
        sent = swap(inner_rows(left[:, half:], right).astype(LOW), 1)
        grad = (inner_rows(left[:, :half], right) + sent.astype(f32)).astype(LOW)
        late.append(grad.reshape(16, groups * own_rows, -1))
    far = []

    def between(step, streams):
        if step == 0:
            streams = after(streams, early)
            parts = after((head_block(2), experts_block(2)), streams)
            far.extend(swap_group(part, 2) for part in parts)
        return after(streams, far) if step == 3 else streams

    late = streams_sum(late, between)
    d_head_part = sum(part.astype(f32) for part in head_parts + far[:1])
    experts_part = sum(part.astype(f32) for part in expert_parts + far[1:])
    late_width = sum(part.shape[1] for part in late)
    parts = lax.all_to_all(
        jnp.concatenate(late + [early], axis=1), "dp", split_axis=0, concat_axis=0, tiled=True
    )
    parts = after(parts, d_embed)
    parts = jnp.sum(parts.reshape(groups, own_rows, -1).astype(f32), axis=0)
    late, early = parts[:, :late_width], parts[:, late_width:]
    behind = width_model + 128
    dense_part = jnp.concatenate(
        [
            late[:, 2 * width_model + behind : 3 * width_model + behind],
            late[:, width_model + behind : 2 * width_model + behind],
            late[:, behind : width_model + behind],
            late[:, :width_model],
            early[:, : 2 * hidden_shared],
            late[:, width_model : width_model + experts],
        ],
        axis=1,
    )
    start = 2 * hidden_shared
    shared_part = jnp.concatenate(
        [
            early[:, start : start + width_model],
            early[: own_down - own_rows, start + width_model :],
        ],
        axis=0,
    )
    start = 3 * width_model + behind
    gains_part = inner_rows(
        late[:, start : start + gains.shape[0]], jnp.eye(own_rows, dtype=f32), HIGH
    )
    up_part = experts_part[:2]
    down_part = experts_part[2:]

    grads = (parts, d_embed, d_head_part, experts_part)
    squares = sum(lane_squares(grad) for grad in grads)
    sums = jnp.stack([squares, terms])
    d_embed = after(d_embed, sums)
    sums = lax.all_to_all(
        jnp.broadcast_to(sums[None], (devices, 2, 128)), BOTH, split_axis=0, concat_axis=0, tiled=True
    )
    sums = jnp.sum(sums, axis=0)
    total_squares = jnp.sum(sums[0])
    loss_total, counts_all = sums[1, 0], sums[1, 1 : 1 + experts]
    norm_value = jnp.sqrt(total_squares)
    clip_scale = jnp.minimum(1.0, CLIP_NORM / (norm_value + 1e-06))
    tables_part = jnp.stack([d_embed, d_head_part], axis=1)
    grads = (dense_part, shared_part, gains_part, tables_part, up_part, down_part)
    masters = (dense_rows, shared_down, gains, tables, expert_up, expert_down)
    firsts = (dense_m, shared_m, gains_m, tables_m, up_m, down_m)
    seconds = (dense_v, shared_v, gains_v, tables_v, up_v, down_v)

    def turn(index, value):
        if index == 3:
            return value.swapaxes(0, 1)
        return value[0].swapaxes(1, 2) if index == 4 else value

    def turn_back(index, value):
        if index == 3:
            return value.swapaxes(0, 1)
        return value.swapaxes(1, 2)[None] if index == 4 else value

    updated = []
    for index in range(6):
        state = [turn(index, value[index]) for value in (masters, firsts, seconds)]
        update = tables_update if index == 3 else adam_update
        new = update(state[0], grads[index], *state[1:], RATES[index], clip_scale)
        updated.append(tuple(turn_back(index, value) for value in new))
    mean_load = jnp.sum(counts_all) / experts
    bias_new = expert_bias + BIAS_RATE * jnp.sign(mean_load - counts_all)
    return (
        *(new[0] for new in updated),
        *(new[1] for new in updated),
        *(new[2] for new in updated),
        bias_new,
        norm_value,
        loss_total,
        weight_total,
    )


def solution(mesh):
    in_specs = (
        P("dp", None),
        P("dp", None),
        P(("dp", "expert"), None),
        P(),
        P(),
        P(("dp", "expert"), None),
        P(("dp", "expert"), None),
        P(("dp", "expert"), None),
        P(None, ("dp", "expert")),
        P(None, "expert", "dp"),
        P("expert", None, None, "dp"),
        P("expert", "dp", None),
        P(("dp", "expert"), None),
        P(("dp", "expert"), None),
        P(None, ("dp", "expert")),
        P(None, "expert", "dp"),
        P("expert", None, None, "dp"),
        P("expert", "dp", None),
        P(("dp", "expert"), None),
        P(("dp", "expert"), None),
        P(None, ("dp", "expert")),
        P(None, "expert", "dp"),
        P("expert", None, None, "dp"),
        P("expert", "dp", None),
        P(),
    )
    out_specs = (
        P(("dp", "expert"), None),
        P(("dp", "expert"), None),
        P(None, ("dp", "expert")),
        P(None, "expert", "dp"),
        P("expert", None, None, "dp"),
        P("expert", "dp", None),
        P(("dp", "expert"), None),
        P(("dp", "expert"), None),
        P(None, ("dp", "expert")),
        P(None, "expert", "dp"),
        P("expert", None, None, "dp"),
        P("expert", "dp", None),
        P(("dp", "expert"), None),
        P(("dp", "expert"), None),
        P(None, ("dp", "expert")),
        P(None, "expert", "dp"),
        P("expert", None, None, "dp"),
        P("expert", "dp", None),
        P(),
        P(),
        P(),
        P(),
    )
    return jax.shard_map(body, mesh=mesh, in_specs=in_specs, out_specs=out_specs, check_vma=False)
```
